128 devices in a mesh: orb: 32 (over y, z, core), aux: 4 (over x).
Axes of the slice: x: 4, y: 4, z: 4, core: 2. Of those that a mesh axis runs over, the one named last changes fastest.
Arguments:
- blocks: float32 [512, 1024, 256], P('orb', 'aux'), may hold values from -0.66 to 0.66
- occ_energy: float32 [512], P('orb'), may hold values from -1.5 to -0.3
- vir_table: float32 [16384], replicated, may hold values from 0.3 to 3
- domain: int32 [512, 256], P('orb'), may hold values from 0 to 16383
- pair_i: int32 [2048], P('orb'), may hold values from 0 to 511, as said below
- pair_j: int32 [2048], P('orb'), may hold values from 0 to 511, as said below
Outputs:
- density: float32 [512, 1024, 256], P('orb', 'aux')
- pair_energy: float32 [2048], P('orb')
The draws below stay inside these ranges and needn't reach their ends.
Inputs may be any that keep to these rules, and one draw needn't show every extreme that they name: `pair_i`: pairs p * 64 to (p + 1) * 64 - 1 have their first orbital among orbitals p * 16 to (p + 1) * 16 - 1; an orbital may be first in many pairs or in none. `pair_j`: the second orbital of a pair lies in another group of 16 consecutive orbitals than its first; among pairs p * 64 to (p + 1) * 64 - 1, all whose second orbitals lie in the same group name the same second orbital.
All inputs are finite; a program needn't handle non-finite values.
Results may differ from the reference program's by a relative error of at most 0.0001.
Values sent between devices are 32-bit elements; how exact they have to be, the bound alone decides.
No kernel may reach another device: no remote copies, remote signals or barrier semaphores. Data moves between devices by JAX's collectives and lax.ppermute only.
A program may use at most 256 MiB of HBM per device.

```python
import jax
import jax.numpy as jnp
from jax import lax

NAUX = 1024
NV = 256
NVIRT = 16384
ORB_DEV = 16
PAIR_DEV = 64
NOCC = 512
NPAIR = 2048


def draw_pair_i(key, part):
    key = jax.random.fold_in(key, 11)
    device_count = NPAIR // PAIR_DEV

    def one_device(device):
        folded = jax.random.fold_in(key, device)
        key_one, key_two, key_three = jax.random.split(folded, 3)
        shuffle = jax.random.permutation(key_one, ORB_DEV)
        first_draw = jax.random.randint(key_two, (PAIR_DEV,), 0, ORB_DEV)
        second_draw = jax.random.randint(key_three, (PAIR_DEV,), 0, ORB_DEV)
        skewed = jnp.minimum(first_draw, second_draw)
        return device * ORB_DEV + shuffle[skewed]
    devices = jnp.arange(device_count, dtype=jnp.int32)
    return jax.vmap(one_device)(devices).reshape(NPAIR).astype(jnp.int32)


def draw_pair_j(key, part):
    key = jax.random.fold_in(key, 23)
    device_count = NPAIR // PAIR_DEV

    def one_device(device):
        folded = jax.random.fold_in(key, device)
        key_one, key_two = jax.random.split(folded)
        picked = jax.random.randint(key_one, (device_count,), 0, ORB_DEV)
        offsets = jax.random.randint(key_two, (PAIR_DEV,), 1, device_count)
        holder = (device + offsets) % device_count
        return holder * ORB_DEV + picked[holder]
    devices = jnp.arange(device_count, dtype=jnp.int32)
    return jax.vmap(one_device)(devices).reshape(NPAIR).astype(jnp.int32)


def plant(values, rng, least, top_value):
    spot = [jax.random.randint(jax.random.fold_in(rng, axis), (), 0, length) for axis, length in enumerate(values.shape)]
    widest = values.shape.index(max(values.shape))
    beside = spot[:widest] + [(spot[widest] + 1) % values.shape[widest]] + spot[widest + 1:]
    return values.at[tuple(spot)].set(least).at[tuple(beside)].set(top_value)


def steps_of(stream_key, extent, cuts, low, high):
    level, own = 1.0, jax.random.fold_in(stream_key, 6)
    for position, shards_of in cuts:
        heights = jnp.exp(jax.random.uniform(jax.random.fold_in(own, position), (shards_of,), jnp.float32, low / len(cuts), high / len(cuts)))
        level = level * jnp.repeat(heights, extent[position] // shards_of).reshape([-1 if axis == position else 1 for axis in range(len(extent))])
    return level


def gaussian(stream_key, extent, width, reach, pieces=(), held_as=jnp.bfloat16):
    array = jax.random.normal(stream_key, extent, jnp.float32) * width
    if len(pieces) > 0:
        array = steps_of(stream_key, extent, pieces, -0.22, 0.18) * array
    return jnp.clip(array, min=-reach, max=reach).astype(held_as)


def setup_inputs(seed: int = 0) -> dict:
    arg_keys = jax.random.split(jax.random.key(seed), 7)
    return {
        "blocks": gaussian(arg_keys[0], (NOCC, NAUX, NV), 0.11, 0.66, ((0, 32), (1, 4)), jnp.float32),
        "occ_energy": jnp.clip(-1.5 + 1.2 * jax.random.uniform(arg_keys[1], (NOCC,), jnp.float32) ** steps_of(arg_keys[1], (NOCC,), ((0, 32),), -0.2, 0.2), -1.5, -0.3),
        "vir_table": jnp.clip(jax.random.uniform(arg_keys[2], (NVIRT,), jnp.float32, 0.3, 3.0), 0.3, 3.0),
        "domain": plant(jax.random.randint(arg_keys[3], (NOCC, NV), 0, NVIRT), jax.random.fold_in(arg_keys[3], 1), 0, NVIRT - 1).astype(jnp.int32),
        "pair_i": draw_pair_i(jax.random.fold_in(arg_keys[6], 71), 0),
        "pair_j": draw_pair_j(jax.random.fold_in(arg_keys[6], 71), 0),
    }


precise = lax.Precision.HIGHEST


def reference(blocks, occ_energy, vir_table, domain, pair_i, pair_j):
    virtual = jnp.take(vir_table, domain, axis=0)
    groups = NPAIR // PAIR_DEV
    first_rows = pair_i.reshape(groups, PAIR_DEV).astype(jnp.int32)
    second_rows = pair_j.reshape(groups, PAIR_DEV).astype(jnp.int32)

    def scan_step(total, pair_rows):
        rows_first, rows_second = pair_rows
        first_blocks = jnp.take(blocks, rows_first, axis=0)
        second_blocks = jnp.take(blocks, rows_second, axis=0)
        integrals = jnp.einsum("pxa,pxb->pab", first_blocks, second_blocks, precision=precise)
        first_vir = jnp.take(virtual, rows_first, axis=0)
        second_vir = jnp.take(virtual, rows_second, axis=0)
        occ_sum = jnp.take(occ_energy, rows_first) + jnp.take(occ_energy, rows_second)
        denominator = first_vir[:, :, None] + second_vir[:, None, :] - occ_sum[:, None, None]
        amplitude = -integrals / denominator
        tilde_form = 2.0 * amplitude - jnp.swapaxes(amplitude, 1, 2)
        energy = jnp.sum(integrals * tilde_form, axis=(1, 2)) / NV
        own_terms = jnp.einsum("pxb,pab->pxa", second_blocks, tilde_form, precision=precise)
        far_terms = jnp.einsum("pxa,pab->pxb", first_blocks, tilde_form, precision=precise)
        total = total.at[rows_first].add(own_terms)
        total = total.at[rows_second].add(far_terms)
        return total, energy

    density, energy = lax.scan(scan_step, jnp.zeros(blocks.shape, jnp.float32), (first_rows, second_rows))
    return density, energy.reshape(NPAIR)
```

```python
import functools

import jax
import jax.numpy as jnp
from jax import lax
from jax.experimental import pallas as pl
from jax.experimental.pallas import tpu as pltpu
from jax.sharding import PartitionSpec as P

PARTNERS = 8
VMEM_BYTES = 56 * 1024 * 1024
f32 = jnp.float32
bf16 = jnp.bfloat16


def split(x):
    high = x.astype(bf16)
    return high, (x - high.astype(f32)).astype(bf16)


def dot3(a, b, dims):
    dot = functools.partial(
        lax.dot_general, dimension_numbers=(dims, ((), ())), preferred_element_type=f32
    )
    return dot(a[0], b[0]) + dot(a[0], b[1]) + dot(a[1], b[0])


TN = ((0,), (0,))
NN = ((1,), (0,))
NT = ((1,), (1,))


def split_seconds(second_refs, high_ref, low_ref):
    rows = high_ref.shape[1]
    for k, ref in enumerate(second_refs):
        high, low = split(ref[0:rows, :])
        high_ref[k] = high
        low_ref[k] = low


def by_first(meta):
    return lambda r: (meta[0, r], 0, 0)


def by_step(meta):
    return lambda r: (r, 0, 0)


def over_pairs(body, meta, ins, outs):
    specs = [
        [pl.BlockSpec((1,) + ref.shape[1:], place(meta)) for ref, place in refs]
        for refs in (ins, outs)
    ]

    def one(*blocks):
        step = pl.program_id(0)

        @pl.when(step < meta[2, 0])
        def _():
            body(step, *blocks)

    pltpu.emit_pipeline(
        one,
        grid=(jnp.maximum(meta[2, 0], 1),),
        in_specs=specs[0],
        out_specs=specs[1],
    )(*[ref for ref, _ in ins], *[ref for ref, _ in outs])


def integral_terms(firsts, k, s_high, s_low):
    total = None
    at = 0
    for first in firsts:
        rows = first.shape[1]
        window = pl.ds(at, rows)
        s = (s_high[k, window, :], s_low[k, window, :])
        term = dot3(split(first[0]), s, TN)
        total = term if total is None else total + term
        at += rows
    return total


def integral_kernel(parts, first_call, meta, *refs):
    firsts, refs = refs[:parts], refs[parts:]
    seconds, refs = refs[:PARTNERS], refs[PARTNERS:]
    before, refs = ([], refs) if first_call else ([refs[0]], refs[1:])
    out, s_high, s_low = refs
    split_seconds(seconds, s_high, s_low)

    def body(step, *blocks):
        total = integral_terms(blocks[:parts], meta[1, step], s_high, s_low)
        if not first_call:
            total = total + blocks[parts][0]
        blocks[-1][0] = total

    over_pairs(
        body, meta,
        [(f, by_first) for f in firsts] + [(b, by_step) for b in before], [(out, by_step)],
    )


def density_terms(firsts, t, i, k, s_high, s_low, owns, far):
    at = 0
    for first, own in zip(firsts, owns):
        rows = first.shape[1]
        window = pl.ds(at, rows)
        s = (s_high[k, window, :], s_low[k, window, :])
        own_window = pl.ds(at % own.shape[1], rows)
        own[i, own_window, :] += dot3(s, t, NT)
        far[k, window, :] += dot3(split(first[0]), t, NN)
        at += rows


def middle_kernel(parts, meta, *refs):
    firsts, refs = refs[:parts], refs[parts:]
    seconds, refs = refs[:PARTNERS], refs[PARTNERS:]
    before, column, row, t_high, t_low, energy, own, far, s_high, s_low = refs
    split_seconds(seconds, s_high, s_low)
    own[...] = jnp.zeros_like(own)
    far[...] = jnp.zeros_like(far)

    def body(step, *blocks):
        firsts = blocks[:parts]
        before, column, t_high, t_low, energy = blocks[parts:]
        i = meta[0, step]
        k = meta[1, step]
        total = before[0] + integral_terms(firsts, k, s_high, s_low)
        width = total.shape[1]
        lanes = column.shape[2]
        left = jnp.concatenate([column[0]] * (width // lanes), axis=1)
        amplitude = -total / (left + row[pl.ds(k, 1), :])
        tilde = 2.0 * amplitude - amplitude.T
        energy[0] = jnp.sum((total * tilde).reshape(width // 8, 8, width), axis=0)
        t = split(tilde)
        t_high[0] = t[0]
        t_low[0] = t[1]
        density_terms(firsts, t, i, k, s_high, s_low, [own] * parts, far)

    over_pairs(
        body, meta,
        [(f, by_first) for f in firsts] + [(before, by_step), (column, by_first)],
        [(t_high, by_step), (t_low, by_step), (energy, by_step)],
    )


def density_kernel(parts, meta, *refs):
    firsts, refs = refs[:parts], refs[parts:]
    seconds, refs = refs[:PARTNERS], refs[PARTNERS:]
    t_high, t_low, refs = refs[0], refs[1], refs[2:]
    owns, refs = refs[:parts], refs[parts:]
    far, s_high, s_low = refs
    split_seconds(seconds, s_high, s_low)
    for own in owns:
        own[...] = jnp.zeros_like(own)
    far[...] = jnp.zeros_like(far)

    def body(step, *blocks):
        t = (blocks[parts][0], blocks[parts + 1][0])
        density_terms(
            blocks[:parts], t, meta[0, step], meta[1, step], s_high, s_low, owns, far
        )

    over_pairs(
        body, meta,
        [(f, by_first) for f in firsts] + [(t_high, by_step), (t_low, by_step)], [],
    )


VMEM = pl.BlockSpec(memory_space=pltpu.VMEM)
SMEM = pl.BlockSpec(memory_space=pltpu.SMEM)
HBM = pl.BlockSpec(memory_space=pl.ANY)


def pair_call(kernel, meta, ins, outs, rows, flops, name):
    width = ins[0][0].shape[-1]
    return pl.pallas_call(
        kernel,
        in_specs=[SMEM] + [spec for _, spec in ins],
        out_specs=[spec for _, spec in outs],
        scratch_shapes=[pltpu.VMEM((PARTNERS, rows, width), bf16)] * 2,
        out_shape=[s for s, _ in outs],
        compiler_params=pltpu.CompilerParams(vmem_limit_bytes=VMEM_BYTES),
        cost_estimate=pl.CostEstimate(
            flops=flops, bytes_accessed=24 * 1024 * 1024, transcendentals=0
        ),
        name=name,
    )(meta, *[a for a, _ in ins])


def gather_kernel(parts, chosen, *refs):
    owns, refs = refs[:parts], refs[parts:]
    arrived, refs = refs[:PARTNERS], refs[PARTNERS:]
    outs, extra = refs[-parts:], refs[:-parts]
    rows = owns[0].shape[1]
    half = rows // 2
    for q in range(parts):
        outs[q][...] = owns[q][...]
    for k in range(PARTNERS):
        c = chosen[k]
        for q in range(parts):
            outs[q][c] += arrived[k][q * rows : (q + 1) * rows, :]
    if parts == 2:
        outs[0][:, :half, :] += extra[0][...]
        outs[1][:, half:, :] += extra[1][...]
    elif extra:
        outs[0][...] += extra[0][...] + extra[1][...]


def gather_call(chosen, owns, arrived, extra, name):
    ins = [*owns, *arrived, *extra]
    return pl.pallas_call(
        functools.partial(gather_kernel, len(owns)),
        in_specs=[SMEM] + [VMEM] * len(ins),
        out_specs=[VMEM] * len(owns),
        out_shape=[jax.ShapeDtypeStruct(o.shape, f32) for o in owns],
        compiler_params=pltpu.CompilerParams(vmem_limit_bytes=VMEM_BYTES),
        cost_estimate=pl.CostEstimate(
            flops=0, bytes_accessed=sum(4 * a.size for a in ins), transcendentals=0
        ),
        name=name,
    )(chosen, *ins)


def shards(orb_size, blocks, occ_energy, vir_table, domain, pair_i, pair_j):
    orb_dev, aux_rows, width = blocks.shape
    pair_dev = pair_i.shape[0]
    p = lax.axis_index("orb")
    x = lax.axis_index("aux")
    aux_size = 4
    half = aux_rows // 2

    ring = [(s, (s + 1) % aux_size) for s in range(aux_size)]
    back = [(t, s) for s, t in ring]
    to_right = lambda a: lax.ppermute(a, "aux", ring)
    to_left = lambda a: lax.ppermute(a, "aux", back)

    def mask_of(k, at):
        return (((k >> 1) ^ at) << 3) | k

    tables = [
        [
            (o * aux_size + s, (o ^ mask_of(k, s)) * aux_size + s)
            for o in range(orb_size)
            for s in range(aux_size)
        ]
        for k in range(PARTNERS)
    ]

    def exchange(payloads, lanes=3):
        out = []
        for k, payload in enumerate(payloads):
            if k >= lanes:
                payload, _ = lax.optimization_barrier((payload, out[k - lanes]))
            out.append(lax.ppermute(payload, ("orb", "aux"), tables[k]))
        return out

    from_left = to_right(blocks)
    from_right = to_left(blocks)

    first_local = pair_i - p * orb_dev
    holder = pair_j // orb_dev
    second_local = pair_j % orb_dev
    device_ids = jnp.arange(orb_size, dtype=jnp.int32)
    held_by = holder[:, None] == device_ids[None, :]
    wanted = jnp.max(jnp.where(held_by, second_local[:, None], -1), axis=0)
    requested = lax.all_to_all(wanted, "orb", split_axis=0, concat_axis=0, tiled=True)
    ks = jnp.arange(PARTNERS, dtype=jnp.int32)
    partners = p ^ mask_of(ks, x)
    chosen = jnp.clip(requested[partners], 0, orb_dev - 1)

    apart = holder ^ p
    mine = ((apart >> 3) ^ ((apart >> 1) & 3)) == x
    slot = apart & 7
    order = jnp.arange(pair_dev, dtype=jnp.int32)
    key = jnp.where(mine, first_local, orb_dev) * pair_dev + order
    place = jnp.sum((key[None, :] < key[:, None]).astype(jnp.int32), axis=1)
    at_place = place[None, :] == order[:, None]
    pick = lambda v: jnp.sum(jnp.where(at_place, v[None, :], 0), axis=1)
    count = jnp.sum(mine.astype(jnp.int32))
    meta = jnp.stack([pick(first_local), pick(slot), jnp.broadcast_to(count, (pair_dev,))])

    virtual = jnp.take(vir_table, domain, axis=0)
    shifted = virtual - occ_energy[:, None]
    lanes = min(128, width)
    column = jnp.broadcast_to(shifted[:, :, None], (orb_dev, width, lanes))

    pick_block = lambda a, k: lax.dynamic_index_in_dim(a, chosen[k], 0, keepdims=False)
    near = exchange([pick_block(blocks, k) for k in range(PARTNERS)])

    opposite_one = to_right(from_left[:, :half])
    opposite_two = to_left(from_right[:, half:])

    flops = 6 * 24 * width * width * aux_rows
    integral_shape = jax.ShapeDtypeStruct((pair_dev, width, width), f32)
    seconds_of = lambda arrays: [(a, VMEM) for a in arrays]
    (integrals,) = pair_call(
        functools.partial(integral_kernel, 1, True), meta,
        [(blocks, HBM), *seconds_of(near)],
        [(integral_shape, HBM)], aux_rows, flops, "integrals_near",
    )

    def beside_payload(k):
        energies = jnp.broadcast_to(pick_block(shifted, k)[None, :], (8, width))
        return jnp.concatenate(
            [pick_block(from_left, k), pick_block(from_right, k), energies], axis=0
        )

    beside = exchange([beside_payload(k) for k in range(PARTNERS)])
    (integrals,) = pair_call(
        functools.partial(integral_kernel, 2, False), meta,
        [(from_left, HBM), (from_right, HBM), *seconds_of(beside), (integrals, HBM)],
        [(integral_shape, HBM)], 2 * aux_rows, 2 * flops, "integrals_beside",
    )
    row = jnp.stack([a[2 * aux_rows] for a in beside])

    across = exchange(
        [
            jnp.concatenate([pick_block(opposite_one, k), pick_block(opposite_two, k)], axis=0)
            for k in range(PARTNERS)
        ],
        lanes=5,
    )
    own_shape = jax.ShapeDtypeStruct((orb_dev, aux_rows, width), f32)
    far_shape = jax.ShapeDtypeStruct((PARTNERS, aux_rows, width), f32)
    t_shape = jax.ShapeDtypeStruct((pair_dev, width, width), bf16)
    t_high, t_low, energy, own_across, far_across = pair_call(
        functools.partial(middle_kernel, 2), meta,
        [
            (opposite_one, HBM), (opposite_two, HBM), *seconds_of(across),
            (integrals, HBM), (column, HBM), (row, VMEM),
        ],
        [
            (t_shape, HBM), (t_shape, HBM),
            (jax.ShapeDtypeStruct((pair_dev, 8, width), f32), HBM),
            (own_shape, VMEM), (far_shape, VMEM),
        ],
        aux_rows, 4 * flops, "amplitudes",
    )
    arrived_across = exchange([far_across[k] for k in range(PARTNERS)], lanes=5)

    own_left, own_right, far_beside = pair_call(
        functools.partial(density_kernel, 2), meta,
        [
            (from_left, HBM), (from_right, HBM), *seconds_of(beside),
            (t_high, HBM), (t_low, HBM),
        ],
        [
            (own_shape, VMEM), (own_shape, VMEM),
            (jax.ShapeDtypeStruct((PARTNERS, 2 * aux_rows, width), f32), VMEM),
        ],
        2 * aux_rows, 4 * flops, "density_beside",
    )
    (sum_across,) = gather_call(chosen, [own_across], arrived_across, [], "sum_across")
    carried_right = to_right(sum_across[:, :half])
    carried_left = to_left(sum_across[:, half:])
    arrived_beside = exchange([far_beside[k] for k in range(PARTNERS)])

    own_near, far_near = pair_call(
        functools.partial(density_kernel, 1), meta,
        [(blocks, HBM), *seconds_of(near), (t_high, HBM), (t_low, HBM)],
        [(own_shape, VMEM), (far_shape, VMEM)],
        aux_rows, 2 * flops, "density_near",
    )
    sum_right, sum_left = gather_call(
        chosen,
        [own_right, own_left],
        [jnp.concatenate([a[aux_rows:], a[:aux_rows]], axis=0) for a in arrived_beside],
        [carried_right, carried_left],
        "sum_beside",
    )
    home_one = to_right(sum_right)
    home_two = to_left(sum_left)
    arrived_near = exchange([far_near[k] for k in range(PARTNERS)])
    (density,) = gather_call(
        chosen, [own_near], arrived_near, [home_one, home_two], "sum_near"
    )

    pair_energy = jnp.sum(energy, axis=(1, 2)) / width
    pair_energy = jnp.where(order < count, pair_energy, 0.0)
    spread = jnp.sum(jnp.where(at_place.T, pair_energy[None, :], 0.0), axis=1)
    return density, lax.psum(spread, "aux")


def solution(mesh):
    placed = (P("orb", "aux", None), P("orb"), P(), P("orb", None), P("orb"), P("orb"))
    return jax.shard_map(
        functools.partial(shards, mesh.shape["orb"]),
        mesh=mesh,
        in_specs=placed,
        out_specs=(P("orb", "aux", None), P("orb")),
        check_vma=False,
    )
```

```python
import functools

import jax
import jax.numpy as jnp
from jax import lax
from jax.experimental import pallas as pl
from jax.experimental.pallas import tpu as pltpu
from jax.sharding import PartitionSpec as P

PARTNERS = 8
VMEM_BYTES = 56 * 1024 * 1024
f32 = jnp.float32
bf16 = jnp.bfloat16


def split(x):
    high = x.astype(bf16)
    return high, (x - high.astype(f32)).astype(bf16)


def dot3(a, b, dims):
    dot = functools.partial(
        lax.dot_general, dimension_numbers=(dims, ((), ())), preferred_element_type=f32
    )
    return dot(a[0], b[0]) + dot(a[0], b[1]) + dot(a[1], b[0])


TN = ((0,), (0,))
NN = ((1,), (0,))
NT = ((1,), (1,))


VMEM = pl.BlockSpec(memory_space=pltpu.VMEM)
SMEM = pl.BlockSpec(memory_space=pltpu.SMEM)
HBM = pl.BlockSpec(memory_space=pl.ANY)
DMA = pltpu.SemaphoreType.DMA


def start_all(copies):
    for copy in copies:
        copy.start()


def wait_all(copies):
    for copy in copies:
        copy.wait()


def load(parts, firsts, seconds, f_in, s_in, f_sem, s_sem):
    rows = s_in.shape[1]
    s_copies = [
        pltpu.make_async_copy(ref.at[pl.ds(0, rows)], s_in.at[k], s_sem.at[k])
        for k, ref in enumerate(seconds)
    ]
    f_copies = []
    at = 0
    for q, ref in enumerate(firsts):
        window = pl.ds(at, ref.shape[1])
        f_copies.append(pltpu.make_async_copy(ref, f_in.at[:, window], f_sem.at[q]))
        at += ref.shape[1]
    start_all(s_copies + f_copies)
    return s_copies, f_copies


def split_first(meta, step, f_in, f_high, f_low):
    i = meta[0, step]
    before = meta[0, jnp.maximum(step, 1) - 1]

    @pl.when((step == 0) | (i != before))
    def _():
        f_high[...], f_low[...] = split(f_in[i])

    return (f_high[...], f_low[...])


def integral_kernel(parts, first_call, meta, *refs):
    firsts, refs = refs[:parts], refs[parts:]
    seconds, refs = refs[:PARTNERS], refs[PARTNERS:]
    before, refs = (None, refs) if first_call else (refs[0], refs[1:])
    out, f_in, s_in, f_high, f_low, s_high, s_low, k_buf, f_sem, s_sem, k_sem, o_sem = refs
    count = meta[2, 0]
    into = lambda r: pltpu.make_async_copy(before.at[r], k_buf.at[r], k_sem.at[r])
    back = lambda r: pltpu.make_async_copy(k_buf.at[r], out.at[r], o_sem.at[r])
    s_copies, f_copies = load(parts, firsts, seconds, f_in, s_in, f_sem, s_sem)
    if not first_call:
        pl.loop(0, count)(lambda r: into(r).start())
    for k in range(PARTNERS):
        s_copies[k].wait()
        s_high[k], s_low[k] = split(s_in[k].T)
    wait_all(f_copies)

    @pl.loop(0, count)
    def _(r):
        k = meta[1, r]
        f = split_first(meta, r, f_in, f_high, f_low)
        total = dot3((s_high[k], s_low[k]), f, NN)
        if not first_call:
            into(r).wait()
            total = total + k_buf[r]
        k_buf[r] = total
        back(r).start()

    pl.loop(0, count)(lambda r: back(r).wait())


def density_terms(i, k, f, s, u, own, far):
    rows = own.shape[2]
    for q in range(own.shape[0]):
        part = slice(q * rows, (q + 1) * rows)
        own[q, i] += dot3((s[0][part], s[1][part]), u, NN)
    far[k] += dot3(f, u, NT)


def middle_kernel(parts, meta, *refs):
    firsts, refs = refs[:parts], refs[parts:]
    seconds, refs = refs[:PARTNERS], refs[PARTNERS:]
    before, first_row, second_row, u_high, u_low, energy, own = refs[:7]
    far_outs, refs = refs[7 : 7 + PARTNERS], refs[7 + PARTNERS :]
    (f_in, s_in, f_high, f_low, s_high, s_low, k_buf, f_sem, s_sem, k_sem, far, column,
     t_high, t_low, uh_buf, ul_buf, h_sem, l_sem, far_sem) = refs
    count = meta[2, 0]
    into = lambda r: pltpu.make_async_copy(before.at[r], k_buf.at[r], k_sem.at[r])
    high = lambda r: pltpu.make_async_copy(uh_buf.at[r], u_high.at[r], h_sem.at[r])
    low = lambda r: pltpu.make_async_copy(ul_buf.at[r], u_low.at[r], l_sem.at[r])
    s_copies, f_copies = load(parts, firsts, seconds, f_in, s_in, f_sem, s_sem)
    pl.loop(0, count)(lambda r: into(r).start())
    own[...] = jnp.zeros_like(own)
    far[...] = jnp.zeros_like(far)
    width = far.shape[2]
    lanes = column.shape[2]
    for k in range(PARTNERS):
        column[k] = jnp.broadcast_to(second_row[k : k + 1, :], (lanes, width)).T
    for k in range(PARTNERS):
        s_copies[k].wait()
        s = s_in[k]
        s_high[k], s_low[k] = split(s)
        t_high[k], t_low[k] = split(s.T)
    wait_all(f_copies)

    @pl.loop(0, count)
    def _(r):
        i = meta[0, r]
        k = meta[1, r]
        f = split_first(meta, r, f_in, f_high, f_low)
        total = dot3((t_high[k], t_low[k]), f, NN)
        into(r).wait()
        total = total + k_buf[r]
        side = jnp.concatenate([column[k]] * (width // lanes), axis=1)
        amplitude = -total / (side + first_row[pl.ds(i, 1), :])
        tilde = 2.0 * amplitude - amplitude.T
        energy[r] = jnp.sum((total * tilde).reshape(width // 8, 8, width), axis=0)
        u = split(tilde)
        uh_buf[r], ul_buf[r] = u
        high(r).start()
        low(r).start()
        density_terms(i, k, f, (s_high[k], s_low[k]), u, own, far)

    outs = [
        pltpu.make_async_copy(far.at[k], far_outs[k], far_sem.at[k]) for k in range(PARTNERS)
    ]
    start_all(outs)

    @pl.loop(0, count)
    def _(r):
        high(r).wait()
        low(r).wait()

    wait_all(outs)


def density_kernel(parts, meta, *refs):
    firsts, refs = refs[:parts], refs[parts:]
    seconds, refs = refs[:PARTNERS], refs[PARTNERS:]
    u_high, u_low, own = refs[:3]
    far_outs, refs = refs[3 : 3 + PARTNERS], refs[3 + PARTNERS :]
    (f_in, s_in, f_high, f_low, s_high, s_low, f_sem, s_sem, far, uh_buf, ul_buf, h_sem,
     l_sem, far_sem) = refs
    count = meta[2, 0]
    high = lambda r: pltpu.make_async_copy(u_high.at[r], uh_buf.at[r], h_sem.at[r])
    low = lambda r: pltpu.make_async_copy(u_low.at[r], ul_buf.at[r], l_sem.at[r])
    s_copies, f_copies = load(parts, firsts, seconds, f_in, s_in, f_sem, s_sem)

    @pl.loop(0, count)
    def _(r):
        high(r).start()
        low(r).start()

    own[...] = jnp.zeros_like(own)
    far[...] = jnp.zeros_like(far)
    for k in range(PARTNERS):
        s_copies[k].wait()
        s_high[k], s_low[k] = split(s_in[k])
    wait_all(f_copies)

    @pl.loop(0, count)
    def _(r):
        k = meta[1, r]
        f = split_first(meta, r, f_in, f_high, f_low)
        high(r).wait()
        low(r).wait()
        u = (uh_buf[r], ul_buf[r])
        density_terms(meta[0, r], k, f, (s_high[k], s_low[k]), u, own, far)

    outs = [
        pltpu.make_async_copy(far.at[k], far_outs[k], far_sem.at[k]) for k in range(PARTNERS)
    ]
    start_all(outs)
    wait_all(outs)


def kernel_call(kernel, ins, outs, scratch, flops, moved, name):
    return pl.pallas_call(
        kernel,
        in_specs=[spec for _, spec in ins],
        out_specs=[spec for _, spec in outs],
        scratch_shapes=scratch,
        out_shape=[s for s, _ in outs],
        compiler_params=pltpu.CompilerParams(vmem_limit_bytes=VMEM_BYTES),
        cost_estimate=pl.CostEstimate(flops=flops, bytes_accessed=moved, transcendentals=0),
        name=name,
    )(*[a for a, _ in ins])


def block_scratch(orb_dev, rows, width):
    return [
        pltpu.VMEM((orb_dev, rows, width), f32),
        pltpu.VMEM((PARTNERS, rows, width), f32),
        pltpu.VMEM((rows, width), bf16),
        pltpu.VMEM((rows, width), bf16),
    ]


def integral_call(meta, firsts, seconds, before, name):
    orb_dev, _, width = firsts[0].shape
    rows = sum(f.shape[1] for f in firsts)
    pairs = meta.shape[1]
    shape = jax.ShapeDtypeStruct((pairs, width, width), f32)
    earlier = [] if before is None else [before]
    (out,) = kernel_call(
        functools.partial(integral_kernel, len(firsts), before is None),
        [(meta, SMEM)] + [(a, HBM) for a in [*firsts, *seconds, *earlier]],
        [(shape, HBM)],
        block_scratch(orb_dev, rows, width)
        + [pltpu.VMEM((PARTNERS, width, rows), bf16)] * 2
        + [pltpu.VMEM((pairs, width, width), f32)]
        + [DMA((len(firsts),)), DMA((PARTNERS,)), DMA((pairs,)), DMA((pairs,))],
        6 * 16 * width * width * rows, 16 * 1024 * 1024, name,
    )
    return out


def middle_call(meta, firsts, seconds, before, first_row, second_row, name):
    orb_dev, _, width = firsts[0].shape
    rows = sum(f.shape[1] for f in firsts)
    pairs = meta.shape[1]
    u_shape = jax.ShapeDtypeStruct((pairs, width, width), bf16)
    far_shape = jax.ShapeDtypeStruct((rows, width), f32)
    outs = kernel_call(
        functools.partial(middle_kernel, len(firsts)),
        [(meta, SMEM)] + [(a, HBM) for a in [*firsts, *seconds, before]]
        + [(first_row, VMEM), (second_row, VMEM)],
        [(u_shape, HBM), (u_shape, HBM), (jax.ShapeDtypeStruct((pairs, 8, width), f32), VMEM)]
        + [(jax.ShapeDtypeStruct((1, orb_dev, rows, width), f32), VMEM)]
        + [(far_shape, HBM)] * PARTNERS,
        block_scratch(orb_dev, rows, width)
        + [pltpu.VMEM((PARTNERS, rows, width), bf16)] * 2
        + [pltpu.VMEM((pairs, width, width), f32)]
        + [DMA((len(firsts),)), DMA((PARTNERS,)), DMA((pairs,))]
        + [pltpu.VMEM((PARTNERS, rows, width), f32)]
        + [pltpu.VMEM((PARTNERS, width, min(128, width)), f32)]
        + [pltpu.VMEM((PARTNERS, width, rows), bf16)] * 2
        + [pltpu.VMEM((pairs, width, width), bf16)] * 2
        + [DMA((pairs,)), DMA((pairs,)), DMA((PARTNERS,))],
        18 * 16 * width * width * rows, 24 * 1024 * 1024, name,
    )
    return outs[0], outs[1], outs[2], outs[3][0], outs[4:]


def density_call(meta, firsts, seconds, u, name):
    orb_dev, _, width = firsts[0].shape
    rows = sum(f.shape[1] for f in firsts)
    pairs = meta.shape[1]
    own_shape = jax.ShapeDtypeStruct((len(firsts), orb_dev, rows // len(firsts), width), f32)
    outs = kernel_call(
        functools.partial(density_kernel, len(firsts)),
        [(meta, SMEM)] + [(a, HBM) for a in [*firsts, *seconds, *u]],
        [(own_shape, VMEM)]
        + [(jax.ShapeDtypeStruct((rows, width), f32), HBM)] * PARTNERS,
        block_scratch(orb_dev, rows, width)
        + [pltpu.VMEM((PARTNERS, rows, width), bf16)] * 2
        + [DMA((len(firsts),)), DMA((PARTNERS,))]
        + [pltpu.VMEM((PARTNERS, rows, width), f32)]
        + [pltpu.VMEM((pairs, width, width), bf16)] * 2
        + [DMA((pairs,)), DMA((pairs,)), DMA((PARTNERS,))],
        12 * 16 * width * width * rows, 24 * 1024 * 1024, name,
    )
    return outs[0], outs[1:]


def sum_kernel(at, cuts, extra_at, chosen, own, *refs):
    arrived, refs = refs[:PARTNERS], refs[PARTNERS:]
    extra, refs = (None, refs) if extra_at is None else (refs[0], refs[1:])
    outs, refs = refs[:cuts], refs[cuts:]
    buf, sem = refs
    rows = own.shape[2]
    copies = [
        pltpu.make_async_copy(ref.at[pl.ds(at, rows)], buf.at[k], sem.at[k])
        for k, ref in enumerate(arrived)
    ]
    start_all(copies)
    part = rows // cuts
    for q in range(cuts):
        outs[q][...] = own[0, :, q * part : (q + 1) * part, :]
    if extra is not None:
        outs[0][:, extra_at : extra_at + extra.shape[1], :] += extra[...]
    for k in range(PARTNERS):
        copies[k].wait()
        for q in range(cuts):
            outs[q][chosen[k]] += buf[k, q * part : (q + 1) * part, :]


def sum_call(chosen, own, arrived, name, at=0, cuts=1, extra=None, extra_at=None):
    orb_dev, rows, width = own.shape
    ins = [(chosen, SMEM), (own[None], VMEM)] + [(a, HBM) for a in arrived]
    if extra is not None:
        ins.append((extra, VMEM))
    shape = jax.ShapeDtypeStruct((orb_dev, rows // cuts, width), f32)
    return kernel_call(
        functools.partial(sum_kernel, at, cuts, extra_at),
        ins, [(shape, VMEM)] * cuts,
        [pltpu.VMEM((PARTNERS, rows, width), f32), DMA((PARTNERS,))],
        0, 12 * 1024 * 1024, name,
    )


def shards(orb_size, blocks, occ_energy, vir_table, domain, pair_i, pair_j):
    orb_dev, aux_rows, width = blocks.shape
    pair_dev = pair_i.shape[0]
    p = lax.axis_index("orb")
    x = lax.axis_index("aux")
    aux_size = 4
    half = aux_rows // 2

    ring = [(s, (s + 1) % aux_size) for s in range(aux_size)]
    back = [(t, s) for s, t in ring]
    to_right = lambda a: lax.ppermute(a, "aux", ring)
    to_left = lambda a: lax.ppermute(a, "aux", back)

    def mask_of(k, at):
        return (((k >> 1) ^ at) << 3) | k

    tables = [
        [
            (o * aux_size + s, (o ^ mask_of(k, s)) * aux_size + s)
            for o in range(orb_size)
            for s in range(aux_size)
        ]
        for k in range(PARTNERS)
    ]

    def exchange(payloads, lanes=3):
        out = []
        for k, payload in enumerate(payloads):
            if k >= lanes:
                payload, _ = lax.optimization_barrier((payload, out[k - lanes]))
            out.append(lax.ppermute(payload, ("orb", "aux"), tables[k]))
        return out

    from_left = to_right(blocks)
    from_right = to_left(blocks)

    first_local = pair_i - p * orb_dev
    holder = pair_j // orb_dev
    second_local = pair_j % orb_dev
    device_ids = jnp.arange(orb_size, dtype=jnp.int32)
    held_by = holder[:, None] == device_ids[None, :]
    wanted = jnp.max(jnp.where(held_by, second_local[:, None], -1), axis=0)
    requested = lax.all_to_all(wanted, "orb", split_axis=0, concat_axis=0, tiled=True)
    ks = jnp.arange(PARTNERS, dtype=jnp.int32)
    partners = p ^ mask_of(ks, x)
    chosen = jnp.clip(requested[partners], 0, orb_dev - 1)

    apart = holder ^ p
    mine = ((apart >> 3) ^ ((apart >> 1) & 3)) == x
    slot = apart & 7
    order = jnp.arange(pair_dev, dtype=jnp.int32)
    key = jnp.where(mine, first_local, orb_dev) * pair_dev + order
    place = jnp.sum((key[None, :] < key[:, None]).astype(jnp.int32), axis=1)
    at_place = place[None, :] == order[:, None]
    pick = lambda v: jnp.sum(jnp.where(at_place, v[None, :], 0), axis=1)
    count = jnp.sum(mine.astype(jnp.int32))
    meta = jnp.stack([pick(first_local), pick(slot), jnp.broadcast_to(count, (pair_dev,))])

    pick_block = lambda a, k: lax.dynamic_index_in_dim(a, chosen[k], 0, keepdims=False)
    near = exchange([pick_block(blocks, k) for k in range(PARTNERS)])
    integrals = integral_call(meta, [blocks], near, None, "integrals_near")

    late_domain, _ = lax.optimization_barrier((domain, near[1]))
    virtual = jnp.take(vir_table, late_domain, axis=0)
    shifted = virtual - occ_energy[:, None]

    from_left, from_right, shifted, _ = lax.optimization_barrier(
        (from_left, from_right, shifted, near)
    )

    opposite_one = to_right(from_left[:, :half])
    opposite_two = to_left(from_right[:, half:])

    def beside_payload(k):
        energies = jnp.broadcast_to(pick_block(shifted, k)[None, :], (8, width))
        return jnp.concatenate(
            [pick_block(from_left, k), pick_block(from_right, k), energies], axis=0
        )

    beside = exchange([beside_payload(k) for k in range(PARTNERS)])
    integrals = integral_call(
        meta, [from_left, from_right], beside, integrals, "integrals_beside"
    )
    second_row = jnp.stack([a[2 * aux_rows] for a in beside])

    across = exchange(
        [
            jnp.concatenate([pick_block(opposite_one, k), pick_block(opposite_two, k)], axis=0)
            for k in range(PARTNERS)
        ],
        lanes=5,
    )
    u_high, u_low, energy, own_across, far_across = middle_call(
        meta, [opposite_one, opposite_two], across, integrals, shifted, second_row, "amplitudes"
    )
    u = (u_high, u_low)
    arrived_across = exchange(far_across, lanes=5)

    own_beside, far_beside = density_call(
        meta, [from_left, from_right], beside, u, "density_beside"
    )
    out_right, out_left = sum_call(chosen, own_across, arrived_across, "sum_across", cuts=2)
    carried_right = to_right(out_right)
    carried_left = to_left(out_left)
    arrived_beside = exchange(far_beside)

    own_near, far_near = density_call(meta, [blocks], near, u, "density_near")
    (sum_right,) = sum_call(
        chosen, own_beside[1], arrived_beside, "sum_right", at=aux_rows,
        extra=carried_right, extra_at=0,
    )
    home_one = to_right(sum_right)
    (sum_left,) = sum_call(
        chosen, own_beside[0], arrived_beside, "sum_left", at=0,
        extra=carried_left, extra_at=half,
    )
    home_two = to_left(sum_left)
    arrived_near = exchange(far_near)
    (sum_near,) = sum_call(chosen, own_near[0], arrived_near, "sum_near")
    density = sum_near + home_one + home_two

    pair_energy = jnp.sum(energy, axis=(1, 2)) / width
    pair_energy = jnp.where(order < count, pair_energy, 0.0)
    spread = jnp.sum(jnp.where(at_place.T, pair_energy[None, :], 0.0), axis=1)
    for step in (1, 2):
        spread = spread + lax.ppermute(
            spread, "aux", [(s, s ^ step) for s in range(aux_size)]
        )
    return density, spread


def solution(mesh):
    placed = (P("orb", "aux", None), P("orb"), P(), P("orb", None), P("orb"), P("orb"))
    return jax.shard_map(
        functools.partial(shards, mesh.shape["orb"]),
        mesh=mesh,
        in_specs=placed,
        out_specs=(P("orb", "aux", None), P("orb")),
        check_vma=False,
    )
```

```python
import functools

import jax
import jax.numpy as jnp
from jax import lax
from jax.experimental import pallas as pl
from jax.experimental.pallas import tpu as pltpu
from jax.sharding import PartitionSpec as P

PARTNERS = 8
LOW_BITS = (2, 6, 4, 1, 3, 7, 5, 0)
VMEM_BYTES = 56 * 1024 * 1024
f32 = jnp.float32
bf16 = jnp.bfloat16


def split(x):
    high = x.astype(bf16)
    return high, (x - high.astype(f32)).astype(bf16)


def dot3(a, b, dims):
    dot = functools.partial(
        lax.dot_general, dimension_numbers=(dims, ((), ())), preferred_element_type=f32
    )
    return dot(a[0], b[0]) + dot(a[0], b[1]) + dot(a[1], b[0])


TN = ((0,), (0,))
NN = ((1,), (0,))
NT = ((1,), (1,))


VMEM = pl.BlockSpec(memory_space=pltpu.VMEM)
SMEM = pl.BlockSpec(memory_space=pltpu.SMEM)
HBM = pl.BlockSpec(memory_space=pl.ANY)
DMA = pltpu.SemaphoreType.DMA


def start_all(copies):
    for copy in copies:
        copy.start()


def wait_all(copies):
    for copy in copies:
        copy.wait()


def load(parts, firsts, seconds, f_in, s_in, f_sem, s_sem):
    rows = s_in.shape[1]
    s_copies = [
        pltpu.make_async_copy(ref.at[pl.ds(0, rows)], s_in.at[k], s_sem.at[k])
        for k, ref in enumerate(seconds)
    ]
    f_copies = []
    at = 0
    for q, ref in enumerate(firsts):
        window = pl.ds(at, ref.shape[1])
        f_copies.append(pltpu.make_async_copy(ref, f_in.at[:, window], f_sem.at[q]))
        at += ref.shape[1]
    start_all(s_copies + f_copies)
    return s_copies, f_copies


def split_first(meta, step, f_in, f_high, f_low):
    i = meta[0, step]
    before = meta[0, jnp.maximum(step, 1) - 1]

    @pl.when((step == 0) | (i != before))
    def _():
        f_high[...], f_low[...] = split(f_in[i])

    return (f_high[...], f_low[...])


def integral_kernel(parts, first_call, meta, *refs):
    firsts, refs = refs[:parts], refs[parts:]
    seconds, refs = refs[:PARTNERS], refs[PARTNERS:]
    before, refs = (None, refs) if first_call else (refs[0], refs[1:])
    out, f_in, s_in, f_high, f_low, s_high, s_low, k_buf, f_sem, s_sem, k_sem, o_sem = refs
    count = meta[2, 0]
    into = lambda r: pltpu.make_async_copy(before.at[r], k_buf.at[r], k_sem.at[r])
    back = lambda r: pltpu.make_async_copy(k_buf.at[r], out.at[r], o_sem.at[r])
    s_copies, f_copies = load(parts, firsts, seconds, f_in, s_in, f_sem, s_sem)
    if not first_call:
        pl.loop(0, count)(lambda r: into(r).start())
    for k in range(PARTNERS):
        s_copies[k].wait()
        s_high[k], s_low[k] = split(s_in[k].T)
    wait_all(f_copies)

    @pl.loop(0, count)
    def _(r):
        k = meta[1, r]
        f = split_first(meta, r, f_in, f_high, f_low)
        total = dot3((s_high[k], s_low[k]), f, NN)
        if not first_call:
            into(r).wait()
            total = total + k_buf[r]
        k_buf[r] = total
        back(r).start()

    pl.loop(0, count)(lambda r: back(r).wait())


def density_terms(i, k, f, s, u, own, far):
    rows = own.shape[2]
    for q in range(own.shape[0]):
        part = slice(q * rows, (q + 1) * rows)
        own[q, i] += dot3((s[0][part], s[1][part]), u, NN)
    far[k] += dot3(f, u, NT)


def middle_kernel(parts, meta, *refs):
    firsts, refs = refs[:parts], refs[parts:]
    seconds, refs = refs[:PARTNERS], refs[PARTNERS:]
    before, first_row, second_row, u_high, u_low, energy, own = refs[:7]
    far_outs, refs = refs[7 : 7 + PARTNERS], refs[7 + PARTNERS :]
    (f_in, s_in, f_high, f_low, s_high, s_low, k_buf, f_sem, s_sem, k_sem, far, column,
     t_high, t_low, uh_buf, ul_buf, h_sem, l_sem, far_sem) = refs
    count = meta[2, 0]
    into = lambda r: pltpu.make_async_copy(before.at[r], k_buf.at[r], k_sem.at[r])
    high = lambda r: pltpu.make_async_copy(uh_buf.at[r], u_high.at[r], h_sem.at[r])
    low = lambda r: pltpu.make_async_copy(ul_buf.at[r], u_low.at[r], l_sem.at[r])
    s_copies, f_copies = load(parts, firsts, seconds, f_in, s_in, f_sem, s_sem)
    pl.loop(0, count)(lambda r: into(r).start())
    own[...] = jnp.zeros_like(own)
    far[...] = jnp.zeros_like(far)
    width = far.shape[2]
    lanes = column.shape[2]
    for k in range(PARTNERS):
        column[k] = jnp.broadcast_to(second_row[k : k + 1, :], (lanes, width)).T
    for k in range(PARTNERS):
        s_copies[k].wait()
        s = s_in[k]
        s_high[k], s_low[k] = split(s)
        t_high[k], t_low[k] = split(s.T)
    wait_all(f_copies)

    @pl.loop(0, count)
    def _(r):
        i = meta[0, r]
        k = meta[1, r]
        f = split_first(meta, r, f_in, f_high, f_low)
        total = dot3((t_high[k], t_low[k]), f, NN)
        into(r).wait()
        total = total + k_buf[r]
        side = jnp.concatenate([column[k]] * (width // lanes), axis=1)
        amplitude = -total / (side + first_row[pl.ds(i, 1), :])
        tilde = 2.0 * amplitude - amplitude.T
        energy[r] = jnp.sum((total * tilde).reshape(width // 8, 8, width), axis=0)
        u = split(tilde)
        uh_buf[r], ul_buf[r] = u
        high(r).start()
        low(r).start()
        density_terms(i, k, f, (s_high[k], s_low[k]), u, own, far)

    outs = [
        pltpu.make_async_copy(far.at[k], far_outs[k], far_sem.at[k]) for k in range(PARTNERS)
    ]
    start_all(outs)

    @pl.loop(0, count)
    def _(r):
        high(r).wait()
        low(r).wait()

    wait_all(outs)


def density_kernel(parts, meta, *refs):
    firsts, refs = refs[:parts], refs[parts:]
    seconds, refs = refs[:PARTNERS], refs[PARTNERS:]
    u_high, u_low, own = refs[:3]
    far_outs, refs = refs[3 : 3 + PARTNERS], refs[3 + PARTNERS :]
    (f_in, s_in, f_high, f_low, s_high, s_low, f_sem, s_sem, far, uh_buf, ul_buf, h_sem,
     l_sem, far_sem) = refs
    count = meta[2, 0]
    high = lambda r: pltpu.make_async_copy(u_high.at[r], uh_buf.at[r], h_sem.at[r])
    low = lambda r: pltpu.make_async_copy(u_low.at[r], ul_buf.at[r], l_sem.at[r])
    s_copies, f_copies = load(parts, firsts, seconds, f_in, s_in, f_sem, s_sem)

    @pl.loop(0, count)
    def _(r):
        high(r).start()
        low(r).start()

    own[...] = jnp.zeros_like(own)
    far[...] = jnp.zeros_like(far)
    for k in range(PARTNERS):
        s_copies[k].wait()
        s_high[k], s_low[k] = split(s_in[k])
    wait_all(f_copies)

    @pl.loop(0, count)
    def _(r):
        k = meta[1, r]
        f = split_first(meta, r, f_in, f_high, f_low)
        high(r).wait()
        low(r).wait()
        u = (uh_buf[r], ul_buf[r])
        density_terms(meta[0, r], k, f, (s_high[k], s_low[k]), u, own, far)

    outs = [
        pltpu.make_async_copy(far.at[k], far_outs[k], far_sem.at[k]) for k in range(PARTNERS)
    ]
    start_all(outs)
    wait_all(outs)


def kernel_call(kernel, ins, outs, scratch, flops, moved, name):
    return pl.pallas_call(
        kernel,
        in_specs=[spec for _, spec in ins],
        out_specs=[spec for _, spec in outs],
        scratch_shapes=scratch,
        out_shape=[s for s, _ in outs],
        compiler_params=pltpu.CompilerParams(vmem_limit_bytes=VMEM_BYTES),
        cost_estimate=pl.CostEstimate(flops=flops, bytes_accessed=moved, transcendentals=0),
        name=name,
    )(*[a for a, _ in ins])


def block_scratch(orb_dev, rows, width):
    return [
        pltpu.VMEM((orb_dev, rows, width), f32),
        pltpu.VMEM((PARTNERS, rows, width), f32),
        pltpu.VMEM((rows, width), bf16),
        pltpu.VMEM((rows, width), bf16),
    ]


def integral_call(meta, firsts, seconds, before, name):
    orb_dev, _, width = firsts[0].shape
    rows = sum(f.shape[1] for f in firsts)
    pairs = meta.shape[1]
    shape = jax.ShapeDtypeStruct((pairs, width, width), f32)
    earlier = [] if before is None else [before]
    (out,) = kernel_call(
        functools.partial(integral_kernel, len(firsts), before is None),
        [(meta, SMEM)] + [(a, HBM) for a in [*firsts, *seconds, *earlier]],
        [(shape, HBM)],
        block_scratch(orb_dev, rows, width)
        + [pltpu.VMEM((PARTNERS, width, rows), bf16)] * 2
        + [pltpu.VMEM((pairs, width, width), f32)]
        + [DMA((len(firsts),)), DMA((PARTNERS,)), DMA((pairs,)), DMA((pairs,))],
        6 * 16 * width * width * rows, 16 * 1024 * 1024, name,
    )
    return out


def middle_call(meta, firsts, seconds, before, first_row, second_row, name):
    orb_dev, _, width = firsts[0].shape
    rows = sum(f.shape[1] for f in firsts)
    pairs = meta.shape[1]
    u_shape = jax.ShapeDtypeStruct((pairs, width, width), bf16)
    far_shape = jax.ShapeDtypeStruct((rows, width), f32)
    outs = kernel_call(
        functools.partial(middle_kernel, len(firsts)),
        [(meta, SMEM)] + [(a, HBM) for a in [*firsts, *seconds, before]]
        + [(first_row, VMEM), (second_row, VMEM)],
        [(u_shape, HBM), (u_shape, HBM), (jax.ShapeDtypeStruct((pairs, 8, width), f32), VMEM)]
        + [(jax.ShapeDtypeStruct((len(firsts), orb_dev, rows // len(firsts), width), f32), VMEM)]
        + [(far_shape, HBM)] * PARTNERS,
        block_scratch(orb_dev, rows, width)
        + [pltpu.VMEM((PARTNERS, rows, width), bf16)] * 2
        + [pltpu.VMEM((pairs, width, width), f32)]
        + [DMA((len(firsts),)), DMA((PARTNERS,)), DMA((pairs,))]
        + [pltpu.VMEM((PARTNERS, rows, width), f32)]
        + [pltpu.VMEM((PARTNERS, width, min(128, width)), f32)]
        + [pltpu.VMEM((PARTNERS, width, rows), bf16)] * 2
        + [pltpu.VMEM((pairs, width, width), bf16)] * 2
        + [DMA((pairs,)), DMA((pairs,)), DMA((PARTNERS,))],
        18 * 16 * width * width * rows, 24 * 1024 * 1024, name,
    )
    return outs[0], outs[1], outs[2], outs[3], outs[4:]


def density_call(meta, firsts, seconds, u, name):
    orb_dev, _, width = firsts[0].shape
    rows = sum(f.shape[1] for f in firsts)
    pairs = meta.shape[1]
    own_shape = jax.ShapeDtypeStruct((len(firsts), orb_dev, rows // len(firsts), width), f32)
    outs = kernel_call(
        functools.partial(density_kernel, len(firsts)),
        [(meta, SMEM)] + [(a, HBM) for a in [*firsts, *seconds, *u]],
        [(own_shape, VMEM)]
        + [(jax.ShapeDtypeStruct((rows, width), f32), HBM)] * PARTNERS,
        block_scratch(orb_dev, rows, width)
        + [pltpu.VMEM((PARTNERS, rows, width), bf16)] * 2
        + [DMA((len(firsts),)), DMA((PARTNERS,))]
        + [pltpu.VMEM((PARTNERS, rows, width), f32)]
        + [pltpu.VMEM((pairs, width, width), bf16)] * 2
        + [DMA((pairs,)), DMA((pairs,)), DMA((PARTNERS,))],
        12 * 16 * width * width * rows, 24 * 1024 * 1024, name,
    )
    return outs[0], outs[1:]


def sum_kernel(chosen, own, *refs):
    parts, _, rows, _ = own.shape
    arrived, refs = refs[:PARTNERS], refs[PARTNERS:]
    buf, sem = refs[-2:]
    extra, outs = refs[: -2 - parts], refs[-2 - parts : -2]
    copies = [
        pltpu.make_async_copy(ref.at[pl.ds(0, parts * rows)], buf.at[k], sem.at[k])
        for k, ref in enumerate(arrived)
    ]
    start_all(copies)
    for q in range(parts):
        outs[q][...] = own[q] + extra[q][...] if extra else own[q]
    for k in range(PARTNERS):
        copies[k].wait()
        for q in range(parts):
            outs[q][chosen[k]] += buf[k, q * rows : (q + 1) * rows, :]


def sum_call(chosen, own, arrived, extra, name):
    parts, orb_dev, rows, width = own.shape
    shape = jax.ShapeDtypeStruct((orb_dev, rows, width), f32)
    return kernel_call(
        sum_kernel,
        [(chosen, SMEM), (own, VMEM)]
        + [(a, HBM) for a in arrived]
        + [(e, VMEM) for e in extra],
        [(shape, VMEM)] * parts,
        [pltpu.VMEM((PARTNERS, parts * rows, width), f32), DMA((PARTNERS,))],
        0, 12 * 1024 * 1024, name,
    )


def shards(orb_size, blocks, occ_energy, vir_table, domain, pair_i, pair_j):
    orb_dev, aux_rows, width = blocks.shape
    pair_dev = pair_i.shape[0]
    p = lax.axis_index("orb")
    x = lax.axis_index("aux")
    aux_size = 4
    half = aux_rows // 2

    ring = [(s, (s + 1) % aux_size) for s in range(aux_size)]
    back = [(t, s) for s, t in ring]
    to_right = lambda a: lax.ppermute(a, "aux", ring)
    to_left = lambda a: lax.ppermute(a, "aux", back)

    def mask_of(k, at):
        low = LOW_BITS[k]
        return (((low >> 1) ^ at) << 3) | low

    tables = [
        [
            (o * aux_size + s, (o ^ mask_of(k, s)) * aux_size + s)
            for o in range(orb_size)
            for s in range(aux_size)
        ]
        for k in range(PARTNERS)
    ]

    def exchange(payloads, lanes=3):
        out = []
        for k, payload in enumerate(payloads):
            if k >= lanes:
                payload, _ = lax.optimization_barrier((payload, out[k - lanes]))
            out.append(lax.ppermute(payload, ("orb", "aux"), tables[k]))
        return out

    rows_a, rows_b = blocks[:, :half], blocks[:, half:]
    left_a = to_right(rows_a)
    right_b = to_left(rows_b)

    first_local = pair_i - p * orb_dev
    holder = pair_j // orb_dev
    second_local = pair_j % orb_dev
    device_ids = jnp.arange(orb_size, dtype=jnp.int32)
    held_by = holder[:, None] == device_ids[None, :]
    wanted = jnp.max(jnp.where(held_by, second_local[:, None], -1), axis=0)
    requested = lax.all_to_all(wanted, "orb", split_axis=0, concat_axis=0, tiled=True)
    partners = jnp.stack([p ^ mask_of(k, x) for k in range(PARTNERS)])
    chosen = jnp.clip(requested[partners], 0, orb_dev - 1)

    apart = holder ^ p
    mine = ((apart >> 3) ^ ((apart >> 1) & 3)) == x
    slot = sum(jnp.where((apart & 7) == low, k, 0) for k, low in enumerate(LOW_BITS))
    order = jnp.arange(pair_dev, dtype=jnp.int32)
    key = jnp.where(mine, first_local, orb_dev) * pair_dev + order
    place = jnp.sum((key[None, :] < key[:, None]).astype(jnp.int32), axis=1)
    at_place = place[None, :] == order[:, None]
    pick = lambda v: jnp.sum(jnp.where(at_place, v[None, :], 0), axis=1)
    count = jnp.sum(mine.astype(jnp.int32))
    meta = jnp.stack([pick(first_local), pick(slot), jnp.broadcast_to(count, (pair_dev,))])

    pick_block = lambda a, k: lax.dynamic_index_in_dim(a, chosen[k], 0, keepdims=False)

    def payloads(*arrays):
        return [
            jnp.concatenate([pick_block(a, k) for a in arrays], axis=0) for k in range(PARTNERS)
        ]

    def after(value, *earlier):
        return lax.optimization_barrier((value, earlier))[0]

    near = exchange([pick_block(blocks, k) for k in range(PARTNERS)])
    integrals = integral_call(meta, [blocks], near, None, "integrals_near")

    virtual = jnp.take(vir_table, after(domain, near[1]), axis=0)
    shifted = virtual - occ_energy[:, None]

    set_a = after((left_a, right_b), near, shifted)
    opposite = (to_right(set_a[0]), to_left(set_a[1]))
    energies = jnp.broadcast_to(shifted[:, None, :], (orb_dev, 8, width))
    got_a = exchange(payloads(*set_a, energies))
    integrals_near = integrals
    integrals = integral_call(meta, set_a, got_a, integrals, "integrals_a")
    integrals_a = integrals
    second_row = jnp.stack([a[2 * half] for a in got_a])

    opposite = after(opposite, got_a, integrals_near)
    set_c = after((rows_b, rows_a), opposite)
    set_c = (to_right(set_c[0]), to_left(set_c[1]))
    got_o = exchange(payloads(*opposite))
    integrals = integral_call(meta, opposite, got_o, integrals, "integrals_o")

    set_c = after(set_c, got_o, integrals_a)
    got_c = exchange(payloads(*set_c), lanes=PARTNERS)
    u_high, u_low, energy, own_c, far_c = middle_call(
        meta, set_c, got_c, integrals, shifted, second_row, "amplitudes"
    )

    back_c = exchange(far_c, lanes=PARTNERS)
    pair_energy = jnp.sum(energy, axis=(1, 2)) / width
    pair_energy = jnp.where(order < count, pair_energy, 0.0)
    spread = jnp.sum(jnp.where(at_place.T, pair_energy[None, :], 0.0), axis=1)
    for step in (1, 2):
        spread = spread + lax.ppermute(
            spread, "aux", [(s, s ^ step) for s in range(aux_size)]
        )
    own_o, far_o = density_call(
        meta, opposite, got_o, (after(u_high, back_c[2]), u_low), "density_o"
    )
    back_c, far_o = after((back_c, far_o), spread)
    sum_left_b, sum_right_a = sum_call(chosen, own_c, back_c, [], "sum_c")
    home_b = to_left(sum_left_b)
    home_a = to_right(sum_right_a)

    back_o = exchange(far_o)
    own_a, far_a = density_call(
        meta, set_a, got_a, (after(u_high, back_o[4]), u_low), "density_a"
    )
    sum_o_a, sum_o_b = sum_call(chosen, own_o, back_o, [], "sum_o")
    sum_o_a, sum_o_b, far_a = after((sum_o_a, sum_o_b, far_a), home_a, home_b)
    carried_a = to_left(sum_o_a)
    carried_b = to_right(sum_o_b)

    back_a = exchange(far_a)
    own_near, far_near = density_call(
        meta, [blocks], near, (after(u_high, back_a[4]), u_low), "density_near"
    )
    carried_a, carried_b, far_near = after((carried_a, carried_b, far_near), back_a)
    sum_left_a, sum_right_b = sum_call(chosen, own_a, back_a, [carried_a, carried_b], "sum_a")
    last_a = to_left(sum_left_a)
    last_b = to_right(sum_right_b)

    back_near = exchange(far_near)
    home = jnp.concatenate([home_a, home_b], axis=1)
    (sum_near,) = sum_call(chosen, own_near, back_near, [home], "sum_near")
    density = sum_near + jnp.concatenate([last_a, last_b], axis=1)
    return density, spread


def solution(mesh):
    placed = (P("orb", "aux", None), P("orb"), P(), P("orb", None), P("orb"), P("orb"))
    return jax.shard_map(
        functools.partial(shards, mesh.shape["orb"]),
        mesh=mesh,
        in_specs=placed,
        out_specs=(P("orb", "aux", None), P("orb")),
        check_vma=False,
    )
```

```python
import functools

import jax
import jax.numpy as jnp
from jax import lax
from jax.experimental import pallas as pl
from jax.experimental.pallas import tpu as pltpu
from jax.sharding import PartitionSpec as P

PARTNERS = 8
LOW_BITS = (2, 6, 4, 1, 3, 7, 5, 0)
VMEM_BYTES = 56 * 1024 * 1024
f32 = jnp.float32
bf16 = jnp.bfloat16


def split(x):
    high = x.astype(bf16)
    return high, (x - high.astype(f32)).astype(bf16)


def dot3(a, b, dims):
    dot = functools.partial(
        lax.dot_general, dimension_numbers=(dims, ((), ())), preferred_element_type=f32
    )
    return dot(a[0], b[0]) + dot(a[0], b[1]) + dot(a[1], b[0])


TN = ((0,), (0,))
NN = ((1,), (0,))
NT = ((1,), (1,))


VMEM = pl.BlockSpec(memory_space=pltpu.VMEM)
SMEM = pl.BlockSpec(memory_space=pltpu.SMEM)
HBM = pl.BlockSpec(memory_space=pl.ANY)
DMA = pltpu.SemaphoreType.DMA


def start_all(copies):
    for copy in copies:
        copy.start()


def wait_all(copies):
    for copy in copies:
        copy.wait()


def load(parts, firsts, seconds, f_in, s_in, f_sem, s_sem):
    rows = s_in.shape[1]
    s_copies = [
        pltpu.make_async_copy(ref.at[pl.ds(0, rows)], s_in.at[k], s_sem.at[k])
        for k, ref in enumerate(seconds)
    ]
    f_copies = []
    at = 0
    for q, ref in enumerate(firsts):
        window = pl.ds(at, ref.shape[1])
        f_copies.append(pltpu.make_async_copy(ref, f_in.at[:, window], f_sem.at[q]))
        at += ref.shape[1]
    start_all(s_copies + f_copies)
    return s_copies, f_copies


def split_first(meta, step, f_in, f_high, f_low):
    i = meta[0, step]
    before = meta[0, jnp.maximum(step, 1) - 1]

    @pl.when((step == 0) | (i != before))
    def _():
        f_high[...], f_low[...] = split(f_in[i])

    return (f_high[...], f_low[...])


def integral_kernel(parts, first_call, meta, *refs):
    firsts, refs = refs[:parts], refs[parts:]
    seconds, refs = refs[:PARTNERS], refs[PARTNERS:]
    before, refs = (None, refs) if first_call else (refs[0], refs[1:])
    out, f_in, s_in, f_high, f_low, s_high, s_low, k_buf, f_sem, s_sem, k_sem, o_sem = refs
    count = meta[2, 0]
    into = lambda r: pltpu.make_async_copy(before.at[r], k_buf.at[r], k_sem.at[r])
    back = lambda r: pltpu.make_async_copy(k_buf.at[r], out.at[r], o_sem.at[r])
    s_copies, f_copies = load(parts, firsts, seconds, f_in, s_in, f_sem, s_sem)
    if not first_call:
        pl.loop(0, count)(lambda r: into(r).start())
    for k in range(PARTNERS):
        s_copies[k].wait()
        s_high[k], s_low[k] = split(s_in[k].T)
    wait_all(f_copies)

    @pl.loop(0, count)
    def _(r):
        k = meta[1, r]
        f = split_first(meta, r, f_in, f_high, f_low)
        total = dot3((s_high[k], s_low[k]), f, NN)
        if not first_call:
            into(r).wait()
            total = total + k_buf[r]
        k_buf[r] = total
        back(r).start()

    pl.loop(0, count)(lambda r: back(r).wait())


def write_absent(meta, own, own_outs, o_sem):
    for i in range(own.shape[1]):

        @pl.when(meta[3, i] == 0)
        def _():
            for q, out in enumerate(own_outs):
                pltpu.make_async_copy(own.at[q, i], out.at[i], o_sem.at[q, i]).start()


def write_complete(meta, r, own, own_outs, o_sem):
    i = meta[0, r]
    after = meta[0, jnp.minimum(r + 1, meta.shape[1] - 1)]

    @pl.when((r == meta[2, 0] - 1) | (after != i))
    def _():
        for q, out in enumerate(own_outs):
            pltpu.make_async_copy(own.at[q, i], out.at[i], o_sem.at[q, i]).start()


def wait_written(own, own_outs, o_sem):
    for i in range(own.shape[1]):
        for q, out in enumerate(own_outs):
            pltpu.make_async_copy(own.at[q, i], out.at[i], o_sem.at[q, i]).wait()


def density_terms(i, k, f, s, u, own, far):
    rows = own.shape[2]
    for q in range(own.shape[0]):
        part = slice(q * rows, (q + 1) * rows)
        own[q, i] += dot3((s[0][part], s[1][part]), u, NN)
    far[k] += dot3(f, u, NT)


def middle_kernel(parts, meta, *refs):
    firsts, refs = refs[:parts], refs[parts:]
    seconds, refs = refs[:PARTNERS], refs[PARTNERS:]
    before, first_row, second_row, u_high, u_low, energy = refs[:6]
    own_outs, refs = refs[6 : 6 + parts], refs[6 + parts :]
    far_outs, refs = refs[:PARTNERS], refs[PARTNERS:]
    (f_in, s_in, f_high, f_low, s_high, s_low, k_buf, f_sem, s_sem, k_sem, far, column,
     t_high, t_low, uh_buf, ul_buf, h_sem, l_sem, far_sem, own, o_sem) = refs
    count = meta[2, 0]
    into = lambda r: pltpu.make_async_copy(before.at[r], k_buf.at[r], k_sem.at[r])
    high = lambda r: pltpu.make_async_copy(uh_buf.at[r], u_high.at[r], h_sem.at[r])
    low = lambda r: pltpu.make_async_copy(ul_buf.at[r], u_low.at[r], l_sem.at[r])
    s_copies, f_copies = load(parts, firsts, seconds, f_in, s_in, f_sem, s_sem)
    pl.loop(0, count)(lambda r: into(r).start())
    own[...] = jnp.zeros_like(own)
    write_absent(meta, own, own_outs, o_sem)
    far[...] = jnp.zeros_like(far)
    width = far.shape[2]
    lanes = column.shape[2]
    for k in range(PARTNERS):
        column[k] = jnp.broadcast_to(second_row[k : k + 1, :], (lanes, width)).T
    for k in range(PARTNERS):
        s_copies[k].wait()
        s = s_in[k]
        s_high[k], s_low[k] = split(s)
        t_high[k], t_low[k] = split(s.T)
    wait_all(f_copies)

    @pl.loop(0, count)
    def _(r):
        i = meta[0, r]
        k = meta[1, r]
        f = split_first(meta, r, f_in, f_high, f_low)
        total = dot3((t_high[k], t_low[k]), f, NN)
        into(r).wait()
        total = total + k_buf[r]
        side = jnp.concatenate([column[k]] * (width // lanes), axis=1)
        amplitude = -total / (side + first_row[pl.ds(i, 1), :])
        tilde = 2.0 * amplitude - amplitude.T
        energy[r] = jnp.sum((total * tilde).reshape(width // 8, 8, width), axis=0)
        u = split(tilde)
        uh_buf[r], ul_buf[r] = u
        high(r).start()
        low(r).start()
        density_terms(i, k, f, (s_high[k], s_low[k]), u, own, far)
        write_complete(meta, r, own, own_outs, o_sem)

    outs = [
        pltpu.make_async_copy(far.at[k], far_outs[k], far_sem.at[k]) for k in range(PARTNERS)
    ]
    start_all(outs)

    @pl.loop(0, count)
    def _(r):
        high(r).wait()
        low(r).wait()

    wait_all(outs)
    wait_written(own, own_outs, o_sem)


def density_kernel(parts, meta, *refs):
    firsts, refs = refs[:parts], refs[parts:]
    seconds, refs = refs[:PARTNERS], refs[PARTNERS:]
    u_high, u_low = refs[:2]
    own_outs, refs = refs[2 : 2 + parts], refs[2 + parts :]
    far_outs, refs = refs[:PARTNERS], refs[PARTNERS:]
    (f_in, s_in, f_high, f_low, s_high, s_low, f_sem, s_sem, far, uh_buf, ul_buf, h_sem,
     l_sem, far_sem, own, o_sem) = refs
    count = meta[2, 0]
    high = lambda r: pltpu.make_async_copy(u_high.at[r], uh_buf.at[r], h_sem.at[r])
    low = lambda r: pltpu.make_async_copy(u_low.at[r], ul_buf.at[r], l_sem.at[r])
    s_copies, f_copies = load(parts, firsts, seconds, f_in, s_in, f_sem, s_sem)

    @pl.loop(0, count)
    def _(r):
        high(r).start()
        low(r).start()

    own[...] = jnp.zeros_like(own)
    write_absent(meta, own, own_outs, o_sem)
    far[...] = jnp.zeros_like(far)
    for k in range(PARTNERS):
        s_copies[k].wait()
        s_high[k], s_low[k] = split(s_in[k])
    wait_all(f_copies)

    @pl.loop(0, count)
    def _(r):
        k = meta[1, r]
        f = split_first(meta, r, f_in, f_high, f_low)
        high(r).wait()
        low(r).wait()
        u = (uh_buf[r], ul_buf[r])
        density_terms(meta[0, r], k, f, (s_high[k], s_low[k]), u, own, far)
        write_complete(meta, r, own, own_outs, o_sem)

    outs = [
        pltpu.make_async_copy(far.at[k], far_outs[k], far_sem.at[k]) for k in range(PARTNERS)
    ]
    start_all(outs)
    wait_all(outs)
    wait_written(own, own_outs, o_sem)


def kernel_call(kernel, ins, outs, scratch, flops, moved, name):
    return pl.pallas_call(
        kernel,
        in_specs=[spec for _, spec in ins],
        out_specs=[spec for _, spec in outs],
        scratch_shapes=scratch,
        out_shape=[s for s, _ in outs],
        compiler_params=pltpu.CompilerParams(vmem_limit_bytes=VMEM_BYTES),
        cost_estimate=pl.CostEstimate(flops=flops, bytes_accessed=moved, transcendentals=0),
        name=name,
    )(*[a for a, _ in ins])


def block_scratch(orb_dev, rows, width):
    return [
        pltpu.VMEM((orb_dev, rows, width), f32),
        pltpu.VMEM((PARTNERS, rows, width), f32),
        pltpu.VMEM((rows, width), bf16),
        pltpu.VMEM((rows, width), bf16),
    ]


def integral_call(meta, firsts, seconds, before, name):
    orb_dev, _, width = firsts[0].shape
    rows = sum(f.shape[1] for f in firsts)
    pairs = meta.shape[1]
    shape = jax.ShapeDtypeStruct((pairs, width, width), f32)
    earlier = [] if before is None else [before]
    (out,) = kernel_call(
        functools.partial(integral_kernel, len(firsts), before is None),
        [(meta, SMEM)] + [(a, HBM) for a in [*firsts, *seconds, *earlier]],
        [(shape, HBM)],
        block_scratch(orb_dev, rows, width)
        + [pltpu.VMEM((PARTNERS, width, rows), bf16)] * 2
        + [pltpu.VMEM((pairs, width, width), f32)]
        + [DMA((len(firsts),)), DMA((PARTNERS,)), DMA((pairs,)), DMA((pairs,))],
        6 * 16 * width * width * rows, 16 * 1024 * 1024, name,
    )
    return out


def middle_call(meta, firsts, seconds, before, first_row, second_row, name):
    orb_dev, _, width = firsts[0].shape
    rows = sum(f.shape[1] for f in firsts)
    pairs = meta.shape[1]
    u_shape = jax.ShapeDtypeStruct((pairs, width, width), bf16)
    far_shape = jax.ShapeDtypeStruct((rows, width), f32)
    outs = kernel_call(
        functools.partial(middle_kernel, len(firsts)),
        [(meta, SMEM)] + [(a, HBM) for a in [*firsts, *seconds, before]]
        + [(first_row, VMEM), (second_row, VMEM)],
        [(u_shape, HBM), (u_shape, HBM), (jax.ShapeDtypeStruct((pairs, 8, width), f32), VMEM)]
        + [(jax.ShapeDtypeStruct(f.shape, f32), HBM) for f in firsts]
        + [(far_shape, HBM)] * PARTNERS,
        block_scratch(orb_dev, rows, width)
        + [pltpu.VMEM((PARTNERS, rows, width), bf16)] * 2
        + [pltpu.VMEM((pairs, width, width), f32)]
        + [DMA((len(firsts),)), DMA((PARTNERS,)), DMA((pairs,))]
        + [pltpu.VMEM((PARTNERS, rows, width), f32)]
        + [pltpu.VMEM((PARTNERS, width, min(128, width)), f32)]
        + [pltpu.VMEM((PARTNERS, width, rows), bf16)] * 2
        + [pltpu.VMEM((pairs, width, width), bf16)] * 2
        + [DMA((pairs,)), DMA((pairs,)), DMA((PARTNERS,))]
        + [pltpu.VMEM((len(firsts),) + firsts[0].shape, f32), DMA((len(firsts), orb_dev))],
        18 * 16 * width * width * rows, 24 * 1024 * 1024, name,
    )
    cut = 3 + len(firsts)
    return outs[0], outs[1], outs[2], outs[3:cut], outs[cut:]


def density_call(meta, firsts, seconds, u, name):
    orb_dev, _, width = firsts[0].shape
    rows = sum(f.shape[1] for f in firsts)
    pairs = meta.shape[1]
    outs = kernel_call(
        functools.partial(density_kernel, len(firsts)),
        [(meta, SMEM)] + [(a, HBM) for a in [*firsts, *seconds, *u]],
        [(jax.ShapeDtypeStruct(f.shape, f32), HBM) for f in firsts]
        + [(jax.ShapeDtypeStruct((rows, width), f32), HBM)] * PARTNERS,
        block_scratch(orb_dev, rows, width)
        + [pltpu.VMEM((PARTNERS, rows, width), bf16)] * 2
        + [DMA((len(firsts),)), DMA((PARTNERS,))]
        + [pltpu.VMEM((PARTNERS, rows, width), f32)]
        + [pltpu.VMEM((pairs, width, width), bf16)] * 2
        + [DMA((pairs,)), DMA((pairs,)), DMA((PARTNERS,))]
        + [pltpu.VMEM((len(firsts),) + firsts[0].shape, f32), DMA((len(firsts), orb_dev))],
        12 * 16 * width * width * rows, 24 * 1024 * 1024, name,
    )
    return outs[: len(firsts)], outs[len(firsts) :]


def sum_kernel(parts, chosen, *refs):
    own, refs = refs[:parts], refs[parts:]
    rows = own[0].shape[1]
    arrived, refs = refs[:PARTNERS], refs[PARTNERS:]
    buf, sem = refs[-2:]
    extra, outs = refs[: -2 - parts], refs[-2 - parts : -2]
    copies = [
        pltpu.make_async_copy(ref.at[pl.ds(0, parts * rows)], buf.at[k], sem.at[k])
        for k, ref in enumerate(arrived)
    ]
    start_all(copies)
    for q in range(parts):
        outs[q][...] = own[q][...] + extra[q][...] if extra else own[q][...]
    for k in range(PARTNERS):
        copies[k].wait()
        for q in range(parts):
            outs[q][chosen[k]] += buf[k, q * rows : (q + 1) * rows, :]


def sum_call(chosen, own, arrived, extra, name):
    parts = len(own)
    orb_dev, rows, width = own[0].shape
    shape = jax.ShapeDtypeStruct((orb_dev, rows, width), f32)
    return kernel_call(
        functools.partial(sum_kernel, parts),
        [(chosen, SMEM)]
        + [(o, VMEM) for o in own]
        + [(a, HBM) for a in arrived]
        + [(e, VMEM) for e in extra],
        [(shape, VMEM)] * parts,
        [pltpu.VMEM((PARTNERS, parts * rows, width), f32), DMA((PARTNERS,))],
        0, 12 * 1024 * 1024, name,
    )


def pick_kernel(parts, chosen, *refs):
    sources, outs, sem = refs[:parts], refs[parts:-1], refs[-1]
    copies = []
    for k, out in enumerate(outs):
        at = 0
        for q, source in enumerate(sources):
            rows = source.shape[1]
            copies.append(
                pltpu.make_async_copy(source.at[chosen[k]], out.at[pl.ds(at, rows)], sem.at[k, q])
            )
            at += rows
    start_all(copies)
    wait_all(copies)


def pick_call(chosen, sources, name):
    rows = sum(a.shape[1] for a in sources)
    shape = jax.ShapeDtypeStruct((rows, sources[0].shape[2]), f32)
    return kernel_call(
        functools.partial(pick_kernel, len(sources)),
        [(chosen, SMEM)] + [(a, HBM) for a in sources],
        [(shape, HBM)] * PARTNERS,
        [DMA((PARTNERS, len(sources)))],
        0, 4 * 1024 * 1024, name,
    )


def look_up(table, index):
    lanes = 128
    high = (index // lanes).reshape(-1, 1) == jnp.arange(table.size // lanes, dtype=jnp.int32)
    low = (index % lanes).reshape(-1, 1) == jnp.arange(lanes, dtype=jnp.int32)
    rows = jnp.dot(
        high.astype(f32), table.reshape(-1, lanes), precision=lax.Precision.HIGHEST
    )
    return jnp.sum(jnp.where(low, rows, 0.0), axis=1).reshape(index.shape)


def shards(orb_size, blocks, occ_energy, vir_table, domain, pair_i, pair_j):
    orb_dev, aux_rows, width = blocks.shape
    pair_dev = pair_i.shape[0]
    p = lax.axis_index("orb")
    x = lax.axis_index("aux")
    aux_size = 4
    half = aux_rows // 2

    ring = [(s, (s + 1) % aux_size) for s in range(aux_size)]
    back = [(t, s) for s, t in ring]
    to_right = lambda a: lax.ppermute(a, "aux", ring)
    to_left = lambda a: lax.ppermute(a, "aux", back)

    def mask_of(k, at):
        low = LOW_BITS[k]
        return (((low >> 1) ^ at) << 3) | low

    tables = [
        [
            (o * aux_size + s, (o ^ mask_of(k, s)) * aux_size + s)
            for o in range(orb_size)
            for s in range(aux_size)
        ]
        for k in range(PARTNERS)
    ]

    def exchange(payloads, lanes=3):
        out = []
        for k, payload in enumerate(payloads):
            if k >= lanes:
                payload, _ = lax.optimization_barrier((payload, out[k - lanes]))
            out.append(lax.ppermute(payload, ("orb", "aux"), tables[k]))
        return out

    rows_a, rows_b = blocks[:, :half], blocks[:, half:]
    left_a = to_right(rows_a)
    right_b = to_left(rows_b)

    first_local = pair_i - p * orb_dev
    holder = pair_j // orb_dev
    second_local = pair_j % orb_dev
    device_ids = jnp.arange(orb_size, dtype=jnp.int32)
    held_by = holder[:, None] == device_ids[None, :]
    wanted = jnp.max(jnp.where(held_by, second_local[:, None], -1), axis=0)
    requested = lax.all_to_all(wanted, "orb", split_axis=0, concat_axis=0, tiled=True)
    low_bits = jnp.array(LOW_BITS, dtype=jnp.int32)
    partners = p ^ ((((low_bits >> 1) ^ x) << 3) | low_bits)
    virtual = look_up(vir_table, domain)
    shifted = virtual - occ_energy[:, None]
    requested = lax.optimization_barrier((requested, shifted))[0]
    chosen = jnp.clip(requested[partners], 0, orb_dev - 1)

    apart = holder ^ p
    mine = ((apart >> 3) ^ ((apart >> 1) & 3)) == x
    slot = sum(jnp.where((apart & 7) == low, k, 0) for k, low in enumerate(LOW_BITS))
    order = jnp.arange(pair_dev, dtype=jnp.int32)
    key = jnp.where(mine, first_local, orb_dev) * pair_dev + order
    place = jnp.sum((key[None, :] < key[:, None]).astype(jnp.int32), axis=1)
    at_place = place[None, :] == order[:, None]
    pick = lambda v: jnp.sum(jnp.where(at_place, v[None, :], 0), axis=1)
    count = jnp.sum(mine.astype(jnp.int32))
    present = jnp.any((first_local[None, :] == order[:, None]) & mine[None, :], axis=1)
    meta = jnp.stack(
        [
            pick(first_local), pick(slot), jnp.broadcast_to(count, (pair_dev,)),
            present.astype(jnp.int32),
        ]
    )

    def after(value, *earlier):
        return lax.optimization_barrier((value, earlier))[0]

    near = exchange(pick_call(chosen, [blocks], "pick_near"))
    integrals = integral_call(meta, [blocks], near, None, "integrals_near")

    set_a = after((left_a, right_b), near)
    opposite = (to_right(set_a[0]), to_left(set_a[1]))
    energies = jnp.broadcast_to(shifted[:, None, :], (orb_dev, 8, width))
    got_a = exchange(pick_call(chosen, [*set_a, energies], "pick_a"))
    integrals_near = integrals
    integrals = integral_call(meta, set_a, got_a, integrals, "integrals_a")
    integrals_a = integrals
    second_row = jnp.stack([a[2 * half] for a in got_a])

    opposite = after(opposite, got_a, integrals_near)
    set_c = after((rows_b, rows_a), opposite)
    set_c = (to_right(set_c[0]), to_left(set_c[1]))
    got_o = exchange(pick_call(chosen, opposite, "pick_o"))
    integrals = integral_call(meta, opposite, got_o, integrals, "integrals_o")

    set_c = after(set_c, got_o, integrals_a)
    got_c = exchange(pick_call(chosen, set_c, "pick_c"), lanes=PARTNERS)
    u_high, u_low, energy, own_c, far_c = middle_call(
        meta, set_c, got_c, integrals, shifted, second_row, "amplitudes"
    )

    back_c = exchange(far_c, lanes=PARTNERS)
    pair_energy = jnp.sum(energy, axis=(1, 2)) / width
    pair_energy = jnp.where(order < count, pair_energy, 0.0)
    spread = jnp.sum(jnp.where(at_place.T, pair_energy[None, :], 0.0), axis=1)
    for step in (1, 2):
        spread = spread + lax.ppermute(
            spread, "aux", [(s, s ^ step) for s in range(aux_size)]
        )
    own_o, far_o = density_call(
        meta, opposite, got_o, (after(u_high, back_c[2]), u_low), "density_o"
    )
    back_c, far_o = after((back_c, far_o), spread)
    sum_left_b, sum_right_a = sum_call(chosen, own_c, back_c, [], "sum_c")
    home_b = to_left(sum_left_b)
    home_a = to_right(sum_right_a)

    back_o = exchange(far_o)
    own_a, far_a = density_call(
        meta, set_a, got_a, (after(u_high, back_o[4]), u_low), "density_a"
    )
    sum_o_a, sum_o_b = sum_call(chosen, own_o, back_o, [], "sum_o")
    sum_o_a, sum_o_b, far_a = after((sum_o_a, sum_o_b, far_a), home_a, home_b)
    carried_a = to_left(sum_o_a)
    carried_b = to_right(sum_o_b)

    back_a = exchange(far_a)
    own_near, far_near = density_call(
        meta, [blocks], near, (after(u_high, back_a[4]), u_low), "density_near"
    )
    carried_a, carried_b, far_near = after((carried_a, carried_b, far_near), back_a)
    sum_left_a, sum_right_b = sum_call(chosen, own_a, back_a, [carried_a, carried_b], "sum_a")
    last_a = to_left(sum_left_a)
    last_b = to_right(sum_right_b)

    back_near = exchange(far_near)
    home = jnp.concatenate([home_a, home_b], axis=1)
    (sum_near,) = sum_call(chosen, own_near, back_near, [home], "sum_near")
    density = sum_near + jnp.concatenate([last_a, last_b], axis=1)
    return density, spread


def solution(mesh):
    placed = (P("orb", "aux", None), P("orb"), P(), P("orb", None), P("orb"), P("orb"))
    return jax.shard_map(
        functools.partial(shards, mesh.shape["orb"]),
        mesh=mesh,
        in_specs=placed,
        out_specs=(P("orb", "aux", None), P("orb")),
        check_vma=False,
    )
```

```python
import functools

import jax
import jax.numpy as jnp
from jax import lax
from jax.experimental import pallas as pl
from jax.experimental.pallas import tpu as pltpu
from jax.sharding import PartitionSpec as P

PARTNERS = 8
LOW_BITS = (2, 6, 4, 1, 3, 7, 5, 0)
VMEM_BYTES = 56 * 1024 * 1024
f32 = jnp.float32
bf16 = jnp.bfloat16


def split(x):
    high = x.astype(bf16)
    return high, (x - high.astype(f32)).astype(bf16)


def dot3(a, b, dims):
    dot = functools.partial(
        lax.dot_general, dimension_numbers=(dims, ((), ())), preferred_element_type=f32
    )
    return dot(a[0], b[0]) + dot(a[0], b[1]) + dot(a[1], b[0])


TN = ((0,), (0,))
NN = ((1,), (0,))
NT = ((1,), (1,))


VMEM = pl.BlockSpec(memory_space=pltpu.VMEM)
SMEM = pl.BlockSpec(memory_space=pltpu.SMEM)
HBM = pl.BlockSpec(memory_space=pl.ANY)
DMA = pltpu.SemaphoreType.DMA


def start_all(copies):
    for copy in copies:
        copy.start()


def wait_all(copies):
    for copy in copies:
        copy.wait()


def load(parts, firsts, seconds, f_in, s_in, f_sem, s_sem):
    rows = s_in.shape[1]
    s_copies = [
        pltpu.make_async_copy(ref.at[pl.ds(0, rows)], s_in.at[k], s_sem.at[k])
        for k, ref in enumerate(seconds)
    ]
    f_copies = []
    at = 0
    for q, ref in enumerate(firsts):
        window = pl.ds(at, ref.shape[1])
        f_copies.append(pltpu.make_async_copy(ref, f_in.at[:, window], f_sem.at[q]))
        at += ref.shape[1]
    start_all(s_copies + f_copies)
    return s_copies, f_copies


def split_first(meta, step, f_in, f_high, f_low):
    i = meta[0, step]
    before = meta[0, jnp.maximum(step, 1) - 1]

    @pl.when((step == 0) | (i != before))
    def _():
        f_high[...], f_low[...] = split(f_in[i])

    return (f_high[...], f_low[...])


def integral_kernel(parts, first_call, meta, *refs):
    firsts, refs = refs[:parts], refs[parts:]
    seconds, refs = refs[:PARTNERS], refs[PARTNERS:]
    before, refs = (None, refs) if first_call else (refs[0], refs[1:])
    out, f_in, s_in, f_high, f_low, s_high, s_low, k_buf, f_sem, s_sem, k_sem, o_sem = refs
    count = meta[2, 0]
    into = lambda r: pltpu.make_async_copy(before.at[r], k_buf.at[r], k_sem.at[r])
    back = lambda r: pltpu.make_async_copy(k_buf.at[r], out.at[r], o_sem.at[r])
    s_copies, f_copies = load(parts, firsts, seconds, f_in, s_in, f_sem, s_sem)
    if not first_call:
        pl.loop(0, count)(lambda r: into(r).start())
    for k in range(PARTNERS):
        s_copies[k].wait()
        s_high[k], s_low[k] = split(s_in[k].T)
    wait_all(f_copies)

    @pl.loop(0, count)
    def _(r):
        k = meta[1, r]
        f = split_first(meta, r, f_in, f_high, f_low)
        total = dot3((s_high[k], s_low[k]), f, NN)
        if not first_call:
            into(r).wait()
            total = total + k_buf[r]
        k_buf[r] = total
        back(r).start()

    pl.loop(0, count)(lambda r: back(r).wait())


def write_absent(meta, own, own_outs, o_sem):
    for i in range(own.shape[1]):

        @pl.when(meta[3, i] == 0)
        def _():
            for q, out in enumerate(own_outs):
                pltpu.make_async_copy(own.at[q, i], out.at[i], o_sem.at[q, i]).start()


def write_complete(meta, r, own, own_outs, o_sem):
    i = meta[0, r]
    after = meta[0, jnp.minimum(r + 1, meta.shape[1] - 1)]

    @pl.when((r == meta[2, 0] - 1) | (after != i))
    def _():
        for q, out in enumerate(own_outs):
            pltpu.make_async_copy(own.at[q, i], out.at[i], o_sem.at[q, i]).start()


def wait_written(own, own_outs, o_sem):
    for i in range(own.shape[1]):
        for q, out in enumerate(own_outs):
            pltpu.make_async_copy(own.at[q, i], out.at[i], o_sem.at[q, i]).wait()


def density_terms(i, k, f, s, u, own, far):
    rows = own.shape[2]
    for q in range(own.shape[0]):
        part = slice(q * rows, (q + 1) * rows)
        own[q, i] += dot3((s[0][part], s[1][part]), u, NN)
    far[k] += dot3(f, u, NT)


def middle_kernel(parts, meta, *refs):
    firsts, refs = refs[:parts], refs[parts:]
    seconds, refs = refs[:PARTNERS], refs[PARTNERS:]
    before, first_row, second_row, u_high, u_low, energy = refs[:6]
    own_outs, refs = refs[6 : 6 + parts], refs[6 + parts :]
    far_outs, refs = refs[:PARTNERS], refs[PARTNERS:]
    (f_in, s_in, f_high, f_low, s_high, s_low, k_buf, f_sem, s_sem, k_sem, far, column,
     t_high, t_low, uh_buf, ul_buf, h_sem, l_sem, far_sem, own, o_sem) = refs
    count = meta[2, 0]
    into = lambda r: pltpu.make_async_copy(before.at[r], k_buf.at[r], k_sem.at[r])
    high = lambda r: pltpu.make_async_copy(uh_buf.at[r], u_high.at[r], h_sem.at[r])
    low = lambda r: pltpu.make_async_copy(ul_buf.at[r], u_low.at[r], l_sem.at[r])
    s_copies, f_copies = load(parts, firsts, seconds, f_in, s_in, f_sem, s_sem)
    pl.loop(0, count)(lambda r: into(r).start())
    own[...] = jnp.zeros_like(own)
    write_absent(meta, own, own_outs, o_sem)
    far[...] = jnp.zeros_like(far)
    width = far.shape[2]
    lanes = column.shape[2]
    for k in range(PARTNERS):
        column[k] = jnp.broadcast_to(second_row[k : k + 1, :], (lanes, width)).T
    for k in range(PARTNERS):
        s_copies[k].wait()
        s = s_in[k]
        s_high[k], s_low[k] = split(s)
        t_high[k], t_low[k] = split(s.T)
    wait_all(f_copies)

    @pl.loop(0, count)
    def _(r):
        i = meta[0, r]
        k = meta[1, r]
        f = split_first(meta, r, f_in, f_high, f_low)
        total = dot3((t_high[k], t_low[k]), f, NN)
        into(r).wait()
        total = total + k_buf[r]
        side = jnp.concatenate([column[k]] * (width // lanes), axis=1)
        amplitude = -total / (side + first_row[pl.ds(i, 1), :])
        tilde = 2.0 * amplitude - amplitude.T
        energy[r] = jnp.sum((total * tilde).reshape(width // 8, 8, width), axis=0)
        u = split(tilde)
        uh_buf[r], ul_buf[r] = u
        high(r).start()
        low(r).start()
        density_terms(i, k, f, (s_high[k], s_low[k]), u, own, far)
        write_complete(meta, r, own, own_outs, o_sem)

    outs = [
        pltpu.make_async_copy(far.at[k], far_outs[k], far_sem.at[k]) for k in range(PARTNERS)
    ]
    start_all(outs)

    @pl.loop(0, count)
    def _(r):
        high(r).wait()
        low(r).wait()

    wait_all(outs)
    wait_written(own, own_outs, o_sem)


def density_kernel(parts, meta, *refs):
    firsts, refs = refs[:parts], refs[parts:]
    seconds, refs = refs[:PARTNERS], refs[PARTNERS:]
    u_high, u_low = refs[:2]
    own_outs, refs = refs[2 : 2 + parts], refs[2 + parts :]
    far_outs, refs = refs[:PARTNERS], refs[PARTNERS:]
    (f_in, s_in, f_high, f_low, s_high, s_low, f_sem, s_sem, far, uh_buf, ul_buf, h_sem,
     l_sem, far_sem, own, o_sem) = refs
    count = meta[2, 0]
    high = lambda r: pltpu.make_async_copy(u_high.at[r], uh_buf.at[r], h_sem.at[r])
    low = lambda r: pltpu.make_async_copy(u_low.at[r], ul_buf.at[r], l_sem.at[r])
    s_copies, f_copies = load(parts, firsts, seconds, f_in, s_in, f_sem, s_sem)

    @pl.loop(0, count)
    def _(r):
        high(r).start()
        low(r).start()

    own[...] = jnp.zeros_like(own)
    write_absent(meta, own, own_outs, o_sem)
    far[...] = jnp.zeros_like(far)
    for k in range(PARTNERS):
        s_copies[k].wait()
        s_high[k], s_low[k] = split(s_in[k])
    wait_all(f_copies)

    @pl.loop(0, count)
    def _(r):
        k = meta[1, r]
        f = split_first(meta, r, f_in, f_high, f_low)
        high(r).wait()
        low(r).wait()
        u = (uh_buf[r], ul_buf[r])
        density_terms(meta[0, r], k, f, (s_high[k], s_low[k]), u, own, far)
        write_complete(meta, r, own, own_outs, o_sem)

    outs = [
        pltpu.make_async_copy(far.at[k], far_outs[k], far_sem.at[k]) for k in range(PARTNERS)
    ]
    start_all(outs)
    wait_all(outs)
    wait_written(own, own_outs, o_sem)


def kernel_call(kernel, ins, outs, scratch, flops, moved, name):
    return pl.pallas_call(
        kernel,
        in_specs=[spec for _, spec in ins],
        out_specs=[spec for _, spec in outs],
        scratch_shapes=scratch,
        out_shape=[s for s, _ in outs],
        compiler_params=pltpu.CompilerParams(vmem_limit_bytes=VMEM_BYTES),
        cost_estimate=pl.CostEstimate(flops=flops, bytes_accessed=moved, transcendentals=0),
        name=name,
    )(*[a for a, _ in ins])


def block_scratch(orb_dev, rows, width):
    return [
        pltpu.VMEM((orb_dev, rows, width), f32),
        pltpu.VMEM((PARTNERS, rows, width), f32),
        pltpu.VMEM((rows, width), bf16),
        pltpu.VMEM((rows, width), bf16),
    ]


def integral_call(meta, firsts, seconds, before, name):
    orb_dev, _, width = firsts[0].shape
    rows = sum(f.shape[1] for f in firsts)
    pairs = meta.shape[1]
    shape = jax.ShapeDtypeStruct((pairs, width, width), f32)
    earlier = [] if before is None else [before]
    (out,) = kernel_call(
        functools.partial(integral_kernel, len(firsts), before is None),
        [(meta, SMEM)] + [(a, HBM) for a in [*firsts, *seconds, *earlier]],
        [(shape, HBM)],
        block_scratch(orb_dev, rows, width)
        + [pltpu.VMEM((PARTNERS, width, rows), bf16)] * 2
        + [pltpu.VMEM((pairs, width, width), f32)]
        + [DMA((len(firsts),)), DMA((PARTNERS,)), DMA((pairs,)), DMA((pairs,))],
        6 * 16 * width * width * rows, 16 * 1024 * 1024, name,
    )
    return out


def middle_call(meta, firsts, seconds, before, first_row, second_row, name):
    orb_dev, _, width = firsts[0].shape
    rows = sum(f.shape[1] for f in firsts)
    pairs = meta.shape[1]
    u_shape = jax.ShapeDtypeStruct((pairs, width, width), bf16)
    far_shape = jax.ShapeDtypeStruct((rows, width), f32)
    outs = kernel_call(
        functools.partial(middle_kernel, len(firsts)),
        [(meta, SMEM)] + [(a, HBM) for a in [*firsts, *seconds, before]]
        + [(first_row, VMEM), (second_row, VMEM)],
        [(u_shape, HBM), (u_shape, HBM), (jax.ShapeDtypeStruct((pairs, 8, width), f32), VMEM)]
        + [(jax.ShapeDtypeStruct(f.shape, f32), HBM) for f in firsts]
        + [(far_shape, HBM)] * PARTNERS,
        block_scratch(orb_dev, rows, width)
        + [pltpu.VMEM((PARTNERS, rows, width), bf16)] * 2
        + [pltpu.VMEM((pairs, width, width), f32)]
        + [DMA((len(firsts),)), DMA((PARTNERS,)), DMA((pairs,))]
        + [pltpu.VMEM((PARTNERS, rows, width), f32)]
        + [pltpu.VMEM((PARTNERS, width, min(128, width)), f32)]
        + [pltpu.VMEM((PARTNERS, width, rows), bf16)] * 2
        + [pltpu.VMEM((pairs, width, width), bf16)] * 2
        + [DMA((pairs,)), DMA((pairs,)), DMA((PARTNERS,))]
        + [pltpu.VMEM((len(firsts),) + firsts[0].shape, f32), DMA((len(firsts), orb_dev))],
        18 * 16 * width * width * rows, 24 * 1024 * 1024, name,
    )
    cut = 3 + len(firsts)
    return outs[0], outs[1], outs[2], outs[3:cut], outs[cut:]


def density_call(meta, firsts, seconds, u, name):
    orb_dev, _, width = firsts[0].shape
    rows = sum(f.shape[1] for f in firsts)
    pairs = meta.shape[1]
    outs = kernel_call(
        functools.partial(density_kernel, len(firsts)),
        [(meta, SMEM)] + [(a, HBM) for a in [*firsts, *seconds, *u]],
        [(jax.ShapeDtypeStruct(f.shape, f32), HBM) for f in firsts]
        + [(jax.ShapeDtypeStruct((rows, width), f32), HBM)] * PARTNERS,
        block_scratch(orb_dev, rows, width)
        + [pltpu.VMEM((PARTNERS, rows, width), bf16)] * 2
        + [DMA((len(firsts),)), DMA((PARTNERS,))]
        + [pltpu.VMEM((PARTNERS, rows, width), f32)]
        + [pltpu.VMEM((pairs, width, width), bf16)] * 2
        + [DMA((pairs,)), DMA((pairs,)), DMA((PARTNERS,))]
        + [pltpu.VMEM((len(firsts),) + firsts[0].shape, f32), DMA((len(firsts), orb_dev))],
        12 * 16 * width * width * rows, 24 * 1024 * 1024, name,
    )
    return outs[: len(firsts)], outs[len(firsts) :]


def sum_kernel(parts, chosen, *refs):
    own, refs = refs[:parts], refs[parts:]
    rows = own[0].shape[1]
    arrived, refs = refs[:PARTNERS], refs[PARTNERS:]
    buf, sem = refs[-2:]
    extra, outs = refs[: -2 - parts], refs[-2 - parts : -2]
    copies = [
        pltpu.make_async_copy(ref.at[pl.ds(0, parts * rows)], buf.at[k], sem.at[k])
        for k, ref in enumerate(arrived)
    ]
    start_all(copies)
    for q in range(parts):
        outs[q][...] = own[q][...] + extra[q][...] if extra else own[q][...]
    for k in range(PARTNERS):
        copies[k].wait()
        for q in range(parts):
            outs[q][chosen[k]] += buf[k, q * rows : (q + 1) * rows, :]


def sum_call(chosen, own, arrived, extra, name):
    parts = len(own)
    orb_dev, rows, width = own[0].shape
    shape = jax.ShapeDtypeStruct((orb_dev, rows, width), f32)
    return kernel_call(
        functools.partial(sum_kernel, parts),
        [(chosen, SMEM)]
        + [(o, VMEM) for o in own]
        + [(a, HBM) for a in arrived]
        + [(e, VMEM) for e in extra],
        [(shape, VMEM)] * parts,
        [pltpu.VMEM((PARTNERS, parts * rows, width), f32), DMA((PARTNERS,))],
        0, 12 * 1024 * 1024, name,
    )


def pick_kernel(parts, chosen, *refs):
    sources, outs = refs[:parts], refs[parts:-3]
    buf, in_sem, out_sem = refs[-3:]
    into = []
    for k in range(PARTNERS):
        at = 0
        for q, source in enumerate(sources):
            window = pl.ds(at, source.shape[1])
            into.append(
                pltpu.make_async_copy(source.at[chosen[k]], buf.at[k, window], in_sem.at[k, q])
            )
            at += source.shape[1]
    start_all(into)
    back = [pltpu.make_async_copy(buf.at[k], out, out_sem.at[k]) for k, out in enumerate(outs)]
    for k in range(PARTNERS):
        wait_all(into[k * parts : (k + 1) * parts])
        back[k].start()
    wait_all(back)


def pick_call(chosen, sources, name):
    rows = sum(a.shape[1] for a in sources)
    shape = jax.ShapeDtypeStruct((rows, sources[0].shape[2]), f32)
    return kernel_call(
        functools.partial(pick_kernel, len(sources)),
        [(chosen, SMEM)] + [(a, HBM) for a in sources],
        [(shape, HBM)] * PARTNERS,
        [
            pltpu.VMEM((PARTNERS,) + shape.shape, f32),
            DMA((PARTNERS, len(sources))), DMA((PARTNERS,)),
        ],
        0, 4 * 1024 * 1024, name,
    )


def look_up(table, index):
    lanes = 128
    high = (index // lanes).reshape(-1, 1) == jnp.arange(table.size // lanes, dtype=jnp.int32)
    low = (index % lanes).reshape(-1, 1) == jnp.arange(lanes, dtype=jnp.int32)
    rows = jnp.dot(
        high.astype(f32), table.reshape(-1, lanes), precision=lax.Precision.HIGHEST
    )
    return jnp.sum(jnp.where(low, rows, 0.0), axis=1).reshape(index.shape)


def shards(orb_size, blocks, occ_energy, vir_table, domain, pair_i, pair_j):
    orb_dev, aux_rows, width = blocks.shape
    pair_dev = pair_i.shape[0]
    p = lax.axis_index("orb")
    x = lax.axis_index("aux")
    aux_size = 4
    half = aux_rows // 2

    ring = [(s, (s + 1) % aux_size) for s in range(aux_size)]
    back = [(t, s) for s, t in ring]
    to_right = lambda a: lax.ppermute(a, "aux", ring)
    to_left = lambda a: lax.ppermute(a, "aux", back)

    def mask_of(k, at):
        low = LOW_BITS[k]
        return (((low >> 1) ^ at) << 3) | low

    tables = [
        [
            (o * aux_size + s, (o ^ mask_of(k, s)) * aux_size + s)
            for o in range(orb_size)
            for s in range(aux_size)
        ]
        for k in range(PARTNERS)
    ]

    def exchange(payloads, lanes=3):
        out = []
        for k, payload in enumerate(payloads):
            if k >= lanes:
                payload, _ = lax.optimization_barrier((payload, out[k - lanes]))
            out.append(lax.ppermute(payload, ("orb", "aux"), tables[k]))
        return out

    rows_a, rows_b = blocks[:, :half], blocks[:, half:]
    left_a = to_right(rows_a)
    right_b = to_left(rows_b)

    first_local = pair_i - p * orb_dev
    holder = pair_j // orb_dev
    second_local = pair_j % orb_dev
    device_ids = jnp.arange(orb_size, dtype=jnp.int32)
    held_by = holder[:, None] == device_ids[None, :]
    wanted = jnp.max(jnp.where(held_by, second_local[:, None], -1), axis=0)
    requested = lax.all_to_all(wanted, "orb", split_axis=0, concat_axis=0, tiled=True)
    low_bits = jnp.array(LOW_BITS, dtype=jnp.int32)
    partners = p ^ ((((low_bits >> 1) ^ x) << 3) | low_bits)
    virtual = look_up(vir_table, domain)
    shifted = virtual - occ_energy[:, None]
    requested = lax.optimization_barrier((requested, shifted))[0]
    chosen = jnp.clip(requested[partners], 0, orb_dev - 1)

    apart = holder ^ p
    mine = ((apart >> 3) ^ ((apart >> 1) & 3)) == x
    slot = sum(jnp.where((apart & 7) == low, k, 0) for k, low in enumerate(LOW_BITS))
    order = jnp.arange(pair_dev, dtype=jnp.int32)
    key = jnp.where(mine, first_local, orb_dev) * pair_dev + order
    place = jnp.sum((key[None, :] < key[:, None]).astype(jnp.int32), axis=1)
    at_place = place[None, :] == order[:, None]
    pick = lambda v: jnp.sum(jnp.where(at_place, v[None, :], 0), axis=1)
    count = jnp.sum(mine.astype(jnp.int32))
    present = jnp.any((first_local[None, :] == order[:, None]) & mine[None, :], axis=1)
    meta = jnp.stack(
        [
            pick(first_local), pick(slot), jnp.broadcast_to(count, (pair_dev,)),
            present.astype(jnp.int32),
        ]
    )

    def after(value, *earlier):
        return lax.optimization_barrier((value, earlier))[0]

    near = exchange(pick_call(chosen, [blocks], "pick_near"))
    integrals = integral_call(meta, [blocks], near, None, "integrals_near")

    set_a = after((left_a, right_b), near[2:5])
    opposite = (to_right(set_a[0]), to_left(set_a[1]))
    set_a = after(set_a, near)
    energies = jnp.broadcast_to(shifted[:, None, :], (orb_dev, 8, width))
    got_a = exchange(pick_call(chosen, [*set_a, energies], "pick_a"))
    integrals_near = integrals
    integrals = integral_call(meta, set_a, got_a, integrals, "integrals_a")
    integrals_a = integrals
    second_row = jnp.stack([a[2 * half] for a in got_a])

    opposite = after(opposite, got_a, integrals_near)
    set_c = after((rows_b, rows_a), opposite)
    set_c = (to_right(set_c[0]), to_left(set_c[1]))
    got_o = exchange(pick_call(chosen, opposite, "pick_o"))
    integrals = integral_call(meta, opposite, got_o, integrals, "integrals_o")

    set_c = after(set_c, got_o, integrals_a)
    got_c = exchange(pick_call(chosen, set_c, "pick_c"), lanes=PARTNERS)
    u_high, u_low, energy, own_c, far_c = middle_call(
        meta, set_c, got_c, integrals, shifted, second_row, "amplitudes"
    )

    back_c = exchange(far_c, lanes=PARTNERS)
    pair_energy = jnp.sum(energy, axis=(1, 2)) / width
    pair_energy = jnp.where(order < count, pair_energy, 0.0)
    spread = jnp.sum(jnp.where(at_place.T, pair_energy[None, :], 0.0), axis=1)
    for step in (1, 2):
        spread = spread + lax.ppermute(
            spread, "aux", [(s, s ^ step) for s in range(aux_size)]
        )
    own_o, far_o = density_call(
        meta, opposite, got_o, (after(u_high, back_c[2]), u_low), "density_o"
    )
    back_c, far_o = after((back_c, far_o), spread)
    sum_left_b, sum_right_a = sum_call(chosen, own_c, back_c, [], "sum_c")
    home_b = to_left(sum_left_b)
    home_a = to_right(sum_right_a)

    back_o = exchange(far_o)
    own_a, far_a = density_call(
        meta, set_a, got_a, (after(u_high, back_o[4]), u_low), "density_a"
    )
    sum_o_a, sum_o_b = sum_call(chosen, own_o, back_o, [], "sum_o")
    sum_o_a, sum_o_b, far_a = after((sum_o_a, sum_o_b, far_a), home_a, home_b)
    carried_a = to_left(sum_o_a)
    carried_b = to_right(sum_o_b)

    back_a = exchange(far_a)
    own_near, far_near = density_call(
        meta, [blocks], near, (after(u_high, back_a[4]), u_low), "density_near"
    )
    carried_a, carried_b, far_near = after((carried_a, carried_b, far_near), back_a)
    sum_left_a, sum_right_b = sum_call(chosen, own_a, back_a, [carried_a, carried_b], "sum_a")
    last_a = to_left(sum_left_a)
    last_b = to_right(sum_right_b)

    back_near = exchange(far_near)
    home = jnp.concatenate([home_a, home_b], axis=1)
    (sum_near,) = sum_call(chosen, own_near, back_near, [home], "sum_near")
    density = sum_near + jnp.concatenate([last_a, last_b], axis=1)
    return density, spread


def solution(mesh):
    placed = (P("orb", "aux", None), P("orb"), P(), P("orb", None), P("orb"), P("orb"))
    return jax.shard_map(
        functools.partial(shards, mesh.shape["orb"]),
        mesh=mesh,
        in_specs=placed,
        out_specs=(P("orb", "aux", None), P("orb")),
        check_vma=False,
    )
```

```python
import functools

import jax
import jax.numpy as jnp
from jax import lax
from jax.experimental import pallas as pl
from jax.experimental.pallas import tpu as pltpu
from jax.sharding import PartitionSpec as P

PARTNERS = 8
LOW_BITS = (2, 6, 4, 1, 3, 7, 5, 0)
VMEM_BYTES = 56 * 1024 * 1024
f32 = jnp.float32
bf16 = jnp.bfloat16


def split(x):
    high = x.astype(bf16)
    return high, (x - high.astype(f32)).astype(bf16)


def dot3(a, b, dims):
    dot = functools.partial(
        lax.dot_general, dimension_numbers=(dims, ((), ())), preferred_element_type=f32
    )
    return dot(a[0], b[0]) + dot(a[0], b[1]) + dot(a[1], b[0])


TN = ((0,), (0,))
NN = ((1,), (0,))
NT = ((1,), (1,))


VMEM = pl.BlockSpec(memory_space=pltpu.VMEM)
SMEM = pl.BlockSpec(memory_space=pltpu.SMEM)
HBM = pl.BlockSpec(memory_space=pl.ANY)
DMA = pltpu.SemaphoreType.DMA


def start_all(copies):
    for copy in copies:
        copy.start()


def wait_all(copies):
    for copy in copies:
        copy.wait()


def load(parts, firsts, seconds, f_in, s_in, f_sem, s_sem):
    rows = s_in.shape[1]
    s_copies = [
        pltpu.make_async_copy(ref.at[pl.ds(0, rows)], s_in.at[k], s_sem.at[k])
        for k, ref in enumerate(seconds)
    ]
    f_copies = []
    at = 0
    for q, ref in enumerate(firsts):
        window = pl.ds(at, ref.shape[1])
        f_copies.append(pltpu.make_async_copy(ref, f_in.at[:, window], f_sem.at[q]))
        at += ref.shape[1]
    start_all(s_copies + f_copies)
    return s_copies, f_copies


def split_first(meta, step, f_in, f_high, f_low):
    i = meta[0, step]
    before = meta[0, jnp.maximum(step, 1) - 1]

    @pl.when((step == 0) | (i != before))
    def _():
        f_high[...], f_low[...] = split(f_in[i])

    return (f_high[...], f_low[...])


def integral_kernel(parts, first_call, meta, *refs):
    firsts, refs = refs[:parts], refs[parts:]
    seconds, refs = refs[:PARTNERS], refs[PARTNERS:]
    before, refs = (None, refs) if first_call else (refs[0], refs[1:])
    out, f_in, s_in, f_high, f_low, s_high, s_low, k_buf, f_sem, s_sem, k_sem, o_sem = refs
    count = meta[2, 0]
    into = lambda r: pltpu.make_async_copy(before.at[r], k_buf.at[r], k_sem.at[r])
    back = lambda r: pltpu.make_async_copy(k_buf.at[r], out.at[r], o_sem.at[r])
    s_copies, f_copies = load(parts, firsts, seconds, f_in, s_in, f_sem, s_sem)
    if not first_call:
        pl.loop(0, count)(lambda r: into(r).start())
    for k in range(PARTNERS):
        s_copies[k].wait()
        s_high[k], s_low[k] = split(s_in[k].T)
    wait_all(f_copies)

    @pl.loop(0, count)
    def _(r):
        k = meta[1, r]
        f = split_first(meta, r, f_in, f_high, f_low)
        total = dot3((s_high[k], s_low[k]), f, NN)
        if not first_call:
            into(r).wait()
            total = total + k_buf[r]
        k_buf[r] = total
        back(r).start()

    pl.loop(0, count)(lambda r: back(r).wait())


def write_absent(meta, own, own_outs, o_sem):
    for i in range(own.shape[1]):

        @pl.when(meta[3, i] == 0)
        def _():
            for q, out in enumerate(own_outs):
                pltpu.make_async_copy(own.at[q, i], out.at[i], o_sem.at[q, i]).start()


def write_complete(meta, r, own, own_outs, o_sem):
    i = meta[0, r]
    after = meta[0, jnp.minimum(r + 1, meta.shape[1] - 1)]

    @pl.when((r == meta[2, 0] - 1) | (after != i))
    def _():
        for q, out in enumerate(own_outs):
            pltpu.make_async_copy(own.at[q, i], out.at[i], o_sem.at[q, i]).start()


def wait_written(own, own_outs, o_sem):
    for i in range(own.shape[1]):
        for q, out in enumerate(own_outs):
            pltpu.make_async_copy(own.at[q, i], out.at[i], o_sem.at[q, i]).wait()


def density_terms(i, k, f, s, u, own, far):
    rows = own.shape[2]
    for q in range(own.shape[0]):
        part = slice(q * rows, (q + 1) * rows)
        own[q, i] += dot3((s[0][part], s[1][part]), u, NN)
    far[k] += dot3(f, u, NT)


def middle_kernel(parts, meta, *refs):
    firsts, refs = refs[:parts], refs[parts:]
    seconds, refs = refs[:PARTNERS], refs[PARTNERS:]
    before, first_row, second_row, u_high, u_low, energy = refs[:6]
    own_outs, refs = refs[6 : 6 + parts], refs[6 + parts :]
    far_outs, refs = refs[:PARTNERS], refs[PARTNERS:]
    (f_in, s_in, f_high, f_low, s_high, s_low, k_buf, f_sem, s_sem, k_sem, far, column,
     t_high, t_low, uh_buf, ul_buf, h_sem, l_sem, far_sem, own, o_sem) = refs
    count = meta[2, 0]
    into = lambda r: pltpu.make_async_copy(before.at[r], k_buf.at[r], k_sem.at[r])
    high = lambda r: pltpu.make_async_copy(uh_buf.at[r], u_high.at[r], h_sem.at[r])
    low = lambda r: pltpu.make_async_copy(ul_buf.at[r], u_low.at[r], l_sem.at[r])
    s_copies, f_copies = load(parts, firsts, seconds, f_in, s_in, f_sem, s_sem)
    pl.loop(0, count)(lambda r: into(r).start())
    own[...] = jnp.zeros_like(own)
    write_absent(meta, own, own_outs, o_sem)
    far[...] = jnp.zeros_like(far)
    width = far.shape[2]
    lanes = column.shape[2]
    for k in range(PARTNERS):
        column[k] = jnp.broadcast_to(second_row[k : k + 1, :], (lanes, width)).T
    for k in range(PARTNERS):
        s_copies[k].wait()
        s = s_in[k]
        s_high[k], s_low[k] = split(s)
        t_high[k], t_low[k] = split(s.T)
    wait_all(f_copies)

    @pl.loop(0, count)
    def _(r):
        i = meta[0, r]
        k = meta[1, r]
        f = split_first(meta, r, f_in, f_high, f_low)
        total = dot3((t_high[k], t_low[k]), f, NN)
        into(r).wait()
        total = total + k_buf[r]
        side = jnp.concatenate([column[k]] * (width // lanes), axis=1)
        amplitude = -total / (side + first_row[pl.ds(i, 1), :])
        tilde = 2.0 * amplitude - amplitude.T
        energy[r] = jnp.sum((total * tilde).reshape(width // 8, 8, width), axis=0)
        u = split(tilde)
        uh_buf[r], ul_buf[r] = u
        high(r).start()
        low(r).start()
        density_terms(i, k, f, (s_high[k], s_low[k]), u, own, far)
        write_complete(meta, r, own, own_outs, o_sem)

    outs = [
        pltpu.make_async_copy(far.at[k], far_outs[k], far_sem.at[k]) for k in range(PARTNERS)
    ]
    start_all(outs)

    @pl.loop(0, count)
    def _(r):
        high(r).wait()
        low(r).wait()

    wait_all(outs)
    wait_written(own, own_outs, o_sem)


def density_kernel(parts, meta, *refs):
    firsts, refs = refs[:parts], refs[parts:]
    seconds, refs = refs[:PARTNERS], refs[PARTNERS:]
    u_high, u_low = refs[:2]
    own_outs, refs = refs[2 : 2 + parts], refs[2 + parts :]
    far_outs, refs = refs[:PARTNERS], refs[PARTNERS:]
    (f_in, s_in, f_high, f_low, s_high, s_low, f_sem, s_sem, far, uh_buf, ul_buf, h_sem,
     l_sem, far_sem, own, o_sem) = refs
    count = meta[2, 0]
    high = lambda r: pltpu.make_async_copy(u_high.at[r], uh_buf.at[r], h_sem.at[r])
    low = lambda r: pltpu.make_async_copy(u_low.at[r], ul_buf.at[r], l_sem.at[r])
    s_copies, f_copies = load(parts, firsts, seconds, f_in, s_in, f_sem, s_sem)

    @pl.loop(0, count)
    def _(r):
        high(r).start()
        low(r).start()

    own[...] = jnp.zeros_like(own)
    write_absent(meta, own, own_outs, o_sem)
    far[...] = jnp.zeros_like(far)
    for k in range(PARTNERS):
        s_copies[k].wait()
        s_high[k], s_low[k] = split(s_in[k])
    wait_all(f_copies)

    @pl.loop(0, count)
    def _(r):
        k = meta[1, r]
        f = split_first(meta, r, f_in, f_high, f_low)
        high(r).wait()
        low(r).wait()
        u = (uh_buf[r], ul_buf[r])
        density_terms(meta[0, r], k, f, (s_high[k], s_low[k]), u, own, far)
        write_complete(meta, r, own, own_outs, o_sem)

    outs = [
        pltpu.make_async_copy(far.at[k], far_outs[k], far_sem.at[k]) for k in range(PARTNERS)
    ]
    start_all(outs)
    wait_all(outs)
    wait_written(own, own_outs, o_sem)


def kernel_call(kernel, ins, outs, scratch, flops, moved, name):
    return pl.pallas_call(
        kernel,
        in_specs=[spec for _, spec in ins],
        out_specs=[spec for _, spec in outs],
        scratch_shapes=scratch,
        out_shape=[s for s, _ in outs],
        compiler_params=pltpu.CompilerParams(vmem_limit_bytes=VMEM_BYTES),
        cost_estimate=pl.CostEstimate(flops=flops, bytes_accessed=moved, transcendentals=0),
        name=name,
    )(*[a for a, _ in ins])


def block_scratch(orb_dev, rows, width):
    return [
        pltpu.VMEM((orb_dev, rows, width), f32),
        pltpu.VMEM((PARTNERS, rows, width), f32),
        pltpu.VMEM((rows, width), bf16),
        pltpu.VMEM((rows, width), bf16),
    ]


def integral_call(meta, firsts, seconds, before, name):
    orb_dev, _, width = firsts[0].shape
    rows = sum(f.shape[1] for f in firsts)
    pairs = meta.shape[1]
    shape = jax.ShapeDtypeStruct((pairs, width, width), f32)
    earlier = [] if before is None else [before]
    (out,) = kernel_call(
        functools.partial(integral_kernel, len(firsts), before is None),
        [(meta, SMEM)] + [(a, HBM) for a in [*firsts, *seconds, *earlier]],
        [(shape, HBM)],
        block_scratch(orb_dev, rows, width)
        + [pltpu.VMEM((PARTNERS, width, rows), bf16)] * 2
        + [pltpu.VMEM((pairs, width, width), f32)]
        + [DMA((len(firsts),)), DMA((PARTNERS,)), DMA((pairs,)), DMA((pairs,))],
        6 * 16 * width * width * rows, 16 * 1024 * 1024, name,
    )
    return out


def middle_call(meta, firsts, seconds, before, first_row, second_row, name):
    orb_dev, _, width = firsts[0].shape
    rows = sum(f.shape[1] for f in firsts)
    pairs = meta.shape[1]
    u_shape = jax.ShapeDtypeStruct((pairs, width, width), bf16)
    far_shape = jax.ShapeDtypeStruct((rows, width), f32)
    outs = kernel_call(
        functools.partial(middle_kernel, len(firsts)),
        [(meta, SMEM)] + [(a, HBM) for a in [*firsts, *seconds, before]]
        + [(first_row, VMEM), (second_row, VMEM)],
        [(u_shape, HBM), (u_shape, HBM), (jax.ShapeDtypeStruct((pairs, 8, width), f32), VMEM)]
        + [(jax.ShapeDtypeStruct(f.shape, f32), HBM) for f in firsts]
        + [(far_shape, HBM)] * PARTNERS,
        block_scratch(orb_dev, rows, width)
        + [pltpu.VMEM((PARTNERS, rows, width), bf16)] * 2
        + [pltpu.VMEM((pairs, width, width), f32)]
        + [DMA((len(firsts),)), DMA((PARTNERS,)), DMA((pairs,))]
        + [pltpu.VMEM((PARTNERS, rows, width), f32)]
        + [pltpu.VMEM((PARTNERS, width, min(128, width)), f32)]
        + [pltpu.VMEM((PARTNERS, width, rows), bf16)] * 2
        + [pltpu.VMEM((pairs, width, width), bf16)] * 2
        + [DMA((pairs,)), DMA((pairs,)), DMA((PARTNERS,))]
        + [pltpu.VMEM((len(firsts),) + firsts[0].shape, f32), DMA((len(firsts), orb_dev))],
        18 * 16 * width * width * rows, 24 * 1024 * 1024, name,
    )
    cut = 3 + len(firsts)
    return outs[0], outs[1], outs[2], outs[3:cut], outs[cut:]


def density_call(meta, firsts, seconds, u, name):
    orb_dev, _, width = firsts[0].shape
    rows = sum(f.shape[1] for f in firsts)
    pairs = meta.shape[1]
    outs = kernel_call(
        functools.partial(density_kernel, len(firsts)),
        [(meta, SMEM)] + [(a, HBM) for a in [*firsts, *seconds, *u]],
        [(jax.ShapeDtypeStruct(f.shape, f32), HBM) for f in firsts]
        + [(jax.ShapeDtypeStruct((rows, width), f32), HBM)] * PARTNERS,
        block_scratch(orb_dev, rows, width)
        + [pltpu.VMEM((PARTNERS, rows, width), bf16)] * 2
        + [DMA((len(firsts),)), DMA((PARTNERS,))]
        + [pltpu.VMEM((PARTNERS, rows, width), f32)]
        + [pltpu.VMEM((pairs, width, width), bf16)] * 2
        + [DMA((pairs,)), DMA((pairs,)), DMA((PARTNERS,))]
        + [pltpu.VMEM((len(firsts),) + firsts[0].shape, f32), DMA((len(firsts), orb_dev))],
        12 * 16 * width * width * rows, 24 * 1024 * 1024, name,
    )
    return outs[: len(firsts)], outs[len(firsts) :]


def sum_kernel(parts, chosen, *refs):
    own, refs = refs[:parts], refs[parts:]
    rows = own[0].shape[1]
    arrived, refs = refs[:PARTNERS], refs[PARTNERS:]
    buf, sem = refs[-2:]
    extra, outs = refs[: -2 - parts], refs[-2 - parts : -2]
    copies = [
        pltpu.make_async_copy(ref.at[pl.ds(0, parts * rows)], buf.at[k], sem.at[k])
        for k, ref in enumerate(arrived)
    ]
    start_all(copies)
    for q in range(parts):
        outs[q][...] = own[q][...] + extra[q][...] if extra else own[q][...]
    for k in range(PARTNERS):
        copies[k].wait()
        for q in range(parts):
            outs[q][chosen[k]] += buf[k, q * rows : (q + 1) * rows, :]


def sum_call(chosen, own, arrived, extra, name):
    parts = len(own)
    orb_dev, rows, width = own[0].shape
    shape = jax.ShapeDtypeStruct((orb_dev, rows, width), f32)
    return kernel_call(
        functools.partial(sum_kernel, parts),
        [(chosen, SMEM)]
        + [(o, VMEM) for o in own]
        + [(a, HBM) for a in arrived]
        + [(e, VMEM) for e in extra],
        [(shape, VMEM)] * parts,
        [pltpu.VMEM((PARTNERS, parts * rows, width), f32), DMA((PARTNERS,))],
        0, 12 * 1024 * 1024, name,
    )


def pick_kernel(parts, chosen, *refs):
    sources, outs = refs[:parts], refs[parts:-3]
    buf, in_sem, out_sem = refs[-3:]
    into = []
    for k in range(PARTNERS):
        at = 0
        for q, source in enumerate(sources):
            window = pl.ds(at, source.shape[1])
            into.append(
                pltpu.make_async_copy(source.at[chosen[k]], buf.at[k, window], in_sem.at[k, q])
            )
            at += source.shape[1]
    start_all(into)
    back = [pltpu.make_async_copy(buf.at[k], out, out_sem.at[k]) for k, out in enumerate(outs)]
    for k in range(PARTNERS):
        wait_all(into[k * parts : (k + 1) * parts])
        back[k].start()
    wait_all(back)


def pick_call(chosen, sources, name):
    rows = sum(a.shape[1] for a in sources)
    shape = jax.ShapeDtypeStruct((rows, sources[0].shape[2]), f32)
    return kernel_call(
        functools.partial(pick_kernel, len(sources)),
        [(chosen, SMEM)] + [(a, HBM) for a in sources],
        [(shape, HBM)] * PARTNERS,
        [
            pltpu.VMEM((PARTNERS,) + shape.shape, f32),
            DMA((PARTNERS, len(sources))), DMA((PARTNERS,)),
        ],
        0, 4 * 1024 * 1024, name,
    )


def look_up(table, index):
    lanes = 128
    high = (index // lanes).reshape(-1, 1) == jnp.arange(table.size // lanes, dtype=jnp.int32)
    low = (index % lanes).reshape(-1, 1) == jnp.arange(lanes, dtype=jnp.int32)
    rows = jnp.dot(
        high.astype(f32), table.reshape(-1, lanes), precision=lax.Precision.HIGHEST
    )
    return jnp.sum(jnp.where(low, rows, 0.0), axis=1).reshape(index.shape)


def shards(orb_size, blocks, occ_energy, vir_table, domain, pair_i, pair_j):
    orb_dev, aux_rows, width = blocks.shape
    pair_dev = pair_i.shape[0]
    p = lax.axis_index("orb")
    x = lax.axis_index("aux")
    aux_size = 4
    half = aux_rows // 2

    ring = [(s, (s + 1) % aux_size) for s in range(aux_size)]
    back = [(t, s) for s, t in ring]
    to_right = lambda a: lax.ppermute(a, "aux", ring)
    to_left = lambda a: lax.ppermute(a, "aux", back)

    def mask_of(k, at):
        low = LOW_BITS[k]
        return (((low >> 1) ^ at) << 3) | low

    tables = [
        [
            (o * aux_size + s, (o ^ mask_of(k, s)) * aux_size + s)
            for o in range(orb_size)
            for s in range(aux_size)
        ]
        for k in range(PARTNERS)
    ]

    def exchange(payloads, lanes=3):
        out = []
        for k, payload in enumerate(payloads):
            if k >= lanes:
                payload, _ = lax.optimization_barrier((payload, out[k - lanes]))
            out.append(lax.ppermute(payload, ("orb", "aux"), tables[k]))
        return out

    rows_a, rows_b = blocks[:, :half], blocks[:, half:]
    left_a = to_right(rows_a)
    right_b = to_left(rows_b)

    first_local = pair_i - p * orb_dev
    holder = pair_j // orb_dev
    second_local = pair_j % orb_dev
    device_ids = jnp.arange(orb_size, dtype=jnp.int32)
    held_by = holder[:, None] == device_ids[None, :]
    wanted = jnp.max(jnp.where(held_by, second_local[:, None], -1), axis=0)
    requested = lax.all_to_all(wanted, "orb", split_axis=0, concat_axis=0, tiled=True)
    low_bits = jnp.array(LOW_BITS, dtype=jnp.int32)
    partners = p ^ ((((low_bits >> 1) ^ x) << 3) | low_bits)
    virtual = look_up(vir_table, domain)
    shifted = virtual - occ_energy[:, None]
    requested = lax.optimization_barrier((requested, shifted))[0]
    chosen = jnp.clip(requested[partners], 0, orb_dev - 1)

    apart = holder ^ p
    mine = ((apart >> 3) ^ ((apart >> 1) & 3)) == x
    slot = sum(jnp.where((apart & 7) == low, k, 0) for k, low in enumerate(LOW_BITS))
    order = jnp.arange(pair_dev, dtype=jnp.int32)
    key = jnp.where(mine, first_local, orb_dev) * pair_dev + order
    place = jnp.sum((key[None, :] < key[:, None]).astype(jnp.int32), axis=1)
    at_place = place[None, :] == order[:, None]
    pick = lambda v: jnp.sum(jnp.where(at_place, v[None, :], 0), axis=1)
    count = jnp.sum(mine.astype(jnp.int32))
    present = jnp.any((first_local[None, :] == order[:, None]) & mine[None, :], axis=1)
    meta = jnp.stack(
        [
            pick(first_local), pick(slot), jnp.broadcast_to(count, (pair_dev,)),
            present.astype(jnp.int32),
        ]
    )

    def after(value, *earlier):
        return lax.optimization_barrier((value, earlier))[0]

    near = exchange(pick_call(chosen, [blocks], "pick_near"))
    integrals = integral_call(meta, [blocks], near, None, "integrals_near")

    set_c = after((rows_b, rows_a), left_a, right_b, near[2:5])
    set_c = (to_right(set_c[0]), to_left(set_c[1]))
    set_a = after((left_a, right_b), near)
    energies = jnp.broadcast_to(shifted[:, None, :], (orb_dev, 8, width))
    got_a = exchange(pick_call(chosen, [*set_a, energies], "pick_a"))
    second_row = jnp.stack([a[2 * half] for a in got_a])

    set_o = after((left_a, right_b), set_c, got_a[2:5])
    set_o = (to_right(set_o[0]), to_left(set_o[1]))
    set_c = after(set_c, got_a, integrals)
    got_c = exchange(pick_call(chosen, set_c, "pick_c"))
    integrals_a = integral_call(meta, set_a, got_a, integrals, "integrals_a")

    set_o = after(set_o, got_c, integrals_a)
    got_o = exchange(pick_call(chosen, set_o, "pick_o"), lanes=PARTNERS)
    integrals_c = integral_call(meta, set_c, got_c, integrals_a, "integrals_c")
    u_high, u_low, energy, own_o, far_o = middle_call(
        meta, set_o, got_o, integrals_c, shifted, second_row, "amplitudes"
    )

    back_o = exchange(far_o, lanes=PARTNERS)
    pair_energy = jnp.sum(energy, axis=(1, 2)) / width
    pair_energy = jnp.where(order < count, pair_energy, 0.0)
    spread = jnp.sum(jnp.where(at_place.T, pair_energy[None, :], 0.0), axis=1)
    late = after(spread, back_o[3])
    spread = spread + sum(
        lax.ppermute(late, "aux", [(s, (s + step) % aux_size) for s in range(aux_size)])
        for step in range(1, aux_size)
    )
    own_c, far_c = density_call(
        meta, set_c, got_c, (after(u_high, back_o[2]), u_low), "density_c"
    )
    back_o, far_c = after((back_o, far_c), spread)
    sum_o_a, sum_o_b = sum_call(chosen, own_o, back_o, [], "sum_o")
    carried_a = to_left(sum_o_a)
    carried_b = to_right(sum_o_b)

    back_c = exchange(far_c)
    own_a, far_a = density_call(
        meta, set_a, got_a, (after(u_high, back_c[4]), u_low), "density_a"
    )
    sum_left_b, sum_right_a = sum_call(chosen, own_c, back_c, [], "sum_c")
    sum_left_b, sum_right_a, far_a = after((sum_left_b, sum_right_a, far_a), carried_a, carried_b)
    home_b = to_left(sum_left_b)
    home_a = to_right(sum_right_a)

    back_a = exchange(far_a)
    own_near, far_near = density_call(
        meta, [blocks], near, (after(u_high, back_a[4]), u_low), "density_near"
    )
    sum_left_a, sum_right_b = sum_call(chosen, own_a, back_a, [carried_a, carried_b], "sum_a")
    sum_left_a, sum_right_b, far_near = after(
        (sum_left_a, sum_right_b, far_near), home_a, home_b
    )
    last_a = to_left(sum_left_a)
    last_b = to_right(sum_right_b)

    back_near = exchange(far_near)
    home = jnp.concatenate([home_a, home_b], axis=1)
    (sum_near,) = sum_call(chosen, own_near, back_near, [home], "sum_near")
    density = sum_near + jnp.concatenate([last_a, last_b], axis=1)
    return density, spread


def solution(mesh):
    placed = (P("orb", "aux", None), P("orb"), P(), P("orb", None), P("orb"), P("orb"))
    return jax.shard_map(
        functools.partial(shards, mesh.shape["orb"]),
        mesh=mesh,
        in_specs=placed,
        out_specs=(P("orb", "aux", None), P("orb")),
        check_vma=False,
    )
```

```python
import functools

import jax
import jax.numpy as jnp
from jax import lax
from jax.experimental import pallas as pl
from jax.experimental.pallas import tpu as pltpu
from jax.sharding import PartitionSpec as P

PARTNERS = 8
LOW_BITS = (2, 6, 4, 1, 3, 7, 5, 0)
VMEM_BYTES = 56 * 1024 * 1024
f32 = jnp.float32
bf16 = jnp.bfloat16


def split(x):
    high = x.astype(bf16)
    return high, (x - high.astype(f32)).astype(bf16)


def dot3(a, b, dims):
    dot = functools.partial(
        lax.dot_general, dimension_numbers=(dims, ((), ())), preferred_element_type=f32
    )
    return dot(a[0], b[0]) + dot(a[0], b[1]) + dot(a[1], b[0])


TN = ((0,), (0,))
NN = ((1,), (0,))
NT = ((1,), (1,))


VMEM = pl.BlockSpec(memory_space=pltpu.VMEM)
SMEM = pl.BlockSpec(memory_space=pltpu.SMEM)
HBM = pl.BlockSpec(memory_space=pl.ANY)
DMA = pltpu.SemaphoreType.DMA


def start_all(copies):
    for copy in copies:
        copy.start()


def wait_all(copies):
    for copy in copies:
        copy.wait()


def load(parts, firsts, seconds, f_in, s_in, f_sem, s_sem):
    rows = s_in.shape[1]
    s_copies = [
        pltpu.make_async_copy(ref.at[pl.ds(0, rows)], s_in.at[k], s_sem.at[k])
        for k, ref in enumerate(seconds)
    ]
    f_copies = []
    at = 0
    for q, ref in enumerate(firsts):
        window = pl.ds(at, ref.shape[1])
        f_copies.append(pltpu.make_async_copy(ref, f_in.at[:, window], f_sem.at[q]))
        at += ref.shape[1]
    start_all(s_copies + f_copies)
    return s_copies, f_copies


def split_first(meta, step, f_in, f_high, f_low):
    i = meta[0, step]
    before = meta[0, jnp.maximum(step, 1) - 1]

    @pl.when((step == 0) | (i != before))
    def _():
        f_high[...], f_low[...] = split(f_in[i])

    return (f_high[...], f_low[...])


def integral_kernel(parts, first_call, meta, *refs):
    firsts, refs = refs[:parts], refs[parts:]
    seconds, refs = refs[:PARTNERS], refs[PARTNERS:]
    before, refs = (None, refs) if first_call else (refs[0], refs[1:])
    out, f_in, s_in, f_high, f_low, s_high, s_low, k_buf, f_sem, s_sem, k_sem, o_sem = refs
    count = meta[2, 0]
    into = lambda r: pltpu.make_async_copy(before.at[r], k_buf.at[r], k_sem.at[r])
    back = lambda r: pltpu.make_async_copy(k_buf.at[r], out.at[r], o_sem.at[r])
    s_copies, f_copies = load(parts, firsts, seconds, f_in, s_in, f_sem, s_sem)
    if not first_call:
        pl.loop(0, count)(lambda r: into(r).start())
    for k in range(PARTNERS):
        s_copies[k].wait()
        s_high[k], s_low[k] = split(s_in[k].T)
    wait_all(f_copies)

    @pl.loop(0, count)
    def _(r):
        k = meta[1, r]
        f = split_first(meta, r, f_in, f_high, f_low)
        total = dot3((s_high[k], s_low[k]), f, NN)
        if not first_call:
            into(r).wait()
            total = total + k_buf[r]
        k_buf[r] = total
        back(r).start()

    pl.loop(0, count)(lambda r: back(r).wait())


def write_absent(meta, own, own_outs, o_sem):
    for i in range(own.shape[1]):

        @pl.when(meta[3, i] == 0)
        def _():
            for q, out in enumerate(own_outs):
                pltpu.make_async_copy(own.at[q, i], out.at[i], o_sem.at[q, i]).start()


def write_complete(meta, r, own, own_outs, o_sem):
    i = meta[0, r]
    after = meta[0, jnp.minimum(r + 1, meta.shape[1] - 1)]

    @pl.when((r == meta[2, 0] - 1) | (after != i))
    def _():
        for q, out in enumerate(own_outs):
            pltpu.make_async_copy(own.at[q, i], out.at[i], o_sem.at[q, i]).start()


def wait_written(own, own_outs, o_sem):
    for i in range(own.shape[1]):
        for q, out in enumerate(own_outs):
            pltpu.make_async_copy(own.at[q, i], out.at[i], o_sem.at[q, i]).wait()


def density_terms(i, k, f, s, u, own, far):
    rows = own.shape[2]
    for q in range(own.shape[0]):
        part = slice(q * rows, (q + 1) * rows)
        own[q, i] += dot3((s[0][part], s[1][part]), u, NN)
    far[k] += dot3(f, u, NT)


def middle_kernel(parts, meta, *refs):
    firsts, refs = refs[:parts], refs[parts:]
    seconds, refs = refs[:PARTNERS], refs[PARTNERS:]
    before, first_row, second_row, u_high, u_low, energy = refs[:6]
    own_outs, refs = refs[6 : 6 + parts], refs[6 + parts :]
    far_outs, refs = refs[:PARTNERS], refs[PARTNERS:]
    (f_in, s_in, f_high, f_low, s_high, s_low, k_buf, f_sem, s_sem, k_sem, far, column,
     t_high, t_low, uh_buf, ul_buf, h_sem, l_sem, far_sem, own, o_sem) = refs
    count = meta[2, 0]
    into = lambda r: pltpu.make_async_copy(before.at[r], k_buf.at[r], k_sem.at[r])
    high = lambda r: pltpu.make_async_copy(uh_buf.at[r], u_high.at[r], h_sem.at[r])
    low = lambda r: pltpu.make_async_copy(ul_buf.at[r], u_low.at[r], l_sem.at[r])
    s_copies, f_copies = load(parts, firsts, seconds, f_in, s_in, f_sem, s_sem)
    pl.loop(0, count)(lambda r: into(r).start())
    own[...] = jnp.zeros_like(own)
    write_absent(meta, own, own_outs, o_sem)
    far[...] = jnp.zeros_like(far)
    width = far.shape[2]
    lanes = column.shape[2]
    for k in range(PARTNERS):
        column[k] = jnp.broadcast_to(second_row[k : k + 1, :], (lanes, width)).T
    for k in range(PARTNERS):
        s_copies[k].wait()
        s = s_in[k]
        s_high[k], s_low[k] = split(s)
        t_high[k], t_low[k] = split(s.T)
    wait_all(f_copies)

    @pl.loop(0, count)
    def _(r):
        i = meta[0, r]
        k = meta[1, r]
        f = split_first(meta, r, f_in, f_high, f_low)
        total = dot3((t_high[k], t_low[k]), f, NN)
        into(r).wait()
        total = total + k_buf[r]
        side = jnp.concatenate([column[k]] * (width // lanes), axis=1)
        amplitude = -total / (side + first_row[pl.ds(i, 1), :])
        tilde = 2.0 * amplitude - amplitude.T
        energy[r] = jnp.sum((total * tilde).reshape(width // 8, 8, width), axis=0)
        u = split(tilde)
        uh_buf[r], ul_buf[r] = u
        high(r).start()
        low(r).start()
        density_terms(i, k, f, (s_high[k], s_low[k]), u, own, far)
        write_complete(meta, r, own, own_outs, o_sem)

    outs = [
        pltpu.make_async_copy(far.at[k], far_outs[k], far_sem.at[k]) for k in range(PARTNERS)
    ]
    start_all(outs)

    @pl.loop(0, count)
    def _(r):
        high(r).wait()
        low(r).wait()

    wait_all(outs)
    wait_written(own, own_outs, o_sem)


def density_kernel(parts, meta, *refs):
    firsts, refs = refs[:parts], refs[parts:]
    seconds, refs = refs[:PARTNERS], refs[PARTNERS:]
    u_high, u_low = refs[:2]
    own_outs, refs = refs[2 : 2 + parts], refs[2 + parts :]
    far_outs, refs = refs[:PARTNERS], refs[PARTNERS:]
    (f_in, s_in, f_high, f_low, s_high, s_low, f_sem, s_sem, far, uh_buf, ul_buf, h_sem,
     l_sem, far_sem, own, o_sem) = refs
    count = meta[2, 0]
    high = lambda r: pltpu.make_async_copy(u_high.at[r], uh_buf.at[r], h_sem.at[r])
    low = lambda r: pltpu.make_async_copy(u_low.at[r], ul_buf.at[r], l_sem.at[r])
    s_copies, f_copies = load(parts, firsts, seconds, f_in, s_in, f_sem, s_sem)

    @pl.loop(0, count)
    def _(r):
        high(r).start()
        low(r).start()

    own[...] = jnp.zeros_like(own)
    write_absent(meta, own, own_outs, o_sem)
    far[...] = jnp.zeros_like(far)
    for k in range(PARTNERS):
        s_copies[k].wait()
        s_high[k], s_low[k] = split(s_in[k])
    wait_all(f_copies)

    @pl.loop(0, count)
    def _(r):
        k = meta[1, r]
        f = split_first(meta, r, f_in, f_high, f_low)
        high(r).wait()
        low(r).wait()
        u = (uh_buf[r], ul_buf[r])
        density_terms(meta[0, r], k, f, (s_high[k], s_low[k]), u, own, far)
        write_complete(meta, r, own, own_outs, o_sem)

    outs = [
        pltpu.make_async_copy(far.at[k], far_outs[k], far_sem.at[k]) for k in range(PARTNERS)
    ]
    start_all(outs)
    wait_all(outs)
    wait_written(own, own_outs, o_sem)


def kernel_call(kernel, ins, outs, scratch, flops, moved, name):
    return pl.pallas_call(
        kernel,
        in_specs=[spec for _, spec in ins],
        out_specs=[spec for _, spec in outs],
        scratch_shapes=scratch,
        out_shape=[s for s, _ in outs],
        compiler_params=pltpu.CompilerParams(vmem_limit_bytes=VMEM_BYTES),
        cost_estimate=pl.CostEstimate(flops=flops, bytes_accessed=moved, transcendentals=0),
        name=name,
    )(*[a for a, _ in ins])


def block_scratch(orb_dev, rows, width):
    return [
        pltpu.VMEM((orb_dev, rows, width), f32),
        pltpu.VMEM((PARTNERS, rows, width), f32),
        pltpu.VMEM((rows, width), bf16),
        pltpu.VMEM((rows, width), bf16),
    ]


def integral_call(meta, firsts, seconds, before, name):
    orb_dev, _, width = firsts[0].shape
    rows = sum(f.shape[1] for f in firsts)
    pairs = meta.shape[1]
    shape = jax.ShapeDtypeStruct((pairs, width, width), f32)
    earlier = [] if before is None else [before]
    (out,) = kernel_call(
        functools.partial(integral_kernel, len(firsts), before is None),
        [(meta, SMEM)] + [(a, HBM) for a in [*firsts, *seconds, *earlier]],
        [(shape, HBM)],
        block_scratch(orb_dev, rows, width)
        + [pltpu.VMEM((PARTNERS, width, rows), bf16)] * 2
        + [pltpu.VMEM((pairs, width, width), f32)]
        + [DMA((len(firsts),)), DMA((PARTNERS,)), DMA((pairs,)), DMA((pairs,))],
        6 * 16 * width * width * rows, 16 * 1024 * 1024, name,
    )
    return out


def middle_call(meta, firsts, seconds, before, first_row, second_row, name):
    orb_dev, _, width = firsts[0].shape
    rows = sum(f.shape[1] for f in firsts)
    pairs = meta.shape[1]
    u_shape = jax.ShapeDtypeStruct((pairs, width, width), bf16)
    far_shape = jax.ShapeDtypeStruct((rows, width), f32)
    outs = kernel_call(
        functools.partial(middle_kernel, len(firsts)),
        [(meta, SMEM)] + [(a, HBM) for a in [*firsts, *seconds, before]]
        + [(first_row, VMEM), (second_row, VMEM)],
        [(u_shape, HBM), (u_shape, HBM), (jax.ShapeDtypeStruct((pairs, 8, width), f32), VMEM)]
        + [(jax.ShapeDtypeStruct(f.shape, f32), HBM) for f in firsts]
        + [(far_shape, HBM)] * PARTNERS,
        block_scratch(orb_dev, rows, width)
        + [pltpu.VMEM((PARTNERS, rows, width), bf16)] * 2
        + [pltpu.VMEM((pairs, width, width), f32)]
        + [DMA((len(firsts),)), DMA((PARTNERS,)), DMA((pairs,))]
        + [pltpu.VMEM((PARTNERS, rows, width), f32)]
        + [pltpu.VMEM((PARTNERS, width, min(128, width)), f32)]
        + [pltpu.VMEM((PARTNERS, width, rows), bf16)] * 2
        + [pltpu.VMEM((pairs, width, width), bf16)] * 2
        + [DMA((pairs,)), DMA((pairs,)), DMA((PARTNERS,))]
        + [pltpu.VMEM((len(firsts),) + firsts[0].shape, f32), DMA((len(firsts), orb_dev))],
        18 * 16 * width * width * rows, 24 * 1024 * 1024, name,
    )
    cut = 3 + len(firsts)
    return outs[0], outs[1], outs[2], outs[3:cut], outs[cut:]


def density_call(meta, firsts, seconds, u, name):
    orb_dev, _, width = firsts[0].shape
    rows = sum(f.shape[1] for f in firsts)
    pairs = meta.shape[1]
    outs = kernel_call(
        functools.partial(density_kernel, len(firsts)),
        [(meta, SMEM)] + [(a, HBM) for a in [*firsts, *seconds, *u]],
        [(jax.ShapeDtypeStruct(f.shape, f32), HBM) for f in firsts]
        + [(jax.ShapeDtypeStruct((rows, width), f32), HBM)] * PARTNERS,
        block_scratch(orb_dev, rows, width)
        + [pltpu.VMEM((PARTNERS, rows, width), bf16)] * 2
        + [DMA((len(firsts),)), DMA((PARTNERS,))]
        + [pltpu.VMEM((PARTNERS, rows, width), f32)]
        + [pltpu.VMEM((pairs, width, width), bf16)] * 2
        + [DMA((pairs,)), DMA((pairs,)), DMA((PARTNERS,))]
        + [pltpu.VMEM((len(firsts),) + firsts[0].shape, f32), DMA((len(firsts), orb_dev))],
        12 * 16 * width * width * rows, 24 * 1024 * 1024, name,
    )
    return outs[: len(firsts)], outs[len(firsts) :]


def sum_kernel(parts, tailed, chosen, *refs):
    own, refs = refs[:parts], refs[parts:]
    orb_dev, rows, _ = own[0].shape
    arrived, refs = refs[:PARTNERS], refs[PARTNERS:]
    buf, sem = refs[-2:]
    extra, outs = refs[: -2 - parts], refs[-2 - parts : -2]
    tails, extra = (extra[-parts:], extra[:-parts]) if tailed else ([], extra)
    copies = [
        pltpu.make_async_copy(ref.at[pl.ds(0, parts * rows)], buf.at[k], sem.at[k])
        for k, ref in enumerate(arrived)
    ]
    start_all(copies)
    held = orb_dev * rows
    for q in range(parts):
        terms = own[q][...].reshape(held, -1)
        if len(extra) == parts:
            terms = terms + extra[q][:held, :]
        outs[q][:held, :] = terms
    if len(extra) > parts:
        piece = rows // len(extra)
        for o in range(orb_dev):
            for q, ref in enumerate(extra):
                window = pl.ds(o * rows + q * piece, piece)
                outs[0][window, :] += ref[pl.ds(o * piece, piece), :]
    for q, tail in enumerate(tails):
        outs[q][held:, :] = tail[...]
    for k in range(PARTNERS):
        copies[k].wait()
        window = pl.ds(pl.multiple_of(chosen[k] * rows, rows), rows)
        for q in range(parts):
            outs[q][window, :] += buf[k, q * rows : (q + 1) * rows, :]


def sum_call(chosen, own, arrived, extra, name, tails=()):
    parts = len(own)
    orb_dev, rows, width = own[0].shape
    tail_rows = tails[0].shape[0] if tails else 0
    shape = jax.ShapeDtypeStruct((orb_dev * rows + tail_rows, width), f32)
    return kernel_call(
        functools.partial(sum_kernel, parts, bool(tails)),
        [(chosen, SMEM)]
        + [(o, VMEM) for o in own]
        + [(a, HBM) for a in arrived]
        + [(e, VMEM) for e in [*extra, *tails]],
        [(shape, VMEM)] * parts,
        [pltpu.VMEM((PARTNERS, parts * rows, width), f32), DMA((PARTNERS,))],
        0, 12 * 1024 * 1024, name,
    )


def pick_kernel(parts, chosen, *refs):
    sources, outs = refs[:parts], refs[parts:-3]
    buf, in_sem, out_sem = refs[-3:]
    into = []
    for k in range(PARTNERS):
        at = 0
        for q, source in enumerate(sources):
            window = pl.ds(at, source.shape[1])
            into.append(
                pltpu.make_async_copy(source.at[chosen[k]], buf.at[k, window], in_sem.at[k, q])
            )
            at += source.shape[1]
    start_all(into)
    back = [pltpu.make_async_copy(buf.at[k], out, out_sem.at[k]) for k, out in enumerate(outs)]
    for k in range(PARTNERS):
        wait_all(into[k * parts : (k + 1) * parts])
        back[k].start()
    wait_all(back)


def pick_call(chosen, sources, name):
    rows = sum(a.shape[1] for a in sources)
    shape = jax.ShapeDtypeStruct((rows, sources[0].shape[2]), f32)
    return kernel_call(
        functools.partial(pick_kernel, len(sources)),
        [(chosen, SMEM)] + [(a, HBM) for a in sources],
        [(shape, HBM)] * PARTNERS,
        [
            pltpu.VMEM((PARTNERS,) + shape.shape, f32),
            DMA((PARTNERS, len(sources))), DMA((PARTNERS,)),
        ],
        0, 4 * 1024 * 1024, name,
    )


def look_up(table, index):
    lanes = 128
    high = (index // lanes).reshape(-1, 1) == jnp.arange(table.size // lanes, dtype=jnp.int32)
    low = (index % lanes).reshape(-1, 1) == jnp.arange(lanes, dtype=jnp.int32)
    rows = jnp.dot(
        high.astype(f32), table.reshape(-1, lanes), precision=lax.Precision.HIGHEST
    )
    return jnp.sum(jnp.where(low, rows, 0.0), axis=1).reshape(index.shape)


def shards(orb_size, blocks, occ_energy, vir_table, domain, pair_i, pair_j):
    orb_dev, aux_rows, width = blocks.shape
    pair_dev = pair_i.shape[0]
    p = lax.axis_index("orb")
    x = lax.axis_index("aux")
    aux_size = 4
    half = aux_rows // 2

    ring = [(s, (s + 1) % aux_size) for s in range(aux_size)]
    back = [(t, s) for s, t in ring]
    to_right = lambda a: lax.ppermute(a, "aux", ring)
    to_left = lambda a: lax.ppermute(a, "aux", back)

    def mask_of(k, at):
        low = LOW_BITS[k]
        return (((low >> 1) ^ at) << 3) | low

    tables = [
        [
            (o * aux_size + s, (o ^ mask_of(k, s)) * aux_size + s)
            for o in range(orb_size)
            for s in range(aux_size)
        ]
        for k in range(PARTNERS)
    ]

    def after(value, *earlier):
        return lax.optimization_barrier((value, earlier))[0]

    def exchange(payloads, lanes=3, work=None):
        out = []
        done = None
        for k, payload in enumerate(payloads):
            if k >= lanes:
                payload = after(payload, out[k - lanes])
            if work is not None and k == min(lanes, 5) + 1:
                payload = after(payload, done)
            out.append(lax.ppermute(payload, ("orb", "aux"), tables[k]))
            if work is not None and k == 0:
                done = work(out[0])
        return out, done

    rows_a, rows_b = blocks[:, :half], blocks[:, half:]
    left_a = to_right(rows_a)
    right_b = to_left(rows_b)

    first_local = pair_i - p * orb_dev
    holder = pair_j // orb_dev
    second_local = pair_j % orb_dev
    device_ids = jnp.arange(orb_size, dtype=jnp.int32)
    held_by = holder[:, None] == device_ids[None, :]
    wanted = jnp.max(jnp.where(held_by, second_local[:, None], -1), axis=0)
    requested = lax.all_to_all(wanted, "orb", split_axis=0, concat_axis=0, tiled=True)
    low_bits = jnp.array(LOW_BITS, dtype=jnp.int32)
    partners = p ^ ((((low_bits >> 1) ^ x) << 3) | low_bits)
    virtual = look_up(vir_table, domain)
    shifted = virtual - occ_energy[:, None]
    requested = lax.optimization_barrier((requested, shifted))[0]
    chosen = jnp.clip(requested[partners], 0, orb_dev - 1)

    apart = holder ^ p
    mine = ((apart >> 3) ^ ((apart >> 1) & 3)) == x
    slot = sum(jnp.where((apart & 7) == low, k, 0) for k, low in enumerate(LOW_BITS))
    order = jnp.arange(pair_dev, dtype=jnp.int32)
    key = jnp.where(mine, first_local, orb_dev) * pair_dev + order
    place = jnp.sum((key[None, :] < key[:, None]).astype(jnp.int32), axis=1)
    at_place = place[None, :] == order[:, None]
    pick = lambda v: jnp.sum(jnp.where(at_place, v[None, :], 0), axis=1)
    count = jnp.sum(mine.astype(jnp.int32))
    present = jnp.any((first_local[None, :] == order[:, None]) & mine[None, :], axis=1)
    meta = jnp.stack(
        [
            pick(first_local), pick(slot), jnp.broadcast_to(count, (pair_dev,)),
            present.astype(jnp.int32),
        ]
    )

    near, _ = exchange(pick_call(chosen, [blocks], "pick_near"))

    set_c = after((rows_b, rows_a), left_a, right_b, near[2:5])
    set_c = (to_right(set_c[0]), to_left(set_c[1]))
    set_a = after((left_a, right_b), near)
    energies = jnp.broadcast_to(shifted[:, None, :], (orb_dev, 8, width))
    got_a, integrals = exchange(
        pick_call(chosen, [*set_a, energies], "pick_a"),
        work=lambda first: integral_call(
            after(meta, first), [blocks], near, None, "integrals_near"
        ),
    )

    set_o = after((left_a, right_b), set_c, got_a[2:5])
    set_o = (to_right(set_o[0]), to_left(set_o[1]))
    set_c = after(set_c, got_a)
    got_c, integrals = exchange(
        pick_call(chosen, set_c, "pick_c"),
        work=lambda first: integral_call(
            after(meta, first), set_a, got_a, integrals, "integrals_a"
        ),
    )
    second_row = jnp.stack([after(a, got_c[0])[2 * half] for a in got_a])

    set_o = after(set_o, got_c)
    got_o, integrals = exchange(
        pick_call(chosen, set_o, "pick_o"),
        lanes=PARTNERS,
        work=lambda first: integral_call(
            after(meta, first), set_c, got_c, integrals, "integrals_c"
        ),
    )
    u_high, u_low, energy, own_o, far_o = middle_call(
        meta, set_o, got_o, integrals, shifted, second_row, "amplitudes"
    )

    def density_work(firsts, seconds, name):
        return lambda first: density_call(
            after(meta, first), firsts, seconds, (u_high, u_low), name
        )

    back_o, (own_c, far_c) = exchange(
        far_o, lanes=PARTNERS, work=density_work(set_c, got_c, "density_c")
    )
    energy = after(energy, back_o[3])
    pair_energy = jnp.sum(energy, axis=(1, 2)) / width
    pair_energy = jnp.where(order < count, pair_energy, 0.0)
    spread = jnp.sum(jnp.where(at_place.T, pair_energy[None, :], 0.0), axis=1)
    tail = jnp.pad(spread[None, :], ((0, 7), (0, width - pair_dev)))
    held = orb_dev * half
    sum_o_a, sum_o_b = sum_call(chosen, own_o, back_o, [], "sum_o", tails=[tail, tail])
    carried_a = to_left(sum_o_a)
    carried_b = to_right(sum_o_b)

    back_c, (own_a, far_a) = exchange(far_c, work=density_work(set_a, got_a, "density_a"))
    sum_left_b, sum_right_a = sum_call(chosen, own_c, back_c, [], "sum_c")
    sum_left_b, sum_right_a, far_a = after((sum_left_b, sum_right_a, far_a), carried_a, carried_b)
    home_b = to_left(sum_left_b)
    home_a = to_right(sum_right_a)

    back_a, (own_near, far_near) = exchange(
        far_a, work=density_work([blocks], near, "density_near")
    )
    sum_left_a, sum_right_b = sum_call(
        chosen, own_a, back_a, [carried_a, carried_b], "sum_a",
        tails=[carried_a[held:], carried_b[held:]],
    )
    sum_left_a, sum_right_b, far_near = after(
        (sum_left_a, sum_right_b, far_near), home_a, home_b
    )
    last_a = to_left(sum_left_a)
    last_b = to_right(sum_right_b)

    back_near, _ = exchange(far_near)
    (sum_near,) = sum_call(chosen, own_near, back_near, [home_a, home_b], "sum_near")
    pieces = [a[:held].reshape(orb_dev, half, width) for a in (last_a, last_b)]
    density = sum_near.reshape(blocks.shape) + jnp.concatenate(pieces, axis=1)
    spread = spread + sum(a[held, :pair_dev] for a in (carried_a, carried_b, last_b))
    return density, spread


def solution(mesh):
    placed = (P("orb", "aux", None), P("orb"), P(), P("orb", None), P("orb"), P("orb"))
    return jax.shard_map(
        functools.partial(shards, mesh.shape["orb"]),
        mesh=mesh,
        in_specs=placed,
        out_specs=(P("orb", "aux", None), P("orb")),
        check_vma=False,
    )
```

```python
import functools

import jax
import jax.numpy as jnp
from jax import lax
from jax.experimental import pallas as pl
from jax.experimental.pallas import tpu as pltpu
from jax.sharding import PartitionSpec as P

PARTNERS = 8
LOW_BITS = (2, 6, 4, 1, 3, 7, 5, 0)
VMEM_BYTES = 56 * 1024 * 1024
f32 = jnp.float32
bf16 = jnp.bfloat16


def split(x):
    high = x.astype(bf16)
    return high, (x - high.astype(f32)).astype(bf16)


def dot3(a, b, dims):
    dot = functools.partial(
        lax.dot_general, dimension_numbers=(dims, ((), ())), preferred_element_type=f32
    )
    return dot(a[0], b[0]) + dot(a[0], b[1]) + dot(a[1], b[0])


TN = ((0,), (0,))
NN = ((1,), (0,))
NT = ((1,), (1,))


VMEM = pl.BlockSpec(memory_space=pltpu.VMEM)
SMEM = pl.BlockSpec(memory_space=pltpu.SMEM)
HBM = pl.BlockSpec(memory_space=pl.ANY)
DMA = pltpu.SemaphoreType.DMA


def start_all(copies):
    for copy in copies:
        copy.start()


def wait_all(copies):
    for copy in copies:
        copy.wait()


def load(parts, firsts, seconds, f_in, s_in, f_sem, s_sem):
    rows = s_in.shape[1]
    s_copies = [
        pltpu.make_async_copy(ref.at[pl.ds(0, rows)], s_in.at[k], s_sem.at[k])
        for k, ref in enumerate(seconds)
    ]
    f_copies = []
    at = 0
    for q, ref in enumerate(firsts):
        window = pl.ds(at, ref.shape[1])
        f_copies.append(pltpu.make_async_copy(ref, f_in.at[:, window], f_sem.at[q]))
        at += ref.shape[1]
    start_all(s_copies + f_copies)
    return s_copies, f_copies


def split_first(meta, step, f_in, f_high, f_low):
    i = meta[0, step]
    before = meta[0, jnp.maximum(step, 1) - 1]

    @pl.when((step == 0) | (i != before))
    def _():
        f_high[...], f_low[...] = split(f_in[i])

    return (f_high[...], f_low[...])


def integral_kernel(parts, first_call, meta, *refs):
    firsts, refs = refs[:parts], refs[parts:]
    seconds, refs = refs[:PARTNERS], refs[PARTNERS:]
    before, refs = (None, refs) if first_call else (refs[0], refs[1:])
    out, f_in, s_in, f_high, f_low, s_high, s_low, k_buf, f_sem, s_sem, k_sem, o_sem = refs
    count = meta[2, 0]
    into = lambda r: pltpu.make_async_copy(before.at[r], k_buf.at[r], k_sem.at[r])
    back = lambda r: pltpu.make_async_copy(k_buf.at[r], out.at[r], o_sem.at[r])
    s_copies, f_copies = load(parts, firsts, seconds, f_in, s_in, f_sem, s_sem)
    if not first_call:
        pl.loop(0, count)(lambda r: into(r).start())
    for k in range(PARTNERS):
        s_copies[k].wait()
        s_high[k], s_low[k] = split(s_in[k].T)
    wait_all(f_copies)

    @pl.loop(0, count)
    def _(r):
        k = meta[1, r]
        f = split_first(meta, r, f_in, f_high, f_low)
        total = dot3((s_high[k], s_low[k]), f, NN)
        if not first_call:
            into(r).wait()
            total = total + k_buf[r]
        k_buf[r] = total
        back(r).start()

    pl.loop(0, count)(lambda r: back(r).wait())


def write_absent(meta, own, own_outs, o_sem):
    for i in range(own.shape[1]):

        @pl.when(meta[3, i] == 0)
        def _():
            for q, out in enumerate(own_outs):
                pltpu.make_async_copy(own.at[q, i], out.at[i], o_sem.at[q, i]).start()


def write_complete(meta, r, own, own_outs, o_sem):
    i = meta[0, r]
    after = meta[0, jnp.minimum(r + 1, meta.shape[1] - 1)]

    @pl.when((r == meta[2, 0] - 1) | (after != i))
    def _():
        for q, out in enumerate(own_outs):
            pltpu.make_async_copy(own.at[q, i], out.at[i], o_sem.at[q, i]).start()


def wait_written(own, own_outs, o_sem):
    for i in range(own.shape[1]):
        for q, out in enumerate(own_outs):
            pltpu.make_async_copy(own.at[q, i], out.at[i], o_sem.at[q, i]).wait()


def density_terms(i, k, f, s, u, own, far):
    rows = own.shape[2]
    for q in range(own.shape[0]):
        part = slice(q * rows, (q + 1) * rows)
        own[q, i] += dot3((s[0][part], s[1][part]), u, NN)
    far[k] += dot3(f, u, NT)


def middle_kernel(parts, meta, *refs):
    firsts, refs = refs[:parts], refs[parts:]
    seconds, refs = refs[:PARTNERS], refs[PARTNERS:]
    before, first_row, second_row, u_high, u_low, energy = refs[:6]
    own_outs, refs = refs[6 : 6 + parts], refs[6 + parts :]
    far_outs, refs = refs[:PARTNERS], refs[PARTNERS:]
    (f_in, s_in, f_high, f_low, s_high, s_low, k_buf, f_sem, s_sem, k_sem, far, column,
     t_high, t_low, uh_buf, ul_buf, h_sem, l_sem, far_sem, own, o_sem) = refs
    count = meta[2, 0]
    into = lambda r: pltpu.make_async_copy(before.at[r], k_buf.at[r], k_sem.at[r])
    high = lambda r: pltpu.make_async_copy(uh_buf.at[r], u_high.at[r], h_sem.at[r])
    low = lambda r: pltpu.make_async_copy(ul_buf.at[r], u_low.at[r], l_sem.at[r])
    s_copies, f_copies = load(parts, firsts, seconds, f_in, s_in, f_sem, s_sem)
    pl.loop(0, count)(lambda r: into(r).start())
    own[...] = jnp.zeros_like(own)
    write_absent(meta, own, own_outs, o_sem)
    far[...] = jnp.zeros_like(far)
    width = far.shape[2]
    lanes = column.shape[2]
    for k in range(PARTNERS):
        column[k] = jnp.broadcast_to(second_row[k : k + 1, :], (lanes, width)).T
    for k in range(PARTNERS):
        s_copies[k].wait()
        s = s_in[k]
        s_high[k], s_low[k] = split(s)
        t_high[k], t_low[k] = split(s.T)
    wait_all(f_copies)

    @pl.loop(0, count)
    def _(r):
        i = meta[0, r]
        k = meta[1, r]
        f = split_first(meta, r, f_in, f_high, f_low)
        total = dot3((t_high[k], t_low[k]), f, NN)
        into(r).wait()
        total = total + k_buf[r]
        side = jnp.concatenate([column[k]] * (width // lanes), axis=1)
        amplitude = -total / (side + first_row[pl.ds(i, 1), :])
        tilde = 2.0 * amplitude - amplitude.T
        energy[r] = jnp.sum((total * tilde).reshape(width // 8, 8, width), axis=0)
        u = split(tilde)
        uh_buf[r], ul_buf[r] = u
        high(r).start()
        low(r).start()
        density_terms(i, k, f, (s_high[k], s_low[k]), u, own, far)
        write_complete(meta, r, own, own_outs, o_sem)

    outs = [
        pltpu.make_async_copy(far.at[k], far_outs[k], far_sem.at[k]) for k in range(PARTNERS)
    ]
    start_all(outs)

    @pl.loop(0, count)
    def _(r):
        high(r).wait()
        low(r).wait()

    wait_all(outs)
    wait_written(own, own_outs, o_sem)


def density_kernel(parts, meta, *refs):
    firsts, refs = refs[:parts], refs[parts:]
    seconds, refs = refs[:PARTNERS], refs[PARTNERS:]
    u_high, u_low = refs[:2]
    own_outs, refs = refs[2 : 2 + parts], refs[2 + parts :]
    far_outs, refs = refs[:PARTNERS], refs[PARTNERS:]
    (f_in, s_in, f_high, f_low, s_high, s_low, f_sem, s_sem, far, uh_buf, ul_buf, h_sem,
     l_sem, far_sem, own, o_sem) = refs
    count = meta[2, 0]
    high = lambda r: pltpu.make_async_copy(u_high.at[r], uh_buf.at[r], h_sem.at[r])
    low = lambda r: pltpu.make_async_copy(u_low.at[r], ul_buf.at[r], l_sem.at[r])
    s_copies, f_copies = load(parts, firsts, seconds, f_in, s_in, f_sem, s_sem)

    @pl.loop(0, count)
    def _(r):
        high(r).start()
        low(r).start()

    own[...] = jnp.zeros_like(own)
    write_absent(meta, own, own_outs, o_sem)
    far[...] = jnp.zeros_like(far)
    for k in range(PARTNERS):
        s_copies[k].wait()
        s_high[k], s_low[k] = split(s_in[k])
    wait_all(f_copies)

    @pl.loop(0, count)
    def _(r):
        k = meta[1, r]
        f = split_first(meta, r, f_in, f_high, f_low)
        high(r).wait()
        low(r).wait()
        u = (uh_buf[r], ul_buf[r])
        density_terms(meta[0, r], k, f, (s_high[k], s_low[k]), u, own, far)
        write_complete(meta, r, own, own_outs, o_sem)

    outs = [
        pltpu.make_async_copy(far.at[k], far_outs[k], far_sem.at[k]) for k in range(PARTNERS)
    ]
    start_all(outs)
    wait_all(outs)
    wait_written(own, own_outs, o_sem)


def kernel_call(kernel, ins, outs, scratch, flops, moved, name):
    return pl.pallas_call(
        kernel,
        in_specs=[spec for _, spec in ins],
        out_specs=[spec for _, spec in outs],
        scratch_shapes=scratch,
        out_shape=[s for s, _ in outs],
        compiler_params=pltpu.CompilerParams(vmem_limit_bytes=VMEM_BYTES),
        cost_estimate=pl.CostEstimate(flops=flops, bytes_accessed=moved, transcendentals=0),
        name=name,
    )(*[a for a, _ in ins])


def block_scratch(orb_dev, rows, width):
    return [
        pltpu.VMEM((orb_dev, rows, width), f32),
        pltpu.VMEM((PARTNERS, rows, width), f32),
        pltpu.VMEM((rows, width), bf16),
        pltpu.VMEM((rows, width), bf16),
    ]


def integral_call(meta, firsts, seconds, before, name):
    orb_dev, _, width = firsts[0].shape
    rows = sum(f.shape[1] for f in firsts)
    pairs = meta.shape[1]
    shape = jax.ShapeDtypeStruct((pairs, width, width), f32)
    earlier = [] if before is None else [before]
    (out,) = kernel_call(
        functools.partial(integral_kernel, len(firsts), before is None),
        [(meta, SMEM)] + [(a, HBM) for a in [*firsts, *seconds, *earlier]],
        [(shape, HBM)],
        block_scratch(orb_dev, rows, width)
        + [pltpu.VMEM((PARTNERS, width, rows), bf16)] * 2
        + [pltpu.VMEM((pairs, width, width), f32)]
        + [DMA((len(firsts),)), DMA((PARTNERS,)), DMA((pairs,)), DMA((pairs,))],
        6 * 16 * width * width * rows, 16 * 1024 * 1024, name,
    )
    return out


def middle_call(meta, firsts, seconds, before, first_row, second_row, name):
    orb_dev, _, width = firsts[0].shape
    rows = sum(f.shape[1] for f in firsts)
    pairs = meta.shape[1]
    u_shape = jax.ShapeDtypeStruct((pairs, width, width), bf16)
    far_shape = jax.ShapeDtypeStruct((rows, width), f32)
    outs = kernel_call(
        functools.partial(middle_kernel, len(firsts)),
        [(meta, SMEM)] + [(a, HBM) for a in [*firsts, *seconds, before]]
        + [(first_row, VMEM), (second_row, VMEM)],
        [(u_shape, HBM), (u_shape, HBM), (jax.ShapeDtypeStruct((pairs, 8, width), f32), VMEM)]
        + [(jax.ShapeDtypeStruct(f.shape, f32), HBM) for f in firsts]
        + [(far_shape, HBM)] * PARTNERS,
        block_scratch(orb_dev, rows, width)
        + [pltpu.VMEM((PARTNERS, rows, width), bf16)] * 2
        + [pltpu.VMEM((pairs, width, width), f32)]
        + [DMA((len(firsts),)), DMA((PARTNERS,)), DMA((pairs,))]
        + [pltpu.VMEM((PARTNERS, rows, width), f32)]
        + [pltpu.VMEM((PARTNERS, width, min(128, width)), f32)]
        + [pltpu.VMEM((PARTNERS, width, rows), bf16)] * 2
        + [pltpu.VMEM((pairs, width, width), bf16)] * 2
        + [DMA((pairs,)), DMA((pairs,)), DMA((PARTNERS,))]
        + [pltpu.VMEM((len(firsts),) + firsts[0].shape, f32), DMA((len(firsts), orb_dev))],
        18 * 16 * width * width * rows, 24 * 1024 * 1024, name,
    )
    cut = 3 + len(firsts)
    return outs[0], outs[1], outs[2], outs[3:cut], outs[cut:]


def density_call(meta, firsts, seconds, u, name):
    orb_dev, _, width = firsts[0].shape
    rows = sum(f.shape[1] for f in firsts)
    pairs = meta.shape[1]
    outs = kernel_call(
        functools.partial(density_kernel, len(firsts)),
        [(meta, SMEM)] + [(a, HBM) for a in [*firsts, *seconds, *u]],
        [(jax.ShapeDtypeStruct(f.shape, f32), HBM) for f in firsts]
        + [(jax.ShapeDtypeStruct((rows, width), f32), HBM)] * PARTNERS,
        block_scratch(orb_dev, rows, width)
        + [pltpu.VMEM((PARTNERS, rows, width), bf16)] * 2
        + [DMA((len(firsts),)), DMA((PARTNERS,))]
        + [pltpu.VMEM((PARTNERS, rows, width), f32)]
        + [pltpu.VMEM((pairs, width, width), bf16)] * 2
        + [DMA((pairs,)), DMA((pairs,)), DMA((PARTNERS,))]
        + [pltpu.VMEM((len(firsts),) + firsts[0].shape, f32), DMA((len(firsts), orb_dev))],
        12 * 16 * width * width * rows, 24 * 1024 * 1024, name,
    )
    return outs[: len(firsts)], outs[len(firsts) :]


def sum_kernel(parts, tailed, chosen, *refs):
    own, refs = refs[:parts], refs[parts:]
    orb_dev, rows, _ = own[0].shape
    arrived, refs = refs[:PARTNERS], refs[PARTNERS:]
    buf, sem = refs[-2:]
    extra, outs = refs[: -2 - parts], refs[-2 - parts : -2]
    tails, extra = (extra[-parts:], extra[:-parts]) if tailed else ([], extra)
    copies = [
        pltpu.make_async_copy(ref.at[pl.ds(0, parts * rows)], buf.at[k], sem.at[k])
        for k, ref in enumerate(arrived)
    ]
    start_all(copies)
    held = orb_dev * rows
    for q in range(parts):
        terms = own[q][...].reshape(held, -1)
        if len(extra) == parts:
            terms = terms + extra[q][:held, :]
        outs[q][:held, :] = terms
    if len(extra) > parts:
        piece = rows // len(extra)
        for o in range(orb_dev):
            for q, ref in enumerate(extra):
                window = pl.ds(o * rows + q * piece, piece)
                outs[0][window, :] += ref[pl.ds(o * piece, piece), :]
    for q, tail in enumerate(tails):
        outs[q][held:, :] = tail[...]
    for k in range(PARTNERS):
        copies[k].wait()
        window = pl.ds(pl.multiple_of(chosen[k] * rows, rows), rows)
        for q in range(parts):
            outs[q][window, :] += buf[k, q * rows : (q + 1) * rows, :]


def sum_call(chosen, own, arrived, extra, name, tails=()):
    parts = len(own)
    orb_dev, rows, width = own[0].shape
    tail_rows = tails[0].shape[0] if tails else 0
    shape = jax.ShapeDtypeStruct((orb_dev * rows + tail_rows, width), f32)
    return kernel_call(
        functools.partial(sum_kernel, parts, bool(tails)),
        [(chosen, SMEM)]
        + [(o, VMEM) for o in own]
        + [(a, HBM) for a in arrived]
        + [(e, VMEM) for e in [*extra, *tails]],
        [(shape, VMEM)] * parts,
        [pltpu.VMEM((PARTNERS, parts * rows, width), f32), DMA((PARTNERS,))],
        0, 12 * 1024 * 1024, name,
    )


def pick_kernel(parts, chosen, *refs):
    sources, outs = refs[:parts], refs[parts:-3]
    buf, in_sem, out_sem = refs[-3:]
    into = []
    for k in range(PARTNERS):
        at = 0
        for q, source in enumerate(sources):
            window = pl.ds(at, source.shape[1])
            into.append(
                pltpu.make_async_copy(source.at[chosen[k]], buf.at[k, window], in_sem.at[k, q])
            )
            at += source.shape[1]
    start_all(into)
    back = [pltpu.make_async_copy(buf.at[k], out, out_sem.at[k]) for k, out in enumerate(outs)]
    for k in range(PARTNERS):
        wait_all(into[k * parts : (k + 1) * parts])
        back[k].start()
    wait_all(back)


def pick_call(chosen, sources, name):
    rows = sum(a.shape[1] for a in sources)
    shape = jax.ShapeDtypeStruct((rows, sources[0].shape[2]), f32)
    return kernel_call(
        functools.partial(pick_kernel, len(sources)),
        [(chosen, SMEM)] + [(a, HBM) for a in sources],
        [(shape, HBM)] * PARTNERS,
        [
            pltpu.VMEM((PARTNERS,) + shape.shape, f32),
            DMA((PARTNERS, len(sources))), DMA((PARTNERS,)),
        ],
        0, 4 * 1024 * 1024, name,
    )


def look_up(table, index):
    lanes = 128
    high = (index // lanes).reshape(-1, 1) == jnp.arange(table.size // lanes, dtype=jnp.int32)
    low = (index % lanes).reshape(-1, 1) == jnp.arange(lanes, dtype=jnp.int32)
    rows = jnp.dot(
        high.astype(f32), table.reshape(-1, lanes), precision=lax.Precision.HIGHEST
    )
    return jnp.sum(jnp.where(low, rows, 0.0), axis=1).reshape(index.shape)


def shards(orb_size, blocks, occ_energy, vir_table, domain, pair_i, pair_j):
    orb_dev, aux_rows, width = blocks.shape
    pair_dev = pair_i.shape[0]
    p = lax.axis_index("orb")
    x = lax.axis_index("aux")
    aux_size = 4
    half = aux_rows // 2

    ring = [(s, (s + 1) % aux_size) for s in range(aux_size)]
    back = [(t, s) for s, t in ring]
    to_right = lambda a: lax.ppermute(a, "aux", ring)
    to_left = lambda a: lax.ppermute(a, "aux", back)

    def mask_of(k, at):
        low = LOW_BITS[k]
        return (((low >> 1) ^ at) << 3) | low

    tables = [
        [
            (o * aux_size + s, (o ^ mask_of(k, s)) * aux_size + s)
            for o in range(orb_size)
            for s in range(aux_size)
        ]
        for k in range(PARTNERS)
    ]

    def after(value, *earlier):
        return lax.optimization_barrier((value, earlier))[0]

    def exchange(payloads, lanes=3, work=None, at=None):
        out = []
        for k, payload in enumerate(payloads):
            if k >= lanes:
                payload = after(payload, out[k - lanes])
            out.append(lax.ppermute(payload, ("orb", "aux"), tables[k]))
        if work is None:
            return out, None
        return out, work(meta if at is None else after(meta, out[at]))

    rows_a, rows_b = blocks[:, :half], blocks[:, half:]
    left_a = to_right(rows_a)
    right_b = to_left(rows_b)

    first_local = pair_i - p * orb_dev
    holder = pair_j // orb_dev
    second_local = pair_j % orb_dev
    device_ids = jnp.arange(orb_size, dtype=jnp.int32)
    held_by = holder[:, None] == device_ids[None, :]
    wanted = jnp.max(jnp.where(held_by, second_local[:, None], -1), axis=0)
    requested = lax.all_to_all(wanted, "orb", split_axis=0, concat_axis=0, tiled=True)
    low_bits = jnp.array(LOW_BITS, dtype=jnp.int32)
    partners = p ^ ((((low_bits >> 1) ^ x) << 3) | low_bits)
    virtual = look_up(vir_table, domain)
    shifted = virtual - occ_energy[:, None]
    requested = lax.optimization_barrier((requested, shifted))[0]
    chosen = jnp.clip(requested[partners], 0, orb_dev - 1)

    apart = holder ^ p
    mine = ((apart >> 3) ^ ((apart >> 1) & 3)) == x
    slot = sum(jnp.where((apart & 7) == low, k, 0) for k, low in enumerate(LOW_BITS))
    order = jnp.arange(pair_dev, dtype=jnp.int32)
    key = jnp.where(mine, first_local, orb_dev) * pair_dev + order
    place = jnp.sum((key[None, :] < key[:, None]).astype(jnp.int32), axis=1)
    at_place = place[None, :] == order[:, None]
    pick = lambda v: jnp.sum(jnp.where(at_place, v[None, :], 0), axis=1)
    count = jnp.sum(mine.astype(jnp.int32))
    present = jnp.any((first_local[None, :] == order[:, None]) & mine[None, :], axis=1)
    meta = jnp.stack(
        [
            pick(first_local), pick(slot), jnp.broadcast_to(count, (pair_dev,)),
            present.astype(jnp.int32),
        ]
    )

    near, _ = exchange(pick_call(chosen, [blocks], "pick_near"))

    set_c = after((rows_b, rows_a), left_a, right_b, near)
    set_c = (to_right(set_c[0]), to_left(set_c[1]))
    set_a = after((left_a, right_b), near)
    energies = jnp.broadcast_to(shifted[:, None, :], (orb_dev, 8, width))
    got_a, integrals = exchange(
        pick_call(chosen, [*set_a, energies], "pick_a"),
        work=lambda meta: integral_call(meta, [blocks], near, None, "integrals_near"),
    )

    set_o = after((left_a, right_b), set_c, got_a, integrals)
    set_o = (to_right(set_o[0]), to_left(set_o[1]))
    set_c = after(set_c, got_a, integrals)
    got_c, integrals = exchange(
        pick_call(chosen, set_c, "pick_c"),
        work=lambda meta: integral_call(meta, set_a, got_a, integrals, "integrals_a"),
    )
    second_row = jnp.stack([after(a, got_c[0])[2 * half] for a in got_a])

    set_o = after(set_o, got_c, integrals)
    got_o, integrals = exchange(
        pick_call(chosen, set_o, "pick_o"),
        lanes=PARTNERS,
        work=lambda meta: integral_call(meta, set_c, got_c, integrals, "integrals_c"),
    )
    u_high, u_low, energy, own_o, far_o = middle_call(
        meta, set_o, got_o, integrals, shifted, second_row, "amplitudes"
    )

    def density_work(firsts, seconds, name):
        return lambda meta: density_call(meta, firsts, seconds, (u_high, u_low), name)

    back_o, (own_c, far_c) = exchange(
        far_o, lanes=PARTNERS, work=density_work(set_c, got_c, "density_c"), at=2
    )
    back_o = after(back_o, far_c)
    energy = after(energy, back_o[3])
    pair_energy = jnp.sum(energy, axis=(1, 2)) / width
    pair_energy = jnp.where(order < count, pair_energy, 0.0)
    spread = jnp.sum(jnp.where(at_place.T, pair_energy[None, :], 0.0), axis=1)
    tail = jnp.pad(spread[None, :], ((0, 7), (0, width - pair_dev)))
    held = orb_dev * half
    sum_o_a, sum_o_b = sum_call(chosen, own_o, back_o, [], "sum_o", tails=[tail, tail])
    carried_a = to_left(sum_o_a)
    carried_b = to_right(sum_o_b)

    back_c, (own_a, far_a) = exchange(far_c, work=density_work(set_a, got_a, "density_a"), at=4)
    sum_left_b, sum_right_a = sum_call(chosen, own_c, back_c, [], "sum_c")
    sum_left_b, sum_right_a, far_a = after((sum_left_b, sum_right_a, far_a), carried_a, carried_b)
    home_b = to_left(sum_left_b)
    home_a = to_right(sum_right_a)

    back_a, (own_near, far_near) = exchange(
        far_a, work=density_work([blocks], near, "density_near"), at=4
    )
    sum_left_a, sum_right_b = sum_call(
        chosen, own_a, back_a, [carried_a, carried_b], "sum_a",
        tails=[carried_a[held:], carried_b[held:]],
    )
    sum_left_a, sum_right_b, far_near = after(
        (sum_left_a, sum_right_b, far_near), home_a, home_b
    )
    last_a = to_left(sum_left_a)
    last_b = to_right(sum_right_b)

    back_near, _ = exchange(far_near)
    (sum_near,) = sum_call(chosen, own_near, back_near, [home_a, home_b], "sum_near")
    pieces = [a[:held].reshape(orb_dev, half, width) for a in (last_a, last_b)]
    density = sum_near.reshape(blocks.shape) + jnp.concatenate(pieces, axis=1)
    spread = spread + sum(a[held, :pair_dev] for a in (carried_a, carried_b, last_b))
    return density, spread


def solution(mesh):
    placed = (P("orb", "aux", None), P("orb"), P(), P("orb", None), P("orb"), P("orb"))
    return jax.shard_map(
        functools.partial(shards, mesh.shape["orb"]),
        mesh=mesh,
        in_specs=placed,
        out_specs=(P("orb", "aux", None), P("orb")),
        check_vma=False,
    )
```

```python
import functools

import jax
import jax.numpy as jnp
from jax import lax
from jax.experimental import pallas as pl
from jax.experimental.pallas import tpu as pltpu
from jax.sharding import PartitionSpec as P

PARTNERS = 8
LOW_BITS = (2, 6, 4, 1, 3, 7, 5, 0)
VMEM_BYTES = 56 * 1024 * 1024
f32 = jnp.float32
bf16 = jnp.bfloat16


def split(x):
    high = x.astype(bf16)
    return high, (x - high.astype(f32)).astype(bf16)


def dot3(a, b, dims):
    dot = functools.partial(
        lax.dot_general, dimension_numbers=(dims, ((), ())), preferred_element_type=f32
    )
    return dot(a[0], b[0]) + dot(a[0], b[1]) + dot(a[1], b[0])


TN = ((0,), (0,))
NN = ((1,), (0,))
NT = ((1,), (1,))


VMEM = pl.BlockSpec(memory_space=pltpu.VMEM)
SMEM = pl.BlockSpec(memory_space=pltpu.SMEM)
HBM = pl.BlockSpec(memory_space=pl.ANY)
DMA = pltpu.SemaphoreType.DMA


def start_all(copies):
    for copy in copies:
        copy.start()


def wait_all(copies):
    for copy in copies:
        copy.wait()


def load(parts, firsts, seconds, f_in, s_in, f_sem, s_sem):
    rows = s_in.shape[1]
    s_copies = [
        pltpu.make_async_copy(ref.at[pl.ds(0, rows)], s_in.at[k], s_sem.at[k])
        for k, ref in enumerate(seconds)
    ]
    f_copies = []
    at = 0
    for q, ref in enumerate(firsts):
        window = pl.ds(at, ref.shape[1])
        f_copies.append(pltpu.make_async_copy(ref, f_in.at[:, window], f_sem.at[q]))
        at += ref.shape[1]
    start_all(s_copies + f_copies)
    return s_copies, f_copies


def split_firsts(meta, f_in, f_high, f_low):
    for i in range(f_in.shape[0]):

        @pl.when(meta[3, i] > 0)
        def _():
            f_high[i], f_low[i] = split(f_in[i])


def by_twos(count, body):
    @pl.loop(0, (count + 1) // 2)
    def _(half):
        first = 2 * half
        second = jnp.minimum(first + 1, count - 1)
        body((first, second), first + 1 < count)


def integral_kernel(parts, first_call, meta, *refs):
    firsts, refs = refs[:parts], refs[parts:]
    seconds, refs = refs[:PARTNERS], refs[PARTNERS:]
    before, refs = (None, refs) if first_call else (refs[0], refs[1:])
    out, f_in, s_in, f_high, f_low, s_high, s_low, k_buf, f_sem, s_sem, k_sem, o_sem = refs
    count = meta[2, 0]
    into = lambda r: pltpu.make_async_copy(before.at[r], k_buf.at[r], k_sem.at[r])
    back = lambda r: pltpu.make_async_copy(k_buf.at[r], out.at[r], o_sem.at[r])
    s_copies, f_copies = load(parts, firsts, seconds, f_in, s_in, f_sem, s_sem)
    if not first_call:
        pl.loop(0, count)(lambda r: into(r).start())
    for k in range(PARTNERS):
        s_copies[k].wait()
        s_high[k], s_low[k] = split(s_in[k].T)
    wait_all(f_copies)

    split_firsts(meta, f_in, f_high, f_low)

    def pairs(steps, live):
        totals = []
        for r in steps:
            i, k = meta[0, r], meta[1, r]
            totals.append(dot3((s_high[k], s_low[k]), (f_high[i], f_low[i]), NN))

        def finish(r, total):
            if not first_call:
                into(r).wait()
                total = total + k_buf[r]
            k_buf[r] = total
            back(r).start()

        finish(steps[0], totals[0])
        pl.when(live)(lambda: finish(steps[1], totals[1]))

    by_twos(count, pairs)
    pl.loop(0, count)(lambda r: back(r).wait())


def write_absent(meta, own, own_outs, o_sem):
    for i in range(own.shape[1]):

        @pl.when(meta[3, i] == 0)
        def _():
            for q, out in enumerate(own_outs):
                pltpu.make_async_copy(own.at[q, i], out.at[i], o_sem.at[q, i]).start()


def write_complete(meta, r, own, own_outs, o_sem):
    i = meta[0, r]
    after = meta[0, jnp.minimum(r + 1, meta.shape[1] - 1)]

    @pl.when((r == meta[2, 0] - 1) | (after != i))
    def _():
        for q, out in enumerate(own_outs):
            pltpu.make_async_copy(own.at[q, i], out.at[i], o_sem.at[q, i]).start()


def wait_written(own, own_outs, o_sem):
    for i in range(own.shape[1]):
        for q, out in enumerate(own_outs):
            pltpu.make_async_copy(own.at[q, i], out.at[i], o_sem.at[q, i]).wait()


def density_terms(i, k, f, s, u, own, far):
    rows = own.shape[2]
    parts = [slice(q * rows, (q + 1) * rows) for q in range(own.shape[0])]
    to_own = [dot3((s[0][part], s[1][part]), u, NN) for part in parts]
    return to_own, dot3(f, u, NT)


def add_terms(i, k, terms, live, own, far):
    to_own, to_far = terms
    keep = (lambda t: t) if live is None else (lambda t: jnp.where(live, t, 0.0))
    for q, term in enumerate(to_own):
        own[q, i] += keep(term)
    far[k] += keep(to_far)


def middle_kernel(parts, meta, *refs):
    firsts, refs = refs[:parts], refs[parts:]
    seconds, refs = refs[:PARTNERS], refs[PARTNERS:]
    before, first_row, second_row, u_high, u_low, energy = refs[:6]
    own_outs, refs = refs[6 : 6 + parts], refs[6 + parts :]
    far_outs, refs = refs[:PARTNERS], refs[PARTNERS:]
    (f_in, s_in, f_high, f_low, s_high, s_low, k_buf, f_sem, s_sem, k_sem, far, column,
     t_high, t_low, uh_buf, ul_buf, h_sem, l_sem, far_sem, own, o_sem) = refs
    count = meta[2, 0]
    into = lambda r: pltpu.make_async_copy(before.at[r], k_buf.at[r], k_sem.at[r])
    high = lambda r: pltpu.make_async_copy(uh_buf.at[r], u_high.at[r], h_sem.at[r])
    low = lambda r: pltpu.make_async_copy(ul_buf.at[r], u_low.at[r], l_sem.at[r])
    s_copies, f_copies = load(parts, firsts, seconds, f_in, s_in, f_sem, s_sem)
    pl.loop(0, count)(lambda r: into(r).start())
    own[...] = jnp.zeros_like(own)
    write_absent(meta, own, own_outs, o_sem)
    far[...] = jnp.zeros_like(far)
    width = far.shape[2]
    lanes = column.shape[2]
    for k in range(PARTNERS):
        column[k] = jnp.broadcast_to(second_row[k : k + 1, :], (lanes, width)).T
    for k in range(PARTNERS):
        s_copies[k].wait()
        s = s_in[k]
        s_high[k], s_low[k] = split(s)
        t_high[k], t_low[k] = split(s.T)
    wait_all(f_copies)
    split_firsts(meta, f_in, f_high, f_low)

    def amplitudes(r):
        i, k = meta[0, r], meta[1, r]
        f = (f_high[i], f_low[i])
        total = dot3((t_high[k], t_low[k]), f, NN) + k_buf[r]
        side = jnp.concatenate([column[k]] * (width // lanes), axis=1)
        amplitude = -total / (side + first_row[pl.ds(i, 1), :])
        tilde = 2.0 * amplitude - amplitude.T
        part = jnp.sum((total * tilde).reshape(width // 8, 8, width), axis=0)
        u = split(tilde)
        return u, part, density_terms(i, k, f, (s_high[k], s_low[k]), u, own, far)

    def pairs(steps, live):
        into(steps[0]).wait()
        pl.when(live)(lambda: into(steps[1]).wait())
        results = [amplitudes(r) for r in steps]
        for r, (u, part, _) in zip(steps, results):
            uh_buf[r], ul_buf[r] = u
            energy[r] = part
        for r, (_, _, terms), there in zip(steps, results, (None, live)):
            add_terms(meta[0, r], meta[1, r], terms, there, own, far)

        def send(r):
            high(r).start()
            low(r).start()
            write_complete(meta, r, own, own_outs, o_sem)

        send(steps[0])
        pl.when(live)(lambda: send(steps[1]))

    by_twos(count, pairs)

    outs = [
        pltpu.make_async_copy(far.at[k], far_outs[k], far_sem.at[k]) for k in range(PARTNERS)
    ]
    start_all(outs)

    @pl.loop(0, count)
    def _(r):
        high(r).wait()
        low(r).wait()

    wait_all(outs)
    wait_written(own, own_outs, o_sem)


def density_kernel(parts, meta, *refs):
    firsts, refs = refs[:parts], refs[parts:]
    seconds, refs = refs[:PARTNERS], refs[PARTNERS:]
    u_high, u_low = refs[:2]
    own_outs, refs = refs[2 : 2 + parts], refs[2 + parts :]
    far_outs, refs = refs[:PARTNERS], refs[PARTNERS:]
    (f_in, s_in, f_high, f_low, s_high, s_low, f_sem, s_sem, far, uh_buf, ul_buf, h_sem,
     l_sem, far_sem, own, o_sem) = refs
    count = meta[2, 0]
    high = lambda r: pltpu.make_async_copy(u_high.at[r], uh_buf.at[r], h_sem.at[r])
    low = lambda r: pltpu.make_async_copy(u_low.at[r], ul_buf.at[r], l_sem.at[r])
    s_copies, f_copies = load(parts, firsts, seconds, f_in, s_in, f_sem, s_sem)

    @pl.loop(0, count)
    def _(r):
        high(r).start()
        low(r).start()

    own[...] = jnp.zeros_like(own)
    write_absent(meta, own, own_outs, o_sem)
    far[...] = jnp.zeros_like(far)
    for k in range(PARTNERS):
        s_copies[k].wait()
        s_high[k], s_low[k] = split(s_in[k])
    wait_all(f_copies)

    split_firsts(meta, f_in, f_high, f_low)

    def pairs(steps, live):
        high(steps[0]).wait()
        low(steps[0]).wait()

        @pl.when(live)
        def _():
            high(steps[1]).wait()
            low(steps[1]).wait()

        places = [(meta[0, r], meta[1, r]) for r in steps]
        terms = [
            density_terms(
                i, k, (f_high[i], f_low[i]), (s_high[k], s_low[k]), (uh_buf[r], ul_buf[r]), own, far
            )
            for r, (i, k) in zip(steps, places)
        ]
        add_terms(*places[0], terms[0], None, own, far)
        add_terms(*places[1], terms[1], live, own, far)
        write_complete(meta, steps[0], own, own_outs, o_sem)

        @pl.when(live)
        def _():
            write_complete(meta, steps[1], own, own_outs, o_sem)

    by_twos(count, pairs)

    outs = [
        pltpu.make_async_copy(far.at[k], far_outs[k], far_sem.at[k]) for k in range(PARTNERS)
    ]
    start_all(outs)
    wait_all(outs)
    wait_written(own, own_outs, o_sem)


def kernel_call(kernel, ins, outs, scratch, flops, moved, name):
    return pl.pallas_call(
        kernel,
        in_specs=[spec for _, spec in ins],
        out_specs=[spec for _, spec in outs],
        scratch_shapes=scratch,
        out_shape=[s for s, _ in outs],
        compiler_params=pltpu.CompilerParams(vmem_limit_bytes=VMEM_BYTES),
        cost_estimate=pl.CostEstimate(flops=flops, bytes_accessed=moved, transcendentals=0),
        name=name,
    )(*[a for a, _ in ins])


def block_scratch(orb_dev, rows, width):
    return [
        pltpu.VMEM((orb_dev, rows, width), f32),
        pltpu.VMEM((PARTNERS, rows, width), f32),
        pltpu.VMEM((orb_dev, rows, width), bf16),
        pltpu.VMEM((orb_dev, rows, width), bf16),
    ]


def integral_call(meta, firsts, seconds, before, name):
    orb_dev, _, width = firsts[0].shape
    rows = sum(f.shape[1] for f in firsts)
    pairs = meta.shape[1]
    shape = jax.ShapeDtypeStruct((pairs, width, width), f32)
    earlier = [] if before is None else [before]
    (out,) = kernel_call(
        functools.partial(integral_kernel, len(firsts), before is None),
        [(meta, SMEM)] + [(a, HBM) for a in [*firsts, *seconds, *earlier]],
        [(shape, HBM)],
        block_scratch(orb_dev, rows, width)
        + [pltpu.VMEM((PARTNERS, width, rows), bf16)] * 2
        + [pltpu.VMEM((pairs, width, width), f32)]
        + [DMA((len(firsts),)), DMA((PARTNERS,)), DMA((pairs,)), DMA((pairs,))],
        6 * 16 * width * width * rows, 16 * 1024 * 1024, name,
    )
    return out


def middle_call(meta, firsts, seconds, before, first_row, second_row, name):
    orb_dev, _, width = firsts[0].shape
    rows = sum(f.shape[1] for f in firsts)
    pairs = meta.shape[1]
    u_shape = jax.ShapeDtypeStruct((pairs, width, width), bf16)
    far_shape = jax.ShapeDtypeStruct((rows, width), f32)
    outs = kernel_call(
        functools.partial(middle_kernel, len(firsts)),
        [(meta, SMEM)] + [(a, HBM) for a in [*firsts, *seconds, before]]
        + [(first_row, VMEM), (second_row, VMEM)],
        [(u_shape, HBM), (u_shape, HBM), (jax.ShapeDtypeStruct((pairs, 8, width), f32), VMEM)]
        + [(jax.ShapeDtypeStruct(f.shape, f32), HBM) for f in firsts]
        + [(far_shape, HBM)] * PARTNERS,
        block_scratch(orb_dev, rows, width)
        + [pltpu.VMEM((PARTNERS, rows, width), bf16)] * 2
        + [pltpu.VMEM((pairs, width, width), f32)]
        + [DMA((len(firsts),)), DMA((PARTNERS,)), DMA((pairs,))]
        + [pltpu.VMEM((PARTNERS, rows, width), f32)]
        + [pltpu.VMEM((PARTNERS, width, min(128, width)), f32)]
        + [pltpu.VMEM((PARTNERS, width, rows), bf16)] * 2
        + [pltpu.VMEM((pairs, width, width), bf16)] * 2
        + [DMA((pairs,)), DMA((pairs,)), DMA((PARTNERS,))]
        + [pltpu.VMEM((len(firsts),) + firsts[0].shape, f32), DMA((len(firsts), orb_dev))],
        18 * 16 * width * width * rows, 24 * 1024 * 1024, name,
    )
    cut = 3 + len(firsts)
    return outs[0], outs[1], outs[2], outs[3:cut], outs[cut:]


def density_call(meta, firsts, seconds, u, name):
    orb_dev, _, width = firsts[0].shape
    rows = sum(f.shape[1] for f in firsts)
    pairs = meta.shape[1]
    outs = kernel_call(
        functools.partial(density_kernel, len(firsts)),
        [(meta, SMEM)] + [(a, HBM) for a in [*firsts, *seconds, *u]],
        [(jax.ShapeDtypeStruct(f.shape, f32), HBM) for f in firsts]
        + [(jax.ShapeDtypeStruct((rows, width), f32), HBM)] * PARTNERS,
        block_scratch(orb_dev, rows, width)
        + [pltpu.VMEM((PARTNERS, rows, width), bf16)] * 2
        + [DMA((len(firsts),)), DMA((PARTNERS,))]
        + [pltpu.VMEM((PARTNERS, rows, width), f32)]
        + [pltpu.VMEM((pairs, width, width), bf16)] * 2
        + [DMA((pairs,)), DMA((pairs,)), DMA((PARTNERS,))]
        + [pltpu.VMEM((len(firsts),) + firsts[0].shape, f32), DMA((len(firsts), orb_dev))],
        12 * 16 * width * width * rows, 24 * 1024 * 1024, name,
    )
    return outs[: len(firsts)], outs[len(firsts) :]


def sum_kernel(parts, tailed, chosen, *refs):
    own, refs = refs[:parts], refs[parts:]
    orb_dev, rows, _ = own[0].shape
    arrived, refs = refs[:PARTNERS], refs[PARTNERS:]
    buf, sem = refs[-2:]
    extra, outs = refs[: -2 - parts], refs[-2 - parts : -2]
    tails, extra = (extra[-parts:], extra[:-parts]) if tailed else ([], extra)
    copies = [
        pltpu.make_async_copy(ref.at[pl.ds(0, parts * rows)], buf.at[k], sem.at[k])
        for k, ref in enumerate(arrived)
    ]
    start_all(copies)
    held = orb_dev * rows
    for q in range(parts):
        terms = own[q][...].reshape(held, -1)
        if len(extra) == parts:
            terms = terms + extra[q][:held, :]
        outs[q][:held, :] = terms
    if len(extra) > parts:
        piece = rows // len(extra)
        for o in range(orb_dev):
            for q, ref in enumerate(extra):
                window = pl.ds(o * rows + q * piece, piece)
                outs[0][window, :] += ref[pl.ds(o * piece, piece), :]
    for q, tail in enumerate(tails):
        outs[q][held:, :] = tail[...]
    for k in range(PARTNERS):
        copies[k].wait()
        window = pl.ds(pl.multiple_of(chosen[k] * rows, rows), rows)
        for q in range(parts):
            outs[q][window, :] += buf[k, q * rows : (q + 1) * rows, :]


def sum_call(chosen, own, arrived, extra, name, tails=()):
    parts = len(own)
    orb_dev, rows, width = own[0].shape
    tail_rows = tails[0].shape[0] if tails else 0
    shape = jax.ShapeDtypeStruct((orb_dev * rows + tail_rows, width), f32)
    return kernel_call(
        functools.partial(sum_kernel, parts, bool(tails)),
        [(chosen, SMEM)]
        + [(o, VMEM) for o in own]
        + [(a, HBM) for a in arrived]
        + [(e, VMEM) for e in [*extra, *tails]],
        [(shape, VMEM)] * parts,
        [pltpu.VMEM((PARTNERS, parts * rows, width), f32), DMA((PARTNERS,))],
        0, 12 * 1024 * 1024, name,
    )


def pick_kernel(parts, chosen, *refs):
    sources, outs = refs[:parts], refs[parts:-3]
    buf, in_sem, out_sem = refs[-3:]
    into = []
    for k in range(PARTNERS):
        at = 0
        for q, source in enumerate(sources):
            window = pl.ds(at, source.shape[1])
            into.append(
                pltpu.make_async_copy(source.at[chosen[k]], buf.at[k, window], in_sem.at[k, q])
            )
            at += source.shape[1]
    start_all(into)
    back = [pltpu.make_async_copy(buf.at[k], out, out_sem.at[k]) for k, out in enumerate(outs)]
    for k in range(PARTNERS):
        wait_all(into[k * parts : (k + 1) * parts])
        back[k].start()
    wait_all(back)


def pick_call(chosen, sources, name):
    rows = sum(a.shape[1] for a in sources)
    shape = jax.ShapeDtypeStruct((rows, sources[0].shape[2]), f32)
    return kernel_call(
        functools.partial(pick_kernel, len(sources)),
        [(chosen, SMEM)] + [(a, HBM) for a in sources],
        [(shape, HBM)] * PARTNERS,
        [
            pltpu.VMEM((PARTNERS,) + shape.shape, f32),
            DMA((PARTNERS, len(sources))), DMA((PARTNERS,)),
        ],
        0, 4 * 1024 * 1024, name,
    )


def look_up(table, index):
    lanes = 128
    high = (index // lanes).reshape(-1, 1) == jnp.arange(table.size // lanes, dtype=jnp.int32)
    low = (index % lanes).reshape(-1, 1) == jnp.arange(lanes, dtype=jnp.int32)
    rows = jnp.dot(
        high.astype(f32), table.reshape(-1, lanes), precision=lax.Precision.HIGHEST
    )
    return jnp.sum(jnp.where(low, rows, 0.0), axis=1).reshape(index.shape)


def shards(orb_size, blocks, occ_energy, vir_table, domain, pair_i, pair_j):
    orb_dev, aux_rows, width = blocks.shape
    pair_dev = pair_i.shape[0]
    p = lax.axis_index("orb")
    x = lax.axis_index("aux")
    aux_size = 4
    half = aux_rows // 2

    ring = [(s, (s + 1) % aux_size) for s in range(aux_size)]
    back = [(t, s) for s, t in ring]
    to_right = lambda a: lax.ppermute(a, "aux", ring)
    to_left = lambda a: lax.ppermute(a, "aux", back)

    def mask_of(k, at):
        low = LOW_BITS[k]
        return (((low >> 1) ^ at) << 3) | low

    tables = [
        [
            (o * aux_size + s, (o ^ mask_of(k, s)) * aux_size + s)
            for o in range(orb_size)
            for s in range(aux_size)
        ]
        for k in range(PARTNERS)
    ]

    def after(value, *earlier):
        return lax.optimization_barrier((value, earlier))[0]

    def exchange(payloads, lanes=3, work=None, at=None):
        out = []
        for k, payload in enumerate(payloads):
            if k >= lanes:
                payload = after(payload, out[k - lanes])
            out.append(lax.ppermute(payload, ("orb", "aux"), tables[k]))
        if work is None:
            return out, None
        return out, work(meta if at is None else after(meta, out[at]))

    first_local = pair_i - p * orb_dev
    holder = pair_j // orb_dev
    second_local = pair_j % orb_dev
    device_ids = jnp.arange(orb_size, dtype=jnp.int32)
    held_by = holder[:, None] == device_ids[None, :]
    wanted = jnp.max(jnp.where(held_by, second_local[:, None], -1), axis=0)
    requested = lax.all_to_all(wanted, "orb", split_axis=0, concat_axis=0, tiled=True)

    early = after(blocks, wanted)
    rows_a, rows_b = early[:, :half], early[:, half:]
    left_a = to_right(rows_a)
    right_b = to_left(rows_b)

    low_bits = jnp.array(LOW_BITS, dtype=jnp.int32)
    partners = p ^ ((((low_bits >> 1) ^ x) << 3) | low_bits)
    virtual = look_up(vir_table, domain)
    shifted = virtual - occ_energy[:, None]
    requested = lax.optimization_barrier((requested, shifted))[0]
    chosen = jnp.clip(requested[partners], 0, orb_dev - 1)

    apart = holder ^ p
    mine = ((apart >> 3) ^ ((apart >> 1) & 3)) == x
    slot = sum(jnp.where((apart & 7) == low, k, 0) for k, low in enumerate(LOW_BITS))
    order = jnp.arange(pair_dev, dtype=jnp.int32)
    key = jnp.where(mine, first_local, orb_dev) * pair_dev + order
    place = jnp.sum((key[None, :] < key[:, None]).astype(jnp.int32), axis=1)
    at_place = place[None, :] == order[:, None]
    pick = lambda v: jnp.sum(jnp.where(at_place, v[None, :], 0), axis=1)
    count = jnp.sum(mine.astype(jnp.int32))
    present = jnp.any((first_local[None, :] == order[:, None]) & mine[None, :], axis=1)
    meta = jnp.stack(
        [
            pick(first_local), pick(slot), jnp.broadcast_to(count, (pair_dev,)),
            present.astype(jnp.int32),
        ]
    )

    near, _ = exchange(pick_call(chosen, [blocks], "pick_near"))

    set_c = after((rows_b, rows_a), left_a, right_b, near)
    set_c = (to_right(set_c[0]), to_left(set_c[1]))
    set_a = after((left_a, right_b), near)
    energies = jnp.broadcast_to(shifted[:, None, :], (orb_dev, 8, width))
    got_a, integrals = exchange(
        pick_call(chosen, [*set_a, energies], "pick_a"),
        work=lambda meta: integral_call(meta, [blocks], near, None, "integrals_near"),
    )

    set_o = after((left_a, right_b), set_c, got_a, integrals)
    set_o = (to_right(set_o[0]), to_left(set_o[1]))
    set_c = after(set_c, got_a, integrals)
    got_c, integrals = exchange(
        pick_call(chosen, set_c, "pick_c"),
        work=lambda meta: integral_call(meta, set_a, got_a, integrals, "integrals_a"),
    )
    second_row = jnp.stack([after(a, got_c[0])[2 * half] for a in got_a])

    set_o = after(set_o, got_c, integrals)
    got_o, integrals = exchange(
        pick_call(chosen, set_o, "pick_o"),
        lanes=PARTNERS,
        work=lambda meta: integral_call(meta, set_c, got_c, integrals, "integrals_c"),
    )
    u_high, u_low, energy, own_o, far_o = middle_call(
        meta, set_o, got_o, integrals, shifted, second_row, "amplitudes"
    )

    def density_work(firsts, seconds, name):
        return lambda meta: density_call(meta, firsts, seconds, (u_high, u_low), name)

    back_o, (own_c, far_c) = exchange(
        far_o, lanes=PARTNERS, work=density_work(set_c, got_c, "density_c"), at=2
    )
    back_o = after(back_o, far_c)
    energy = after(energy, back_o[3])
    pair_energy = jnp.sum(energy, axis=(1, 2)) / width
    pair_energy = jnp.where(order < count, pair_energy, 0.0)
    spread = jnp.sum(jnp.where(at_place.T, pair_energy[None, :], 0.0), axis=1)
    tail = jnp.pad(spread[None, :], ((0, 7), (0, width - pair_dev)))
    held = orb_dev * half
    sum_o_a, sum_o_b = sum_call(chosen, own_o, back_o, [], "sum_o", tails=[tail, tail])
    carried_a = to_left(sum_o_a)
    carried_b = to_right(sum_o_b)

    back_c, (own_a, far_a) = exchange(far_c, work=density_work(set_a, got_a, "density_a"), at=4)
    sum_left_b, sum_right_a = sum_call(chosen, own_c, back_c, [], "sum_c")
    sum_left_b, sum_right_a, far_a = after((sum_left_b, sum_right_a, far_a), carried_a, carried_b)
    home_b = to_left(sum_left_b)
    home_a = to_right(sum_right_a)

    back_a, (own_near, far_near) = exchange(
        far_a, work=density_work([blocks], near, "density_near"), at=4
    )
    sum_left_a, sum_right_b = sum_call(
        chosen, own_a, back_a, [carried_a, carried_b], "sum_a",
        tails=[carried_a[held:], carried_b[held:]],
    )
    sum_left_a, sum_right_b, far_near = after(
        (sum_left_a, sum_right_b, far_near), home_a, home_b
    )
    last_a = to_left(sum_left_a)
    last_b = to_right(sum_right_b)

    back_near, _ = exchange(far_near)
    (sum_near,) = sum_call(chosen, own_near, back_near, [home_a, home_b], "sum_near")
    pieces = [a[:held].reshape(orb_dev, half, width) for a in (last_a, last_b)]
    density = sum_near.reshape(blocks.shape) + jnp.concatenate(pieces, axis=1)
    spread = spread + sum(a[held, :pair_dev] for a in (carried_a, carried_b, last_b))
    return density, spread


def solution(mesh):
    placed = (P("orb", "aux", None), P("orb"), P(), P("orb", None), P("orb"), P("orb"))
    return jax.shard_map(
        functools.partial(shards, mesh.shape["orb"]),
        mesh=mesh,
        in_specs=placed,
        out_specs=(P("orb", "aux", None), P("orb")),
        check_vma=False,
    )
```

```python
import functools

import jax
import jax.numpy as jnp
from jax import lax
from jax.experimental import pallas as pl
from jax.experimental.pallas import tpu as pltpu
from jax.sharding import PartitionSpec as P

PARTNERS = 8
LOW_BITS = (2, 6, 4, 1, 3, 7, 5, 0)
VMEM_BYTES = 56 * 1024 * 1024
f32 = jnp.float32
bf16 = jnp.bfloat16


def split(x):
    high = x.astype(bf16)
    return high, (x - high.astype(f32)).astype(bf16)


def dot3(a, b, dims):
    dot = functools.partial(
        lax.dot_general, dimension_numbers=(dims, ((), ())), preferred_element_type=f32
    )
    return dot(a[0], b[0]) + dot(a[0], b[1]) + dot(a[1], b[0])


TN = ((0,), (0,))
NN = ((1,), (0,))
NT = ((1,), (1,))


VMEM = pl.BlockSpec(memory_space=pltpu.VMEM)
SMEM = pl.BlockSpec(memory_space=pltpu.SMEM)
HBM = pl.BlockSpec(memory_space=pl.ANY)
DMA = pltpu.SemaphoreType.DMA


def start_all(copies):
    for copy in copies:
        copy.start()


def wait_all(copies):
    for copy in copies:
        copy.wait()


def load(parts, firsts, seconds, f_in, s_in, f_sem, s_sem):
    rows = s_in.shape[1]
    s_copies = [
        pltpu.make_async_copy(ref.at[pl.ds(0, rows)], s_in.at[k], s_sem.at[k])
        for k, ref in enumerate(seconds)
    ]
    f_copies = []
    at = 0
    for q, ref in enumerate(firsts):
        window = pl.ds(at, ref.shape[1])
        f_copies.append(pltpu.make_async_copy(ref, f_in.at[:, window], f_sem.at[q]))
        at += ref.shape[1]
    start_all(s_copies + f_copies)
    return s_copies, f_copies


def split_firsts(meta, f_in, f_high, f_low):
    for i in range(f_in.shape[0]):

        @pl.when(meta[3, i] > 0)
        def _():
            f_high[i], f_low[i] = split(f_in[i])


def by_twos(count, body):
    @pl.loop(0, (count + 1) // 2)
    def _(half):
        first = 2 * half
        second = jnp.minimum(first + 1, count - 1)
        body((first, second), first + 1 < count)


def integral_kernel(parts, first_call, meta, *refs):
    firsts, refs = refs[:parts], refs[parts:]
    seconds, refs = refs[:PARTNERS], refs[PARTNERS:]
    before, refs = (None, refs) if first_call else (refs[0], refs[1:])
    out, f_in, s_in, f_high, f_low, s_high, s_low, k_buf, f_sem, s_sem, k_sem, o_sem = refs
    count = meta[2, 0]
    into = lambda r: pltpu.make_async_copy(before.at[r], k_buf.at[r], k_sem.at[r])
    back = lambda r: pltpu.make_async_copy(k_buf.at[r], out.at[r], o_sem.at[r])
    s_copies, f_copies = load(parts, firsts, seconds, f_in, s_in, f_sem, s_sem)
    if not first_call:
        pl.loop(0, count)(lambda r: into(r).start())
    for k in range(PARTNERS):
        s_copies[k].wait()
        s_high[k], s_low[k] = split(s_in[k].T)
    wait_all(f_copies)

    split_firsts(meta, f_in, f_high, f_low)

    def pairs(steps, live):
        totals = []
        for r in steps:
            i, k = meta[0, r], meta[1, r]
            totals.append(dot3((s_high[k], s_low[k]), (f_high[i], f_low[i]), NN))

        def finish(r, total):
            if not first_call:
                into(r).wait()
                total = total + k_buf[r]
            k_buf[r] = total
            back(r).start()

        finish(steps[0], totals[0])
        pl.when(live)(lambda: finish(steps[1], totals[1]))

    by_twos(count, pairs)
    pl.loop(0, count)(lambda r: back(r).wait())


def write_absent(meta, own, own_outs, o_sem):
    for i in range(own.shape[1]):

        @pl.when(meta[3, i] == 0)
        def _():
            for q, out in enumerate(own_outs):
                pltpu.make_async_copy(own.at[q, i], out.at[i], o_sem.at[q, i]).start()


def write_complete(meta, r, own, own_outs, o_sem):
    i = meta[0, r]
    after = meta[0, jnp.minimum(r + 1, meta.shape[1] - 1)]

    @pl.when((r == meta[2, 0] - 1) | (after != i))
    def _():
        for q, out in enumerate(own_outs):
            pltpu.make_async_copy(own.at[q, i], out.at[i], o_sem.at[q, i]).start()


def wait_written(own, own_outs, o_sem):
    for i in range(own.shape[1]):
        for q, out in enumerate(own_outs):
            pltpu.make_async_copy(own.at[q, i], out.at[i], o_sem.at[q, i]).wait()


def density_terms(i, k, f, s, u, own, far):
    rows = own.shape[2]
    parts = [slice(q * rows, (q + 1) * rows) for q in range(own.shape[0])]
    to_own = [dot3((s[0][part], s[1][part]), u, NN) for part in parts]
    return to_own, dot3(f, u, NT)


def add_terms(i, k, terms, live, own, far):
    to_own, to_far = terms
    keep = (lambda t: t) if live is None else (lambda t: jnp.where(live, t, 0.0))
    for q, term in enumerate(to_own):
        own[q, i] += keep(term)
    far[k] += keep(to_far)


def middle_kernel(parts, meta, *refs):
    firsts, refs = refs[:parts], refs[parts:]
    seconds, refs = refs[:PARTNERS], refs[PARTNERS:]
    before, first_row, second_row, u_high, u_low, energy = refs[:6]
    own_outs, refs = refs[6 : 6 + parts], refs[6 + parts :]
    far_outs, refs = refs[:PARTNERS], refs[PARTNERS:]
    (f_in, s_in, f_high, f_low, s_high, s_low, k_buf, f_sem, s_sem, k_sem, far, column,
     t_high, t_low, uh_buf, ul_buf, h_sem, l_sem, far_sem, own, o_sem) = refs
    count = meta[2, 0]
    into = lambda r: pltpu.make_async_copy(before.at[r], k_buf.at[r], k_sem.at[r])
    high = lambda r: pltpu.make_async_copy(uh_buf.at[r], u_high.at[r], h_sem.at[r])
    low = lambda r: pltpu.make_async_copy(ul_buf.at[r], u_low.at[r], l_sem.at[r])
    s_copies, f_copies = load(parts, firsts, seconds, f_in, s_in, f_sem, s_sem)
    pl.loop(0, count)(lambda r: into(r).start())
    own[...] = jnp.zeros_like(own)
    write_absent(meta, own, own_outs, o_sem)
    far[...] = jnp.zeros_like(far)
    width = far.shape[2]
    lanes = column.shape[2]
    for k in range(PARTNERS):
        column[k] = jnp.broadcast_to(second_row[k : k + 1, :], (lanes, width)).T
    for k in range(PARTNERS):
        s_copies[k].wait()
        s = s_in[k]
        s_high[k], s_low[k] = split(s)
        t_high[k], t_low[k] = split(s.T)
    wait_all(f_copies)
    split_firsts(meta, f_in, f_high, f_low)

    def amplitudes(r):
        i, k = meta[0, r], meta[1, r]
        f = (f_high[i], f_low[i])
        total = dot3((t_high[k], t_low[k]), f, NN) + k_buf[r]
        side = jnp.concatenate([column[k]] * (width // lanes), axis=1)
        amplitude = -total / (side + first_row[pl.ds(i, 1), :])
        tilde = 2.0 * amplitude - amplitude.T
        part = jnp.sum((total * tilde).reshape(width // 8, 8, width), axis=0)
        u = split(tilde)
        return u, part, density_terms(i, k, f, (s_high[k], s_low[k]), u, own, far)

    def pairs(steps, live):
        into(steps[0]).wait()
        pl.when(live)(lambda: into(steps[1]).wait())
        results = [amplitudes(r) for r in steps]
        for r, (u, part, _) in zip(steps, results):
            uh_buf[r], ul_buf[r] = u
            energy[r] = part
        for r, (_, _, terms), there in zip(steps, results, (None, live)):
            add_terms(meta[0, r], meta[1, r], terms, there, own, far)

        def send(r):
            high(r).start()
            low(r).start()
            write_complete(meta, r, own, own_outs, o_sem)

        send(steps[0])
        pl.when(live)(lambda: send(steps[1]))

    by_twos(count, pairs)

    outs = [
        pltpu.make_async_copy(far.at[k], far_outs[k], far_sem.at[k]) for k in range(PARTNERS)
    ]
    start_all(outs)

    @pl.loop(0, count)
    def _(r):
        high(r).wait()
        low(r).wait()

    wait_all(outs)
    wait_written(own, own_outs, o_sem)


def density_kernel(parts, meta, *refs):
    firsts, refs = refs[:parts], refs[parts:]
    seconds, refs = refs[:PARTNERS], refs[PARTNERS:]
    u_high, u_low = refs[:2]
    own_outs, refs = refs[2 : 2 + parts], refs[2 + parts :]
    far_outs, refs = refs[:PARTNERS], refs[PARTNERS:]
    (f_in, s_in, f_high, f_low, s_high, s_low, f_sem, s_sem, far, uh_buf, ul_buf, h_sem,
     l_sem, far_sem, own, o_sem) = refs
    count = meta[2, 0]
    high = lambda r: pltpu.make_async_copy(u_high.at[r], uh_buf.at[r], h_sem.at[r])
    low = lambda r: pltpu.make_async_copy(u_low.at[r], ul_buf.at[r], l_sem.at[r])
    s_copies, f_copies = load(parts, firsts, seconds, f_in, s_in, f_sem, s_sem)

    @pl.loop(0, count)
    def _(r):
        high(r).start()
        low(r).start()

    own[...] = jnp.zeros_like(own)
    write_absent(meta, own, own_outs, o_sem)
    far[...] = jnp.zeros_like(far)
    for k in range(PARTNERS):
        s_copies[k].wait()
        s_high[k], s_low[k] = split(s_in[k])
    wait_all(f_copies)

    split_firsts(meta, f_in, f_high, f_low)

    def pairs(steps, live):
        high(steps[0]).wait()
        low(steps[0]).wait()

        @pl.when(live)
        def _():
            high(steps[1]).wait()
            low(steps[1]).wait()

        places = [(meta[0, r], meta[1, r]) for r in steps]
        terms = [
            density_terms(
                i, k, (f_high[i], f_low[i]), (s_high[k], s_low[k]), (uh_buf[r], ul_buf[r]), own, far
            )
            for r, (i, k) in zip(steps, places)
        ]
        add_terms(*places[0], terms[0], None, own, far)
        add_terms(*places[1], terms[1], live, own, far)
        write_complete(meta, steps[0], own, own_outs, o_sem)

        @pl.when(live)
        def _():
            write_complete(meta, steps[1], own, own_outs, o_sem)

    by_twos(count, pairs)

    outs = [
        pltpu.make_async_copy(far.at[k], far_outs[k], far_sem.at[k]) for k in range(PARTNERS)
    ]
    start_all(outs)
    wait_all(outs)
    wait_written(own, own_outs, o_sem)


def kernel_call(kernel, ins, outs, scratch, flops, moved, name):
    return pl.pallas_call(
        kernel,
        in_specs=[spec for _, spec in ins],
        out_specs=[spec for _, spec in outs],
        scratch_shapes=scratch,
        out_shape=[s for s, _ in outs],
        compiler_params=pltpu.CompilerParams(vmem_limit_bytes=VMEM_BYTES),
        cost_estimate=pl.CostEstimate(flops=flops, bytes_accessed=moved, transcendentals=0),
        name=name,
    )(*[a for a, _ in ins])


def block_scratch(orb_dev, rows, width):
    return [
        pltpu.VMEM((orb_dev, rows, width), f32),
        pltpu.VMEM((PARTNERS, rows, width), f32),
        pltpu.VMEM((orb_dev, rows, width), bf16),
        pltpu.VMEM((orb_dev, rows, width), bf16),
    ]


def integral_call(meta, firsts, seconds, before, name):
    orb_dev, _, width = firsts[0].shape
    rows = sum(f.shape[1] for f in firsts)
    pairs = meta.shape[1]
    shape = jax.ShapeDtypeStruct((pairs, width, width), f32)
    earlier = [] if before is None else [before]
    (out,) = kernel_call(
        functools.partial(integral_kernel, len(firsts), before is None),
        [(meta, SMEM)] + [(a, HBM) for a in [*firsts, *seconds, *earlier]],
        [(shape, HBM)],
        block_scratch(orb_dev, rows, width)
        + [pltpu.VMEM((PARTNERS, width, rows), bf16)] * 2
        + [pltpu.VMEM((pairs, width, width), f32)]
        + [DMA((len(firsts),)), DMA((PARTNERS,)), DMA((pairs,)), DMA((pairs,))],
        6 * 16 * width * width * rows, 16 * 1024 * 1024, name,
    )
    return out


def middle_call(meta, firsts, seconds, before, first_row, second_row, name):
    orb_dev, _, width = firsts[0].shape
    rows = sum(f.shape[1] for f in firsts)
    pairs = meta.shape[1]
    u_shape = jax.ShapeDtypeStruct((pairs, width, width), bf16)
    far_shape = jax.ShapeDtypeStruct((rows, width), f32)
    outs = kernel_call(
        functools.partial(middle_kernel, len(firsts)),
        [(meta, SMEM)] + [(a, HBM) for a in [*firsts, *seconds, before]]
        + [(first_row, VMEM), (second_row, VMEM)],
        [(u_shape, HBM), (u_shape, HBM), (jax.ShapeDtypeStruct((pairs, 8, width), f32), VMEM)]
        + [(jax.ShapeDtypeStruct(f.shape, f32), HBM) for f in firsts]
        + [(far_shape, HBM)] * PARTNERS,
        block_scratch(orb_dev, rows, width)
        + [pltpu.VMEM((PARTNERS, rows, width), bf16)] * 2
        + [pltpu.VMEM((pairs, width, width), f32)]
        + [DMA((len(firsts),)), DMA((PARTNERS,)), DMA((pairs,))]
        + [pltpu.VMEM((PARTNERS, rows, width), f32)]
        + [pltpu.VMEM((PARTNERS, width, min(128, width)), f32)]
        + [pltpu.VMEM((PARTNERS, width, rows), bf16)] * 2
        + [pltpu.VMEM((pairs, width, width), bf16)] * 2
        + [DMA((pairs,)), DMA((pairs,)), DMA((PARTNERS,))]
        + [pltpu.VMEM((len(firsts),) + firsts[0].shape, f32), DMA((len(firsts), orb_dev))],
        18 * 16 * width * width * rows, 24 * 1024 * 1024, name,
    )
    cut = 3 + len(firsts)
    return outs[0], outs[1], outs[2], outs[3:cut], outs[cut:]


def density_call(meta, firsts, seconds, u, name):
    orb_dev, _, width = firsts[0].shape
    rows = sum(f.shape[1] for f in firsts)
    pairs = meta.shape[1]
    outs = kernel_call(
        functools.partial(density_kernel, len(firsts)),
        [(meta, SMEM)] + [(a, HBM) for a in [*firsts, *seconds, *u]],
        [(jax.ShapeDtypeStruct(f.shape, f32), HBM) for f in firsts]
        + [(jax.ShapeDtypeStruct((rows, width), f32), HBM)] * PARTNERS,
        block_scratch(orb_dev, rows, width)
        + [pltpu.VMEM((PARTNERS, rows, width), bf16)] * 2
        + [DMA((len(firsts),)), DMA((PARTNERS,))]
        + [pltpu.VMEM((PARTNERS, rows, width), f32)]
        + [pltpu.VMEM((pairs, width, width), bf16)] * 2
        + [DMA((pairs,)), DMA((pairs,)), DMA((PARTNERS,))]
        + [pltpu.VMEM((len(firsts),) + firsts[0].shape, f32), DMA((len(firsts), orb_dev))],
        12 * 16 * width * width * rows, 24 * 1024 * 1024, name,
    )
    return outs[: len(firsts)], outs[len(firsts) :]


def sum_kernel(parts, extras, tailed, chosen, *refs):
    own, refs = refs[:parts], refs[parts:]
    arrived, refs = refs[:PARTNERS], refs[PARTNERS:]
    extra, refs = refs[:extras], refs[extras:]
    tails, refs = (refs[:parts], refs[parts:]) if tailed else ([], refs)
    outs, refs = refs[:parts], refs[parts:]
    acc, buf, e_buf, own_sem, sem, e_sem, out_sem, tail_sem = refs
    orb_dev, rows = acc.shape[1], acc.shape[2]
    held = orb_dev * rows
    own_copies = [pltpu.make_async_copy(own[q], acc.at[q], own_sem.at[q]) for q in range(parts)]
    copies = [
        pltpu.make_async_copy(ref.at[pl.ds(0, parts * rows)], buf.at[k], sem.at[k])
        for k, ref in enumerate(arrived)
    ]
    e_rows = e_buf.shape[1]
    e_copies = [
        pltpu.make_async_copy(ref.at[pl.ds(0, e_rows)], e_buf.at[q], e_sem.at[q])
        for q, ref in enumerate(extra)
    ]
    tail_copies = [
        pltpu.make_async_copy(tail, outs[q].at[pl.ds(held, tail.shape[0])], tail_sem.at[q])
        for q, tail in enumerate(tails)
    ]
    start_all(copies + own_copies + e_copies + tail_copies)
    wait_all(own_copies)
    for k in range(PARTNERS):
        copies[k].wait()
        for q in range(parts):
            acc[q, chosen[k]] += buf[k, q * rows : (q + 1) * rows, :]
    wait_all(e_copies)
    piece = e_rows // orb_dev
    backs = []
    for o in range(orb_dev):
        for q in range(extras):
            term = e_buf[q, o * piece : (o + 1) * piece, :]
            if extras == parts:
                acc[q, o] += term
            else:
                acc[0, o, q * piece : (q + 1) * piece, :] += term
        for q in range(parts):
            place = outs[q].at[pl.ds(o * rows, rows)]
            backs.append(pltpu.make_async_copy(acc.at[q, o], place, out_sem.at[q, o]))
            backs[-1].start()
    wait_all(backs + tail_copies)


def sum_call(chosen, own, arrived, extra, name, tails=()):
    parts = len(own)
    orb_dev, rows, width = own[0].shape
    tail_rows = tails[0].shape[0] if tails else 0
    shape = jax.ShapeDtypeStruct((orb_dev * rows + tail_rows, width), f32)
    extras = len(extra)
    e_rows = orb_dev * rows * parts // extras if extras else 8
    return kernel_call(
        functools.partial(sum_kernel, parts, extras, bool(tails)),
        [(chosen, SMEM)]
        + [(a, HBM) for a in [*own, *arrived, *extra]]
        + [(t, VMEM) for t in tails],
        [(shape, HBM)] * parts,
        [
            pltpu.VMEM((parts, orb_dev, rows, width), f32),
            pltpu.VMEM((PARTNERS, parts * rows, width), f32),
            pltpu.VMEM((max(extras, 1), e_rows, width), f32),
            DMA((parts,)), DMA((PARTNERS,)), DMA((max(extras, 1),)), DMA((parts, orb_dev)),
            DMA((parts,)),
        ],
        0, 12 * 1024 * 1024, name,
    )


def pick_kernel(parts, chosen, *refs):
    sources, outs = refs[:parts], refs[parts:-3]
    buf, in_sem, out_sem = refs[-3:]
    into = []
    for k in range(PARTNERS):
        at = 0
        for q, source in enumerate(sources):
            window = pl.ds(at, source.shape[1])
            into.append(
                pltpu.make_async_copy(source.at[chosen[k]], buf.at[k, window], in_sem.at[k, q])
            )
            at += source.shape[1]
    start_all(into)
    back = [pltpu.make_async_copy(buf.at[k], out, out_sem.at[k]) for k, out in enumerate(outs)]
    for k in range(PARTNERS):
        wait_all(into[k * parts : (k + 1) * parts])
        back[k].start()
    wait_all(back)


def pick_call(chosen, sources, name):
    rows = sum(a.shape[1] for a in sources)
    shape = jax.ShapeDtypeStruct((rows, sources[0].shape[2]), f32)
    return kernel_call(
        functools.partial(pick_kernel, len(sources)),
        [(chosen, SMEM)] + [(a, HBM) for a in sources],
        [(shape, HBM)] * PARTNERS,
        [
            pltpu.VMEM((PARTNERS,) + shape.shape, f32),
            DMA((PARTNERS, len(sources))), DMA((PARTNERS,)),
        ],
        0, 4 * 1024 * 1024, name,
    )


def look_up(table, index):
    lanes = 128
    high = (index // lanes).reshape(-1, 1) == jnp.arange(table.size // lanes, dtype=jnp.int32)
    low = (index % lanes).reshape(-1, 1) == jnp.arange(lanes, dtype=jnp.int32)
    rows = jnp.dot(
        high.astype(f32), table.reshape(-1, lanes), precision=lax.Precision.HIGHEST
    )
    return jnp.sum(jnp.where(low, rows, 0.0), axis=1).reshape(index.shape)


def shards(orb_size, blocks, occ_energy, vir_table, domain, pair_i, pair_j):
    orb_dev, aux_rows, width = blocks.shape
    pair_dev = pair_i.shape[0]
    p = lax.axis_index("orb")
    x = lax.axis_index("aux")
    aux_size = 4
    half = aux_rows // 2

    ring = [(s, (s + 1) % aux_size) for s in range(aux_size)]
    back = [(t, s) for s, t in ring]
    to_right = lambda a: lax.ppermute(a, "aux", ring)
    to_left = lambda a: lax.ppermute(a, "aux", back)

    def mask_of(k, at):
        low = LOW_BITS[k]
        return (((low >> 1) ^ at) << 3) | low

    tables = [
        [
            (o * aux_size + s, (o ^ mask_of(k, s)) * aux_size + s)
            for o in range(orb_size)
            for s in range(aux_size)
        ]
        for k in range(PARTNERS)
    ]

    def after(value, *earlier):
        return lax.optimization_barrier((value, earlier))[0]

    def exchange(payloads, lanes=3, work=None, at=None):
        out = []
        for k, payload in enumerate(payloads):
            if k >= lanes:
                payload = after(payload, out[k - lanes])
            out.append(lax.ppermute(payload, ("orb", "aux"), tables[k]))
        if work is None:
            return out, None
        return out, work(meta if at is None else after(meta, out[at]))

    first_local = pair_i - p * orb_dev
    holder = pair_j // orb_dev
    second_local = pair_j % orb_dev
    device_ids = jnp.arange(orb_size, dtype=jnp.int32)
    held_by = holder[:, None] == device_ids[None, :]
    wanted = jnp.max(jnp.where(held_by, second_local[:, None], -1), axis=0)
    requested = lax.all_to_all(wanted, "orb", split_axis=0, concat_axis=0, tiled=True)

    rows_a, rows_b = after((blocks[:, :half], blocks[:, half:]), requested)
    left_a = to_right(rows_a)
    right_b = to_left(rows_b)

    low_bits = jnp.array(LOW_BITS, dtype=jnp.int32)
    partners = p ^ ((((low_bits >> 1) ^ x) << 3) | low_bits)
    virtual = look_up(vir_table, domain)
    shifted = virtual - occ_energy[:, None]
    requested = lax.optimization_barrier((requested, shifted))[0]
    chosen = jnp.clip(requested[partners], 0, orb_dev - 1)

    apart = holder ^ p
    mine = ((apart >> 3) ^ ((apart >> 1) & 3)) == x
    slot = sum(jnp.where((apart & 7) == low, k, 0) for k, low in enumerate(LOW_BITS))
    order = jnp.arange(pair_dev, dtype=jnp.int32)
    key = jnp.where(mine, first_local, orb_dev) * pair_dev + order
    place = jnp.sum((key[None, :] < key[:, None]).astype(jnp.int32), axis=1)
    at_place = place[None, :] == order[:, None]
    pick = lambda v: jnp.sum(jnp.where(at_place, v[None, :], 0), axis=1)
    count = jnp.sum(mine.astype(jnp.int32))
    present = jnp.any((first_local[None, :] == order[:, None]) & mine[None, :], axis=1)
    meta = jnp.stack(
        [
            pick(first_local), pick(slot), jnp.broadcast_to(count, (pair_dev,)),
            present.astype(jnp.int32),
        ]
    )

    near, _ = exchange(pick_call(chosen, [blocks], "pick_near"))

    set_c = after((rows_b, rows_a), left_a, right_b, near)
    set_c = (to_right(set_c[0]), to_left(set_c[1]))
    set_a = after((left_a, right_b), near)
    energies = jnp.broadcast_to(shifted[:, None, :], (orb_dev, 8, width))
    got_a, integrals = exchange(
        pick_call(chosen, [*set_a, energies], "pick_a"),
        work=lambda meta: integral_call(meta, [blocks], near, None, "integrals_near"),
    )

    set_o = after((left_a, right_b), set_c, got_a, integrals)
    set_o = (to_right(set_o[0]), to_left(set_o[1]))
    set_c = after(set_c, got_a, integrals)
    got_c, integrals = exchange(
        pick_call(chosen, set_c, "pick_c"),
        work=lambda meta: integral_call(meta, set_a, got_a, integrals, "integrals_a"),
    )
    second_row = jnp.stack([after(a, got_c[0])[2 * half] for a in got_a])

    set_o = after(set_o, got_c, integrals)
    got_o, integrals = exchange(
        pick_call(chosen, set_o, "pick_o"),
        lanes=PARTNERS,
        work=lambda meta: integral_call(meta, set_c, got_c, integrals, "integrals_c"),
    )
    u_high, u_low, energy, own_o, far_o = middle_call(
        meta, set_o, got_o, integrals, shifted, second_row, "amplitudes"
    )

    def density_work(firsts, seconds, name):
        return lambda meta: density_call(meta, firsts, seconds, (u_high, u_low), name)

    back_o, (own_c, far_c) = exchange(
        far_o, lanes=PARTNERS, work=density_work(set_c, got_c, "density_c"), at=2
    )
    back_o = after(back_o, far_c)
    energy = after(energy, back_o[3])
    pair_energy = jnp.sum(energy, axis=(1, 2)) / width
    pair_energy = jnp.where(order < count, pair_energy, 0.0)
    spread = jnp.sum(jnp.where(at_place.T, pair_energy[None, :], 0.0), axis=1)
    tail = jnp.pad(spread[None, :], ((0, 7), (0, width - pair_dev)))
    held = orb_dev * half
    sum_o_a, sum_o_b = sum_call(chosen, own_o, back_o, [], "sum_o", tails=[tail, tail])
    carried_a = to_left(sum_o_a)
    carried_b = to_right(sum_o_b)

    back_c, (own_a, far_a) = exchange(far_c, work=density_work(set_a, got_a, "density_a"), at=4)
    sum_left_b, sum_right_a = sum_call(chosen, own_c, back_c, [], "sum_c")
    sum_left_b, sum_right_a, far_a = after((sum_left_b, sum_right_a, far_a), carried_a, carried_b)
    home_b = to_left(sum_left_b)
    home_a = to_right(sum_right_a)

    back_a, (own_near, far_near) = exchange(
        far_a, work=density_work([blocks], near, "density_near"), at=4
    )
    sum_left_a, sum_right_b = sum_call(
        chosen, own_a, back_a, [carried_a, carried_b], "sum_a",
        tails=[carried_a[held:], carried_b[held:]],
    )
    sum_left_a, sum_right_b, far_near = after(
        (sum_left_a, sum_right_b, far_near), home_a, home_b
    )
    last_a = to_left(sum_left_a)
    last_b = to_right(sum_right_b)

    back_near, _ = exchange(far_near)
    (sum_near,) = sum_call(chosen, own_near, back_near, [home_a, home_b], "sum_near")
    pieces = [a[:held].reshape(orb_dev, half, width) for a in (last_a, last_b)]
    density = sum_near.reshape(blocks.shape) + jnp.concatenate(pieces, axis=1)
    spread = spread + sum(a[held, :pair_dev] for a in (carried_a, carried_b, last_b))
    return density, spread


def solution(mesh):
    placed = (P("orb", "aux", None), P("orb"), P(), P("orb", None), P("orb"), P("orb"))
    return jax.shard_map(
        functools.partial(shards, mesh.shape["orb"]),
        mesh=mesh,
        in_specs=placed,
        out_specs=(P("orb", "aux", None), P("orb")),
        check_vma=False,
    )
```

```python
import functools

import jax
import jax.numpy as jnp
from jax import lax
from jax.experimental import pallas as pl
from jax.experimental.pallas import tpu as pltpu
from jax.sharding import PartitionSpec as P

PARTNERS = 8
LOW_BITS = (2, 6, 4, 1, 3, 7, 5, 0)
VMEM_BYTES = 56 * 1024 * 1024
f32 = jnp.float32
bf16 = jnp.bfloat16


def split(x):
    high = x.astype(bf16)
    return high, (x - high.astype(f32)).astype(bf16)


def dot3(a, b, dims):
    dot = functools.partial(
        lax.dot_general, dimension_numbers=(dims, ((), ())), preferred_element_type=f32
    )
    return dot(a[0], b[0]) + dot(a[0], b[1]) + dot(a[1], b[0])


TN = ((0,), (0,))
NN = ((1,), (0,))
NT = ((1,), (1,))


VMEM = pl.BlockSpec(memory_space=pltpu.VMEM)
SMEM = pl.BlockSpec(memory_space=pltpu.SMEM)
HBM = pl.BlockSpec(memory_space=pl.ANY)
DMA = pltpu.SemaphoreType.DMA


def start_all(copies):
    for copy in copies:
        copy.start()


def wait_all(copies):
    for copy in copies:
        copy.wait()


def load(parts, firsts, seconds, f_in, s_in, f_sem, s_sem):
    rows = s_in.shape[1]
    s_copies = [
        pltpu.make_async_copy(ref.at[pl.ds(0, rows)], s_in.at[k], s_sem.at[k])
        for k, ref in enumerate(seconds)
    ]
    f_copies = []
    at = 0
    for q, ref in enumerate(firsts):
        window = pl.ds(at, ref.shape[1])
        f_copies.append(pltpu.make_async_copy(ref, f_in.at[:, window], f_sem.at[q]))
        at += ref.shape[1]
    start_all(s_copies + f_copies)
    return s_copies, f_copies


def split_firsts(meta, f_in, f_high, f_low):
    for i in range(f_in.shape[0]):

        @pl.when(meta[3, i] > 0)
        def _():
            f_high[i], f_low[i] = split(f_in[i])


def by_twos(count, body):
    @pl.loop(0, (count + 1) // 2)
    def _(half):
        first = 2 * half
        second = jnp.minimum(first + 1, count - 1)
        body((first, second), first + 1 < count)


def integral_kernel(parts, first_call, meta, *refs):
    firsts, refs = refs[:parts], refs[parts:]
    seconds, refs = refs[:PARTNERS], refs[PARTNERS:]
    before, refs = (None, refs) if first_call else (refs[0], refs[1:])
    out, f_in, s_in, f_high, f_low, s_high, s_low, k_buf, f_sem, s_sem, k_sem, o_sem = refs
    count = meta[2, 0]
    into = lambda r: pltpu.make_async_copy(before.at[r], k_buf.at[r], k_sem.at[r])
    back = lambda r: pltpu.make_async_copy(k_buf.at[r], out.at[r], o_sem.at[r])
    s_copies, f_copies = load(parts, firsts, seconds, f_in, s_in, f_sem, s_sem)
    if not first_call:
        pl.loop(0, count)(lambda r: into(r).start())
    for k in range(PARTNERS):
        s_copies[k].wait()
        s_high[k], s_low[k] = split(s_in[k].T)
    wait_all(f_copies)

    split_firsts(meta, f_in, f_high, f_low)

    def pairs(steps, live):
        totals = []
        for r in steps:
            i, k = meta[0, r], meta[1, r]
            totals.append(dot3((s_high[k], s_low[k]), (f_high[i], f_low[i]), NN))

        def finish(r, total):
            if not first_call:
                into(r).wait()
                total = total + k_buf[r]
            k_buf[r] = total
            back(r).start()

        finish(steps[0], totals[0])
        pl.when(live)(lambda: finish(steps[1], totals[1]))

    by_twos(count, pairs)
    pl.loop(0, count)(lambda r: back(r).wait())


def write_absent(meta, own, own_outs, o_sem):
    for i in range(own.shape[1]):

        @pl.when(meta[3, i] == 0)
        def _():
            for q, out in enumerate(own_outs):
                pltpu.make_async_copy(own.at[q, i], out.at[i], o_sem.at[q, i]).start()


def write_complete(meta, r, own, own_outs, o_sem):
    i = meta[0, r]
    after = meta[0, jnp.minimum(r + 1, meta.shape[1] - 1)]

    @pl.when((r == meta[2, 0] - 1) | (after != i))
    def _():
        for q, out in enumerate(own_outs):
            pltpu.make_async_copy(own.at[q, i], out.at[i], o_sem.at[q, i]).start()


def wait_written(own, own_outs, o_sem):
    for i in range(own.shape[1]):
        for q, out in enumerate(own_outs):
            pltpu.make_async_copy(own.at[q, i], out.at[i], o_sem.at[q, i]).wait()


def density_terms(i, k, f, s, u, own, far):
    rows = own.shape[2]
    parts = [slice(q * rows, (q + 1) * rows) for q in range(own.shape[0])]
    to_own = [dot3((s[0][part], s[1][part]), u, NN) for part in parts]
    return to_own, dot3(f, u, NT)


def add_terms(i, k, terms, live, own, far):
    to_own, to_far = terms
    keep = (lambda t: t) if live is None else (lambda t: jnp.where(live, t, 0.0))
    for q, term in enumerate(to_own):
        own[q, i] += keep(term)
    far[k] += keep(to_far)


def middle_kernel(parts, meta, *refs):
    firsts, refs = refs[:parts], refs[parts:]
    seconds, refs = refs[:PARTNERS], refs[PARTNERS:]
    before, first_row, second_row, u_high, u_low, energy = refs[:6]
    own_outs, refs = refs[6 : 6 + parts], refs[6 + parts :]
    far_outs, refs = refs[:PARTNERS], refs[PARTNERS:]
    (f_in, s_in, f_high, f_low, s_high, s_low, k_buf, f_sem, s_sem, k_sem, far, column,
     t_high, t_low, uh_buf, ul_buf, h_sem, l_sem, far_sem, own, o_sem) = refs
    count = meta[2, 0]
    into = lambda r: pltpu.make_async_copy(before.at[r], k_buf.at[r], k_sem.at[r])
    high = lambda r: pltpu.make_async_copy(uh_buf.at[r], u_high.at[r], h_sem.at[r])
    low = lambda r: pltpu.make_async_copy(ul_buf.at[r], u_low.at[r], l_sem.at[r])
    s_copies, f_copies = load(parts, firsts, seconds, f_in, s_in, f_sem, s_sem)
    pl.loop(0, count)(lambda r: into(r).start())
    own[...] = jnp.zeros_like(own)
    write_absent(meta, own, own_outs, o_sem)
    far[...] = jnp.zeros_like(far)
    width = far.shape[2]
    lanes = column.shape[2]
    for k in range(PARTNERS):
        column[k] = jnp.broadcast_to(second_row[k : k + 1, :], (lanes, width)).T
    for k in range(PARTNERS):
        s_copies[k].wait()
        s = s_in[k]
        s_high[k], s_low[k] = split(s)
        t_high[k], t_low[k] = split(s.T)
    wait_all(f_copies)
    split_firsts(meta, f_in, f_high, f_low)

    def amplitudes(r):
        i, k = meta[0, r], meta[1, r]
        f = (f_high[i], f_low[i])
        total = dot3((t_high[k], t_low[k]), f, NN) + k_buf[r]
        side = jnp.concatenate([column[k]] * (width // lanes), axis=1)
        amplitude = -total / (side + first_row[pl.ds(i, 1), :])
        tilde = 2.0 * amplitude - amplitude.T
        part = jnp.sum((total * tilde).reshape(width // 8, 8, width), axis=0)
        u = split(tilde)
        return u, part, density_terms(i, k, f, (s_high[k], s_low[k]), u, own, far)

    def pairs(steps, live):
        into(steps[0]).wait()
        pl.when(live)(lambda: into(steps[1]).wait())
        results = [amplitudes(r) for r in steps]
        for r, (u, part, _) in zip(steps, results):
            uh_buf[r], ul_buf[r] = u
            energy[r] = part
        for r, (_, _, terms), there in zip(steps, results, (None, live)):
            add_terms(meta[0, r], meta[1, r], terms, there, own, far)

        def send(r):
            high(r).start()
            low(r).start()
            write_complete(meta, r, own, own_outs, o_sem)

        send(steps[0])
        pl.when(live)(lambda: send(steps[1]))

    by_twos(count, pairs)

    outs = [
        pltpu.make_async_copy(far.at[k], far_outs[k], far_sem.at[k]) for k in range(PARTNERS)
    ]
    start_all(outs)

    @pl.loop(0, count)
    def _(r):
        high(r).wait()
        low(r).wait()

    wait_all(outs)
    wait_written(own, own_outs, o_sem)


def density_kernel(parts, meta, *refs):
    firsts, refs = refs[:parts], refs[parts:]
    seconds, refs = refs[:PARTNERS], refs[PARTNERS:]
    u_high, u_low = refs[:2]
    own_outs, refs = refs[2 : 2 + parts], refs[2 + parts :]
    far_outs, refs = refs[:PARTNERS], refs[PARTNERS:]
    (f_in, s_in, f_high, f_low, s_high, s_low, f_sem, s_sem, far, uh_buf, ul_buf, h_sem,
     l_sem, far_sem, own, o_sem) = refs
    count = meta[2, 0]
    high = lambda r: pltpu.make_async_copy(u_high.at[r], uh_buf.at[r], h_sem.at[r])
    low = lambda r: pltpu.make_async_copy(u_low.at[r], ul_buf.at[r], l_sem.at[r])
    s_copies, f_copies = load(parts, firsts, seconds, f_in, s_in, f_sem, s_sem)

    @pl.loop(0, count)
    def _(r):
        high(r).start()
        low(r).start()

    own[...] = jnp.zeros_like(own)
    write_absent(meta, own, own_outs, o_sem)
    far[...] = jnp.zeros_like(far)
    for k in range(PARTNERS):
        s_copies[k].wait()
        s_high[k], s_low[k] = split(s_in[k])
    wait_all(f_copies)

    split_firsts(meta, f_in, f_high, f_low)

    def pairs(steps, live):
        high(steps[0]).wait()
        low(steps[0]).wait()

        @pl.when(live)
        def _():
            high(steps[1]).wait()
            low(steps[1]).wait()

        places = [(meta[0, r], meta[1, r]) for r in steps]
        terms = [
            density_terms(
                i, k, (f_high[i], f_low[i]), (s_high[k], s_low[k]), (uh_buf[r], ul_buf[r]), own, far
            )
            for r, (i, k) in zip(steps, places)
        ]
        add_terms(*places[0], terms[0], None, own, far)
        add_terms(*places[1], terms[1], live, own, far)
        write_complete(meta, steps[0], own, own_outs, o_sem)

        @pl.when(live)
        def _():
            write_complete(meta, steps[1], own, own_outs, o_sem)

    by_twos(count, pairs)

    outs = [
        pltpu.make_async_copy(far.at[k], far_outs[k], far_sem.at[k]) for k in range(PARTNERS)
    ]
    start_all(outs)
    wait_all(outs)
    wait_written(own, own_outs, o_sem)


def kernel_call(kernel, ins, outs, scratch, flops, moved, name):
    return pl.pallas_call(
        kernel,
        in_specs=[spec for _, spec in ins],
        out_specs=[spec for _, spec in outs],
        scratch_shapes=scratch,
        out_shape=[s for s, _ in outs],
        compiler_params=pltpu.CompilerParams(vmem_limit_bytes=VMEM_BYTES),
        cost_estimate=pl.CostEstimate(flops=flops, bytes_accessed=moved, transcendentals=0),
        name=name,
    )(*[a for a, _ in ins])


def block_scratch(orb_dev, rows, width):
    return [
        pltpu.VMEM((orb_dev, rows, width), f32),
        pltpu.VMEM((PARTNERS, rows, width), f32),
        pltpu.VMEM((orb_dev, rows, width), bf16),
        pltpu.VMEM((orb_dev, rows, width), bf16),
    ]


def integral_call(meta, firsts, seconds, before, name):
    orb_dev, _, width = firsts[0].shape
    rows = sum(f.shape[1] for f in firsts)
    pairs = meta.shape[1]
    shape = jax.ShapeDtypeStruct((pairs, width, width), f32)
    earlier = [] if before is None else [before]
    (out,) = kernel_call(
        functools.partial(integral_kernel, len(firsts), before is None),
        [(meta, SMEM)] + [(a, HBM) for a in [*firsts, *seconds, *earlier]],
        [(shape, HBM)],
        block_scratch(orb_dev, rows, width)
        + [pltpu.VMEM((PARTNERS, width, rows), bf16)] * 2
        + [pltpu.VMEM((pairs, width, width), f32)]
        + [DMA((len(firsts),)), DMA((PARTNERS,)), DMA((pairs,)), DMA((pairs,))],
        6 * 16 * width * width * rows, 16 * 1024 * 1024, name,
    )
    return out


def middle_call(meta, firsts, seconds, before, first_row, second_row, name):
    orb_dev, _, width = firsts[0].shape
    rows = sum(f.shape[1] for f in firsts)
    pairs = meta.shape[1]
    u_shape = jax.ShapeDtypeStruct((pairs, width, width), bf16)
    far_shape = jax.ShapeDtypeStruct((rows, width), f32)
    outs = kernel_call(
        functools.partial(middle_kernel, len(firsts)),
        [(meta, SMEM)] + [(a, HBM) for a in [*firsts, *seconds, before]]
        + [(first_row, VMEM), (second_row, VMEM)],
        [(u_shape, HBM), (u_shape, HBM), (jax.ShapeDtypeStruct((pairs, 8, width), f32), VMEM)]
        + [(jax.ShapeDtypeStruct(f.shape, f32), HBM) for f in firsts]
        + [(far_shape, HBM)] * PARTNERS,
        block_scratch(orb_dev, rows, width)
        + [pltpu.VMEM((PARTNERS, rows, width), bf16)] * 2
        + [pltpu.VMEM((pairs, width, width), f32)]
        + [DMA((len(firsts),)), DMA((PARTNERS,)), DMA((pairs,))]
        + [pltpu.VMEM((PARTNERS, rows, width), f32)]
        + [pltpu.VMEM((PARTNERS, width, min(128, width)), f32)]
        + [pltpu.VMEM((PARTNERS, width, rows), bf16)] * 2
        + [pltpu.VMEM((pairs, width, width), bf16)] * 2
        + [DMA((pairs,)), DMA((pairs,)), DMA((PARTNERS,))]
        + [pltpu.VMEM((len(firsts),) + firsts[0].shape, f32), DMA((len(firsts), orb_dev))],
        18 * 16 * width * width * rows, 24 * 1024 * 1024, name,
    )
    cut = 3 + len(firsts)
    return outs[0], outs[1], outs[2], outs[3:cut], outs[cut:]


def density_call(meta, firsts, seconds, u, name):
    orb_dev, _, width = firsts[0].shape
    rows = sum(f.shape[1] for f in firsts)
    pairs = meta.shape[1]
    outs = kernel_call(
        functools.partial(density_kernel, len(firsts)),
        [(meta, SMEM)] + [(a, HBM) for a in [*firsts, *seconds, *u]],
        [(jax.ShapeDtypeStruct(f.shape, f32), HBM) for f in firsts]
        + [(jax.ShapeDtypeStruct((rows, width), f32), HBM)] * PARTNERS,
        block_scratch(orb_dev, rows, width)
        + [pltpu.VMEM((PARTNERS, rows, width), bf16)] * 2
        + [DMA((len(firsts),)), DMA((PARTNERS,))]
        + [pltpu.VMEM((PARTNERS, rows, width), f32)]
        + [pltpu.VMEM((pairs, width, width), bf16)] * 2
        + [DMA((pairs,)), DMA((pairs,)), DMA((PARTNERS,))]
        + [pltpu.VMEM((len(firsts),) + firsts[0].shape, f32), DMA((len(firsts), orb_dev))],
        12 * 16 * width * width * rows, 24 * 1024 * 1024, name,
    )
    return outs[: len(firsts)], outs[len(firsts) :]


def sum_kernel(parts, extras, tailed, chosen, *refs):
    own, refs = refs[:parts], refs[parts:]
    arrived, refs = refs[:PARTNERS], refs[PARTNERS:]
    extra, refs = refs[:extras], refs[extras:]
    tails, refs = (refs[:parts], refs[parts:]) if tailed else ([], refs)
    outs, refs = refs[:parts], refs[parts:]
    acc, buf, e_buf, own_sem, sem, e_sem, out_sem, tail_sem = refs
    orb_dev, rows = acc.shape[1], acc.shape[2]
    held = orb_dev * rows
    own_copies = [pltpu.make_async_copy(own[q], acc.at[q], own_sem.at[q]) for q in range(parts)]
    copies = [
        pltpu.make_async_copy(ref.at[pl.ds(0, parts * rows)], buf.at[k], sem.at[k])
        for k, ref in enumerate(arrived)
    ]
    e_rows = e_buf.shape[1]
    e_copies = [
        pltpu.make_async_copy(ref.at[pl.ds(0, e_rows)], e_buf.at[q], e_sem.at[q])
        for q, ref in enumerate(extra)
    ]
    tail_copies = [
        pltpu.make_async_copy(tail, outs[q].at[pl.ds(held, tail.shape[0])], tail_sem.at[q])
        for q, tail in enumerate(tails)
    ]
    start_all(copies + own_copies + e_copies + tail_copies)
    wait_all(own_copies)
    for k in range(PARTNERS):
        copies[k].wait()
        for q in range(parts):
            acc[q, chosen[k]] += buf[k, q * rows : (q + 1) * rows, :]
    wait_all(e_copies)
    piece = e_rows // orb_dev
    backs = []
    for o in range(orb_dev):
        for q in range(extras):
            term = e_buf[q, o * piece : (o + 1) * piece, :]
            if extras == parts:
                acc[q, o] += term
            else:
                acc[0, o, q * piece : (q + 1) * piece, :] += term
        for q in range(parts):
            place = outs[q].at[pl.ds(o * rows, rows)]
            backs.append(pltpu.make_async_copy(acc.at[q, o], place, out_sem.at[q, o]))
            backs[-1].start()
    wait_all(backs + tail_copies)


def sum_call(chosen, own, arrived, extra, name, tails=()):
    parts = len(own)
    orb_dev, rows, width = own[0].shape
    tail_rows = tails[0].shape[0] if tails else 0
    shape = jax.ShapeDtypeStruct((orb_dev * rows + tail_rows, width), f32)
    extras = len(extra)
    e_rows = orb_dev * rows * parts // extras if extras else 8
    return kernel_call(
        functools.partial(sum_kernel, parts, extras, bool(tails)),
        [(chosen, SMEM)]
        + [(a, HBM) for a in [*own, *arrived, *extra]]
        + [(t, VMEM) for t in tails],
        [(shape, HBM)] * parts,
        [
            pltpu.VMEM((parts, orb_dev, rows, width), f32),
            pltpu.VMEM((PARTNERS, parts * rows, width), f32),
            pltpu.VMEM((max(extras, 1), e_rows, width), f32),
            DMA((parts,)), DMA((PARTNERS,)), DMA((max(extras, 1),)), DMA((parts, orb_dev)),
            DMA((parts,)),
        ],
        0, 12 * 1024 * 1024, name,
    )


def pick_kernel(parts, chosen, *refs):
    sources, outs = refs[:parts], refs[parts:-3]
    buf, in_sem, out_sem = refs[-3:]
    into = []
    for k in range(PARTNERS):
        at = 0
        for q, source in enumerate(sources):
            window = pl.ds(at, source.shape[1])
            into.append(
                pltpu.make_async_copy(source.at[chosen[k]], buf.at[k, window], in_sem.at[k, q])
            )
            at += source.shape[1]
    start_all(into)
    back = [pltpu.make_async_copy(buf.at[k], out, out_sem.at[k]) for k, out in enumerate(outs)]
    for k in range(PARTNERS):
        wait_all(into[k * parts : (k + 1) * parts])
        back[k].start()
    wait_all(back)


def pick_call(chosen, sources, name):
    rows = sum(a.shape[1] for a in sources)
    shape = jax.ShapeDtypeStruct((rows, sources[0].shape[2]), f32)
    return kernel_call(
        functools.partial(pick_kernel, len(sources)),
        [(chosen, SMEM)] + [(a, HBM) for a in sources],
        [(shape, HBM)] * PARTNERS,
        [
            pltpu.VMEM((PARTNERS,) + shape.shape, f32),
            DMA((PARTNERS, len(sources))), DMA((PARTNERS,)),
        ],
        0, 4 * 1024 * 1024, name,
    )


def look_up(table, index):
    lanes = 128
    high = (index // lanes).reshape(-1, 1) == jnp.arange(table.size // lanes, dtype=jnp.int32)
    low = (index % lanes).reshape(-1, 1) == jnp.arange(lanes, dtype=jnp.int32)
    rows = jnp.dot(
        high.astype(f32), table.reshape(-1, lanes), precision=lax.Precision.HIGHEST
    )
    return jnp.sum(jnp.where(low, rows, 0.0), axis=1).reshape(index.shape)


def shards(orb_size, blocks, occ_energy, vir_table, domain, pair_i, pair_j):
    orb_dev, aux_rows, width = blocks.shape
    pair_dev = pair_i.shape[0]
    p = lax.axis_index("orb")
    x = lax.axis_index("aux")
    aux_size = 4
    half = aux_rows // 2

    ring = [(s, (s + 1) % aux_size) for s in range(aux_size)]
    back = [(t, s) for s, t in ring]
    to_right = lambda a: lax.ppermute(a, "aux", ring)
    to_left = lambda a: lax.ppermute(a, "aux", back)

    def mask_of(k, at):
        low = LOW_BITS[k]
        return (((low >> 1) ^ at) << 3) | low

    tables = [
        [
            (o * aux_size + s, (o ^ mask_of(k, s)) * aux_size + s)
            for o in range(orb_size)
            for s in range(aux_size)
        ]
        for k in range(PARTNERS)
    ]

    def after(value, *earlier):
        return lax.optimization_barrier((value, earlier))[0]

    def exchange(payloads, lanes=3, work=None, at=None):
        out = []
        for k, payload in enumerate(payloads):
            if k >= lanes:
                payload = after(payload, out[k - lanes])
            out.append(lax.ppermute(payload, ("orb", "aux"), tables[k]))
        if work is None:
            return out, None
        return out, work(meta if at is None else after(meta, out[at]))

    first_local = pair_i - p * orb_dev
    holder = pair_j // orb_dev
    second_local = pair_j % orb_dev
    device_ids = jnp.arange(orb_size, dtype=jnp.int32)
    held_by = holder[:, None] == device_ids[None, :]
    wanted = jnp.max(jnp.where(held_by, second_local[:, None], -1), axis=0)
    requested = lax.all_to_all(wanted, "orb", split_axis=0, concat_axis=0, tiled=True)

    rows_a, rows_b = after((blocks[:, :half], blocks[:, half:]), requested)
    left_a = to_right(rows_a)
    right_b = to_left(rows_b)

    low_bits = jnp.array(LOW_BITS, dtype=jnp.int32)
    partners = p ^ ((((low_bits >> 1) ^ x) << 3) | low_bits)
    virtual = look_up(vir_table, domain)
    shifted = virtual - occ_energy[:, None]
    requested = lax.optimization_barrier((requested, shifted))[0]
    chosen = jnp.clip(requested[partners], 0, orb_dev - 1)

    apart = holder ^ p
    mine = ((apart >> 3) ^ ((apart >> 1) & 3)) == x
    slot = sum(jnp.where((apart & 7) == low, k, 0) for k, low in enumerate(LOW_BITS))
    order = jnp.arange(pair_dev, dtype=jnp.int32)
    key = jnp.where(mine, first_local, orb_dev) * pair_dev + order
    place = jnp.sum((key[None, :] < key[:, None]).astype(jnp.int32), axis=1)
    at_place = place[None, :] == order[:, None]
    pick = lambda v: jnp.sum(jnp.where(at_place, v[None, :], 0), axis=1)
    count = jnp.sum(mine.astype(jnp.int32))
    present = jnp.any((first_local[None, :] == order[:, None]) & mine[None, :], axis=1)
    meta = jnp.stack(
        [
            pick(first_local), pick(slot), jnp.broadcast_to(count, (pair_dev,)),
            present.astype(jnp.int32),
        ]
    )

    near, _ = exchange(pick_call(chosen, [blocks], "pick_near"))

    set_c = after((rows_b, rows_a), left_a, right_b, near)
    set_c = (to_right(set_c[0]), to_left(set_c[1]))
    set_a = after((left_a, right_b), near)
    energies = jnp.broadcast_to(shifted[:, None, :], (orb_dev, 8, width))
    got_a, integrals = exchange(
        pick_call(chosen, [*set_a, energies], "pick_a"),
        work=lambda meta: integral_call(meta, [blocks], near, None, "integrals_near"),
    )

    set_o = after((left_a, right_b), set_c, got_a, integrals)
    set_o = (to_right(set_o[0]), to_left(set_o[1]))
    set_c = after(set_c, got_a, integrals)
    got_c, integrals = exchange(
        pick_call(chosen, set_c, "pick_c"),
        work=lambda meta: integral_call(meta, set_a, got_a, integrals, "integrals_a"),
    )
    second_row = jnp.stack([after(a, got_c[0])[2 * half] for a in got_a])

    set_o = after(set_o, got_c, integrals)
    got_o, integrals = exchange(
        pick_call(chosen, set_o, "pick_o"),
        lanes=PARTNERS,
        work=lambda meta: integral_call(meta, set_c, got_c, integrals, "integrals_c"),
    )
    u_high, u_low, energy, own_o, far_o = middle_call(
        meta, set_o, got_o, integrals, shifted, second_row, "amplitudes"
    )

    def density_work(firsts, seconds, name):
        return lambda meta: density_call(meta, firsts, seconds, (u_high, u_low), name)

    back_o, _ = exchange(far_o, lanes=PARTNERS)
    energy = after(energy, back_o[0])
    pair_energy = jnp.sum(energy, axis=(1, 2)) / width
    pair_energy = jnp.where(order < count, pair_energy, 0.0)
    spread = jnp.sum(jnp.where(at_place.T, pair_energy[None, :], 0.0), axis=1)
    tail = jnp.pad(spread[None, :], ((0, 7), (0, width - pair_dev)))
    own_c, far_c = density_work(set_c, got_c, "density_c")(after(meta, back_o[2], tail))
    back_o = after(back_o, far_c)
    held = orb_dev * half
    sum_o_a, sum_o_b = sum_call(chosen, own_o, back_o, [], "sum_o", tails=[tail, tail])
    carried_a = to_left(sum_o_a)
    carried_b = to_right(sum_o_b)

    back_c, (own_a, far_a) = exchange(far_c, work=density_work(set_a, got_a, "density_a"), at=4)
    sum_left_b, sum_right_a = sum_call(chosen, own_c, back_c, [], "sum_c")
    sum_left_b, sum_right_a, far_a = after((sum_left_b, sum_right_a, far_a), carried_a, carried_b)
    home_b = to_left(sum_left_b)
    home_a = to_right(sum_right_a)

    back_a, (own_near, far_near) = exchange(
        far_a, work=density_work([blocks], near, "density_near"), at=4
    )
    sum_left_a, sum_right_b = sum_call(
        chosen, own_a, back_a, [carried_a, carried_b], "sum_a",
        tails=[carried_a[held:], carried_b[held:]],
    )
    sum_left_a, sum_right_b, far_near = after(
        (sum_left_a, sum_right_b, far_near), home_a, home_b
    )
    last_a = to_left(sum_left_a)
    last_b = to_right(sum_right_b)

    back_near, _ = exchange(far_near)
    (sum_near,) = sum_call(chosen, own_near, back_near, [home_a, home_b], "sum_near")
    pieces = [a[:held].reshape(orb_dev, half, width) for a in (last_a, last_b)]
    density = sum_near.reshape(blocks.shape) + jnp.concatenate(pieces, axis=1)
    spread = spread + sum(a[held, :pair_dev] for a in (carried_a, carried_b, last_b))
    return density, spread


def solution(mesh):
    placed = (P("orb", "aux", None), P("orb"), P(), P("orb", None), P("orb"), P("orb"))
    return jax.shard_map(
        functools.partial(shards, mesh.shape["orb"]),
        mesh=mesh,
        in_specs=placed,
        out_specs=(P("orb", "aux", None), P("orb")),
        check_vma=False,
    )
```
